512 devices in a mesh: scan: 128 (over x, z, core), mode: 4 (over y).
Axes of the slice: x: 4, y: 4, z: 16, core: 2. Of those that a mesh axis runs over, the one named last changes fastest.
Arguments:
- object_field: float32 [2, 12288, 1536], P(None, 'scan', 'mode'), may hold values from -6 to 6
- probe: float32 [4, 2, 256, 256], P('mode'), may hold values from -6 to 6
- measured: float32 [128, 256, 256], P('scan'), may hold values from 0.5 to 8
- positions: int32 [128, 2], P('scan'), may hold values from -96 to 12128, as said below
Outputs:
- new_object: float32 [2, 12288, 1536], P(None, 'scan', 'mode')
- new_probe: float32 [4, 2, 256, 256], P('mode')
The draws below stay inside these ranges and needn't reach their ends.
Inputs may be any that keep to these rules, and one draw needn't show every extreme that they name: `positions`: A pattern held at scan index s has its corner row between s * 96 - 96 and s * 96 + 2 * 96 - 256, and its corner column between 0 and 1280; some pattern sits at each end of the row band.
All inputs are finite; a program needn't handle non-finite values.
Results may differ from the reference program's by a relative error of at most 0.0003.
Values sent between devices are 32-bit elements; how exact they have to be, the bound alone decides.
A program may use at most 64 MiB of HBM per device.

```python
import math
import jax
import jax.numpy as jnp
from jax import lax

PATCH = 256
TY = 96
PAT_DEV = 1
MODES = 4
PATTERNS = 128
OY = 12288
OX = 1536


def draw_positions(key, part):
    key = jax.random.fold_in(key, 7)
    subkeys = jax.random.split(key, 2)
    band_width = 3 * TY - PATCH
    owner_index = jnp.arange(PATTERNS, dtype=jnp.int32) // PAT_DEV
    offset = jax.random.randint(subkeys[0], (PATTERNS,), 0, band_width + 1, dtype=jnp.int32)
    offset = offset.at[0].set(0).at[PATTERNS - 1].set(band_width)
    corner_rows = owner_index * TY - TY + offset
    corner_cols = jax.random.randint(subkeys[1], (PATTERNS,), 0, OX - PATCH + 1, dtype=jnp.int32)
    corner_cols = corner_cols.at[0].set(OX - PATCH)
    return jnp.stack([corner_rows, corner_cols], axis=1)


def block_scale(stream_key, dims, pieces, least, top_value):
    level, own = 1.0, jax.random.fold_in(stream_key, 6)
    for position, shards_of in pieces:
        draws = jnp.exp(jax.random.uniform(jax.random.fold_in(own, position), (shards_of,), jnp.float32, least / len(pieces), top_value / len(pieces)))
        level = level * jnp.repeat(draws, dims[position] // shards_of).reshape([-1 if axis == position else 1 for axis in range(len(dims))])
    return level


def gaussian(stream_key, shape, deviation, bound, shards=(), kind=jnp.bfloat16):
    values = deviation * jax.random.normal(stream_key, shape, jnp.float32)
    if shards:
        values = values * block_scale(stream_key, shape, shards, -0.22, 0.18)
    return jnp.clip(values, -bound, bound).astype(kind)


def setup_inputs(seed: int = 0) -> dict:
    seeds = jax.random.split(jax.random.key(seed), 5)
    return {
        "object_field": gaussian(seeds[0], (2, OY, OX), 1.0, 6.0, ((1, 128), (2, 4)), jnp.float32),
        "probe": gaussian(seeds[1], (MODES, 2, PATCH, PATCH), 1.0, 6.0, ((0, 4),), jnp.float32),
        "measured": jnp.clip(jnp.exp(math.log(8.0) - 2.7725887 * jax.random.uniform(seeds[2], (PATTERNS, PATCH, PATCH), jnp.float32) ** block_scale(seeds[2], (PATTERNS, PATCH, PATCH), ((0, 128),), -0.2, 0.2)), 0.5, 8.0),
        "positions": draw_positions(jax.random.fold_in(seeds[4], 71), 0),
    }


object_rate = 0.25

def reference(object_field, probe, measured, positions):
    padded = jnp.pad(object_field, ((0, 0), (TY, TY), (0, 0)))
    probe_modes = lax.complex(probe[:, 0], probe[:, 1])

    def one_pattern(state_pair, inputs):
        gradient, probe_sum = state_pair
        corner, amplitude = inputs
        row_at = (corner[0] + TY).astype(jnp.int32)
        col_at = corner[1].astype(jnp.int32)
        anchor = jnp.zeros((), jnp.int32)
        cut_patch = lax.dynamic_slice(padded, (anchor, row_at, col_at), (2, PATCH, PATCH))
        patch_complex = lax.complex(cut_patch[0], cut_patch[1])
        exit_wave = probe_modes * patch_complex[None]
        far_field = jnp.fft.fft2(exit_wave, norm='ortho')
        intensity = lax.optimization_barrier(jnp.sum(far_field.real ** 2 + far_field.imag ** 2, axis=0))
        factor = 1.0 - amplitude / jnp.sqrt(jnp.maximum(intensity, 1.0))
        back_wave = jnp.fft.ifft2(far_field * factor[None], norm='ortho')
        object_term = lax.optimization_barrier(jnp.sum(jnp.conj(probe_modes) * back_wave, axis=0))
        probe_term = jnp.conj(patch_complex)[None] * back_wave
        stacked = jnp.stack([object_term.real, object_term.imag])
        previous = lax.dynamic_slice(gradient, (anchor, row_at, col_at), (2, PATCH, PATCH))
        gradient = lax.dynamic_update_slice(gradient, previous + stacked, (anchor, row_at, col_at))
        probe_sum = probe_sum + jnp.stack([probe_term.real, probe_term.imag], axis=1)
        return ((gradient, probe_sum), None)
    grad_init = jnp.zeros_like(padded)
    probe_init = jnp.zeros_like(probe)
    (gradient, probe_sum), unused = lax.scan(one_pattern, (grad_init, probe_init), (positions, measured))
    new_object = object_field - object_rate * gradient[:, TY:TY + OY]
    new_probe = probe - probe_sum / math.sqrt(PATTERNS)
    return (new_object, new_probe)
```

```python
import functools
import math

import jax
import jax.numpy as jnp
import ml_dtypes
import numpy as np
from jax import lax
from jax.experimental import pallas as pl
from jax.experimental.pallas import tpu as pltpu
from jax.sharding import PartitionSpec as P

MESH = pl.DeviceIdType.MESH
F32 = jnp.float32
BF16 = jnp.bfloat16
X_CHIPS = 4
MODES = 4
PATCH = 256
ROWS = 96
COLS = 384
LANES = 128
UNITS = PATCH * PATCH // (8 * LANES)
CHUNK = 64
CHUNKS = PATCH // CHUNK
object_rate = 0.25


def dft_blocks():
    index = np.arange(PATCH)
    angle = 2.0 * math.pi / PATCH * (np.outer(index, index) % PATCH)
    scale = 1.0 / math.sqrt(PATCH)
    real, imag = np.cos(angle) * scale, -np.sin(angle) * scale
    forward = np.block([[real, imag], [-imag, real]])
    parts = []
    for matrix in (forward, forward.T):
        high = matrix.astype(ml_dtypes.bfloat16)
        low = (matrix - high.astype(np.float64)).astype(ml_dtypes.bfloat16)
        parts += [high, low]
    return np.stack(parts)


def split(value):
    high = value.astype(BF16)
    return high, (value - high.astype(F32)).astype(BF16)


def dot(left, right):
    return jnp.dot(left, right, preferred_element_type=F32)


def column_mask(corner, block, shape):
    lane = lax.broadcasted_iota(jnp.int32, shape, 1) + block * LANES
    corner = jnp.broadcast_to(corner, shape)
    return (lane >= corner) & (lane < corner + PATCH)


class Wires:
    def __init__(self, send, recv):
        self.send, self.recv, self.started = send, recv, []

    def put(self, src, dst, scan, mode):
        slot = len(self.started)
        copy = pltpu.make_async_remote_copy(
            src_ref=src,
            dst_ref=dst,
            send_sem=self.send.at[slot],
            recv_sem=self.recv.at[slot],
            device_id=(scan, mode),
            device_id_type=MESH,
        )
        copy.start()
        self.started.append(copy)
        return copy


def kernel(
    scans, chips_x, chips_z,
    pos_ref, obj_ref, probe_ref, meas_ref, dft_ref,
    new_obj_ref, new_probe_ref,
    strip, corners, pick_next, pick_prev, from_prev, from_next,
    patch, wave, stack, far, power, power_a, power_sum, power_b,
    term, term_a, term_sum, term_b, total_term, rim_up, rim_down, grad_prev, grad_next,
    pgrad, pcore, units, units_x, shard, units_z, gathered, gathered_other,
    send_sem, recv_sem,
):
    s = lax.axis_index("scan")
    m = lax.axis_index("mode")
    core = lax.rem(s, 2)
    z = lax.rem(lax.div(s, 2), chips_z)
    x = lax.div(s, 2 * chips_z)
    nxt, prv = lax.rem(s + 1, scans), lax.rem(s + scans - 1, scans)
    m_up, m_dn = lax.rem(m + 1, MODES), lax.rem(m + MODES - 1, MODES)
    pair_a = jnp.where(lax.rem(m, 2) == 0, m + 1, m - 1)
    pair_b = MODES - 1 - m
    other_core = jnp.where(core == 0, s + 1, s - 1)
    wires = Wires(send_sem, recv_sem)

    def at_x(step):
        return (lax.rem(x + step, chips_x) * chips_z + z) * 2 + core

    def at_z(step):
        return (x * chips_z + lax.rem(z + step, chips_z)) * 2 + core

    partners = [(s, m_up), (s, m_dn), (nxt, m), (prv, m)]
    partners += [(at_x(step), m) for step in range(1, chips_x)]
    partners += [(at_z(step), m) for step in range(1, chips_z)]
    barrier = pltpu.get_barrier_semaphore()
    for partner in partners:
        pl.semaphore_signal(barrier, inc=1, device_id=partner, device_id_type=MESH)
    pl.semaphore_wait(barrier, len(partners))

    up_re = wires.put(obj_ref.at[0], strip.at[m, 0], s, m_up)
    dn_im = wires.put(obj_ref.at[1], strip.at[m, 1], s, m_dn)
    row_at = pos_ref[0, 0]
    col_at = pos_ref[0, 1]
    corners[1] = jnp.full((8, LANES), col_at, jnp.int32)
    pos_next = wires.put(corners.at[1], corners.at[0], nxt, m)
    pos_prev = wires.put(corners.at[1], corners.at[2], prv, m)
    up_im = wires.put(obj_ref.at[1], strip.at[m, 1], s, m_up)
    dn_re = wires.put(obj_ref.at[0], strip.at[m, 0], s, m_dn)
    strip[m] = obj_ref[...]
    offset = row_at - ROWS * s + ROWS
    turn = jnp.bitwise_and(col_at, PATCH - 1)
    for part in range(2):
        rolled = pltpu.roll(probe_ref[0, part], turn, 1)
        wave[part] = pltpu.roll(rolled, offset, 0)
    pos_next.wait_recv()
    pos_prev.wait_recv()
    up_re.wait_recv()
    fwd_re = wires.put(strip.at[m_dn, 0], strip.at[m_dn, 0], s, m_up)
    dn_im.wait_recv()
    fwd_im = wires.put(strip.at[m_up, 1], strip.at[m_up, 1], s, m_dn)

    def chosen(part, who, half):
        shape = (ROWS, LANES)
        corner = corners[who, 0:1, :]
        picked = jnp.zeros(shape, F32)
        for block in range(half, MODES * COLS // LANES, 2):
            tile, inner = divmod(block, COLS // LANES)
            cells = strip[tile, part, :, inner * LANES : (inner + 1) * LANES]
            picked = jnp.where(column_mask(corner, block, shape), cells, picked)
        return picked

    halos = []
    for part in range(2):
        if part == 0:
            dn_re.wait_recv()
            fwd_re.wait_recv()
        else:
            up_im.wait_recv()
            fwd_im.wait_recv()
        for half in range(2):
            lanes = slice(half * LANES, (half + 1) * LANES)
            pick_next[part, :, lanes] = chosen(part, 2, half)
            pick_prev[part, :, lanes] = chosen(part, 0, half)
        halos.append(wires.put(pick_next.at[part], from_prev.at[part], nxt, m))
        halos.append(wires.put(pick_prev.at[part], from_next.at[part], prv, m))
        for half in range(2):
            lanes = slice(half * LANES, (half + 1) * LANES)
            patch[part, ROWS : 2 * ROWS, lanes] = chosen(part, 1, half)
    for halo in halos:
        halo.wait_recv()
    seam = lax.broadcasted_iota(jnp.int32, (32, PATCH), 0)
    for part in range(2):
        above = jnp.where(s > 0, from_prev[part], 0.0)
        below = jnp.where(s < scans - 1, from_next[part], 0.0)
        patch[part, 0:32] = jnp.where(seam >= offset, above[0:32], below[64:96])
        patch[part, 32:96] = above[32:96]
        patch[part, 192:256] = below[0:64]

    def along_rows(value, which):
        high, low = split(value)
        return dot(high, dft_ref[which]) + dot(low, dft_ref[which]) + dot(high, dft_ref[which + 1])

    def along_columns(rows, which):
        first = dot(dft_ref[which, rows, :], stack[0]) + dot(dft_ref[which, rows, :], stack[1])
        return first + dot(dft_ref[which + 1, rows, :], stack[0])

    def keep(value, rows):
        high, low = split(value)
        for part in range(2):
            lanes = slice(part * PATCH, (part + 1) * PATCH)
            into = slice(part * PATCH + rows.start, part * PATCH + rows.stop)
            stack[0, into] = high[:, lanes]
            stack[1, into] = low[:, lanes]

    slices = [slice(i * CHUNK, (i + 1) * CHUNK) for i in range(CHUNKS)]
    for rows in slices:
        p_re, p_im = wave[0, rows], wave[1, rows]
        o_re, o_im = patch[0, rows], patch[1, rows]
        exit_wave = jnp.concatenate([p_re * o_re - p_im * o_im, p_re * o_im + p_im * o_re], axis=1)
        keep(along_rows(exit_wave, 0), rows)

    def route(i):
        return (pair_a, pair_b) if i % 2 == 0 else (pair_b, pair_a)

    hops = []
    for i, rows in enumerate(slices):
        f_re = along_columns(rows, 2)
        f_im = along_columns(slice(PATCH + rows.start, PATCH + rows.stop), 2)
        far[0, rows] = f_re
        far[1, rows] = f_im
        power[rows] = f_re * f_re + f_im * f_im
        hops.append(wires.put(power.at[rows], power_a.at[rows], s, route(i)[0]))
    more = []
    for i, rows in enumerate(slices):
        hops[i].wait_recv()
        power_sum[rows] = power[rows] + power_a[rows]
        more.append(wires.put(power_sum.at[rows], power_b.at[rows], s, route(i)[1]))
    for i, rows in enumerate(slices):
        more[i].wait_recv()
        intensity = power_sum[rows] + power_b[rows]
        factor = 1.0 - meas_ref[0, rows] / jnp.sqrt(jnp.maximum(intensity, 1.0))
        scaled = jnp.concatenate([far[0, rows] * factor, far[1, rows] * factor], axis=1)
        keep(along_rows(scaled, 2), rows)

    hops = []
    for i, rows in enumerate(slices):
        b_re = along_columns(rows, 0)
        b_im = along_columns(slice(PATCH + rows.start, PATCH + rows.stop), 0)
        p_re, p_im = wave[0, rows], wave[1, rows]
        term[0, rows] = p_re * b_re + p_im * b_im
        term[1, rows] = p_re * b_im - p_im * b_re
        hops.append(wires.put(term.at[:, rows], term_a.at[:, rows], s, route(i)[0]))
        o_re, o_im = patch[0, rows], patch[1, rows]
        pgrad[0, rows] = o_re * b_re + o_im * b_im
        pgrad[1, rows] = o_re * b_im - o_im * b_re

    for part in range(2):
        turned = pltpu.roll(pgrad[part], PATCH - offset, 0)
        pgrad[part] = pltpu.roll(turned, PATCH - turn, 1)
    to_core = wires.put(pgrad.at[1 - core], pcore, other_core, m)

    more = []
    for i, rows in enumerate(slices[:2]):
        hops[i].wait_recv()
        term_sum[:, rows] = term[:, rows] + term_a[:, rows]
        more.append(wires.put(term_sum.at[:, rows], term_b.at[:, rows], s, route(i)[1]))

    def unit_slices(unit):
        return slice(unit // 2 * 8, unit // 2 * 8 + 8), slice(unit % 2 * LANES, (unit % 2 + 1) * LANES)

    to_core.wait_recv()
    own = pgrad.at[core]
    for unit in range(UNITS):
        rows, lanes = unit_slices(unit)
        units[unit] = own[rows, lanes] + pcore[rows, lanes]
    per_x = UNITS // chips_x
    per_z = per_x // chips_z
    to_x = []
    for step in range(1, chips_x):
        there = lax.rem(x + step, chips_x) * per_x
        to_x.append(wires.put(units.at[pl.ds(there, per_x)], units_x.at[step], at_x(step), m))

    for i, rows in list(enumerate(slices))[2:]:
        hops[i].wait_recv()
        term_sum[:, rows] = term[:, rows] + term_a[:, rows]
        more.append(wires.put(term_sum.at[:, rows], term_b.at[:, rows], s, route(i)[1]))

    total = units[pl.ds(x * per_x, per_x)]
    for step in range(1, chips_x):
        to_x[step - 1].wait_recv()
        total = total + units_x[step]
    shard[...] = total
    to_z = []
    for step in range(1, chips_z):
        there = lax.rem(z + step, chips_z) * per_z
        to_z.append(wires.put(shard.at[pl.ds(there, per_z)], units_z.at[step], at_z(step), m))
    total = shard[pl.ds(z * per_z, per_z)]
    for step in range(1, chips_z):
        to_z[step - 1].wait_recv()
        total = total + units_z[step]
    first = x * per_x + z * per_z
    scale = 1.0 / math.sqrt(scans)
    for i in range(per_z):
        unit = first + i
        rows = pl.ds(pl.multiple_of(lax.div(unit, 2) * 8, 8), 8)
        lanes = pl.ds(pl.multiple_of(lax.rem(unit, 2) * LANES, LANES), LANES)
        gathered[unit] = probe_ref[0, core, rows, lanes] - total[i] * scale
    mine = gathered.at[pl.ds(first, per_z)]
    back_z = [wires.put(mine, mine, at_z(step), m) for step in range(1, chips_z)]

    for i, rows in enumerate(slices):
        more[i].wait_recv()
        total_term[:, rows] = term_sum[:, rows] + term_b[:, rows]
    for part in range(2):
        edge = total_term[part, 0:32]
        rim_up[part, 0:32] = jnp.where(seam >= offset, edge, 0.0)
        rim_up[part, 32:96] = total_term[part, 32:96]
        rim_down[part, 0:64] = total_term[part, 192:256]
        rim_down[part, 64:96] = jnp.where(seam < offset, edge, 0.0)
    to_prev = wires.put(rim_up, grad_next, prv, m)
    to_next = wires.put(rim_down, grad_prev, nxt, m)

    for copy in back_z:
        copy.wait_recv()
    mine = gathered.at[pl.ds(x * per_x, per_x)]
    back_x = [wires.put(mine, mine, at_x(step), m) for step in range(1, chips_x)]

    to_prev.wait_recv()
    to_next.wait_recv()
    shape = (ROWS, LANES)
    for inner in range(COLS // LANES):
        block = m * (COLS // LANES) + inner
        lanes = pl.ds(pl.multiple_of(lax.rem(block, 2) * LANES, LANES), LANES)
        masks = [column_mask(corners[who, 0:1, :], block, shape) for who in range(3)]
        for part in range(2):
            above = jnp.where(s > 0, grad_prev[part, :, lanes], 0.0)
            below = jnp.where(s < scans - 1, grad_next[part, :, lanes], 0.0)
            total = jnp.where(masks[1], total_term[part, ROWS : 2 * ROWS, lanes], 0.0)
            total = total + jnp.where(masks[0], above, 0.0) + jnp.where(masks[2], below, 0.0)
            here = slice(inner * LANES, (inner + 1) * LANES)
            new_obj_ref[part, :, here] = obj_ref[part, :, here] - object_rate * total

    for copy in back_x:
        copy.wait_recv()
    back_core = wires.put(gathered, gathered_other, other_core, m)
    for unit in range(UNITS):
        rows, lanes = unit_slices(unit)
        new_probe_ref[0, core, rows, lanes] = gathered[unit]
    back_core.wait_recv()
    for unit in range(UNITS):
        rows, lanes = unit_slices(unit)
        new_probe_ref[0, 1 - core, rows, lanes] = gathered_other[unit]
    for copy in wires.started:
        copy.wait_send()


def per_device(scans, chips_x, object_field, probe, measured, positions):
    chips_z = scans // (2 * chips_x)
    per_x = UNITS // chips_x
    per_z = per_x // chips_z
    wire_count = 12 + 6 * CHUNKS // 2 + 4 + 2 + 2 * (chips_x + chips_z) + CHUNKS
    field = pltpu.VMEM((2, PATCH, PATCH), F32)
    plane = pltpu.VMEM((PATCH, PATCH), F32)
    rim = pltpu.VMEM((2, ROWS, PATCH), F32)
    vmem = pl.BlockSpec(memory_space=pltpu.VMEM)
    return pl.pallas_call(
        functools.partial(kernel, scans, chips_x, chips_z),
        out_shape=(
            jax.ShapeDtypeStruct(object_field.shape, F32),
            jax.ShapeDtypeStruct(probe.shape, F32),
        ),
        in_specs=[pl.BlockSpec(memory_space=pltpu.SMEM)] + [vmem] * 4,
        out_specs=(vmem, vmem),
        scratch_shapes=[
            pltpu.VMEM((MODES, 2, ROWS, COLS), F32),
            pltpu.VMEM((3, 8, LANES), jnp.int32),
            rim, rim, rim, rim,
            field, field,
            pltpu.VMEM((2, 2 * PATCH, PATCH), BF16),
            field,
            plane, plane, plane, plane,
            field, field, field, field, field,
            rim, rim, rim, rim,
            field, plane,
            pltpu.VMEM((UNITS, 8, LANES), F32),
            pltpu.VMEM((chips_x, per_x, 8, LANES), F32),
            pltpu.VMEM((per_x, 8, LANES), F32),
            pltpu.VMEM((chips_z, per_z, 8, LANES), F32),
            pltpu.VMEM((UNITS, 8, LANES), F32),
            pltpu.VMEM((UNITS, 8, LANES), F32),
            pltpu.SemaphoreType.DMA((wire_count,)),
            pltpu.SemaphoreType.DMA((wire_count,)),
        ],
        compiler_params=pltpu.CompilerParams(
            collective_id=0, has_side_effects=True, vmem_limit_bytes=48 << 20
        ),
        cost_estimate=pl.CostEstimate(flops=1 << 31, bytes_accessed=4 << 20, transcendentals=0),
    )(positions, object_field, probe, measured, jnp.asarray(dft_blocks()))


def solution(mesh):
    return jax.shard_map(
        functools.partial(per_device, mesh.shape["scan"], X_CHIPS),
        mesh=mesh,
        in_specs=(
            P(None, "scan", "mode"),
            P("mode", None, None, None),
            P("scan", None, None),
            P("scan", None),
        ),
        out_specs=(P(None, "scan", "mode"), P("mode", None, None, None)),
        check_vma=False,
    )
```

```python
import functools
import math

import jax
import jax.numpy as jnp
import ml_dtypes
import numpy as np
from jax import lax
from jax.experimental import pallas as pl
from jax.experimental.pallas import tpu as pltpu
from jax.sharding import PartitionSpec as P

MESH = pl.DeviceIdType.MESH
F32 = jnp.float32
BF16 = jnp.bfloat16
X_CHIPS = 4
MODES = 4
PATCH = 256
ROWS = 96
THIRD = 32
COLS = 384
LANES = 128
UNITS = PATCH * PATCH // (8 * LANES)
CHUNK = 64
CHUNKS = PATCH // CHUNK
object_rate = 0.25


def dft_parts():
    index = np.arange(PATCH)
    angle = 2.0 * math.pi / PATCH * (np.outer(index, index) % PATCH)
    scale = 1.0 / math.sqrt(PATCH)
    return np.stack([np.cos(angle) * scale, -np.sin(angle) * scale]).astype(np.float32)


def split(value):
    high = value.astype(BF16)
    return high, (value - high.astype(F32)).astype(BF16)


def dot(left, right):
    return jnp.dot(left, right, preferred_element_type=F32)


def column_mask(corner, block, shape):
    lane = lax.broadcasted_iota(jnp.int32, shape, 1) + block * LANES
    return (lane >= corner) & (lane < corner + PATCH)


class Wires:
    def __init__(self, send, recv):
        self.send, self.recv, self.started = send, recv, []

    def put(self, src, dst, scan, mode):
        slot = len(self.started)
        copy = pltpu.make_async_remote_copy(
            src_ref=src,
            dst_ref=dst,
            send_sem=self.send.at[slot],
            recv_sem=self.recv.at[slot],
            device_id=(scan, mode),
            device_id_type=MESH,
        )
        copy.start()
        self.started.append(copy)
        return copy


def kernel(
    scans, chips_x, chips_z,
    pos_ref, obj_ref, probe_hbm, meas_hbm, dft_hbm,
    new_obj_ref, new_probe_ref,
    probe_ref, meas_ref, dft_ref, row_ops, col_ops,
    strip, corners, pick_next, pick_prev, from_prev, from_next,
    patch, wave, stack, far, power, power_a, power_sum, power_b,
    term, term_a, term_sum, term_b, total_term, rim_up, rim_down, grad_prev, grad_next,
    pgrad, pcore, units, units_x, shard, units_z, gathered, gathered_other,
    send_sem, recv_sem, local_sem,
):
    s = lax.axis_index("scan")
    m = lax.axis_index("mode")
    core = lax.rem(s, 2)
    z = lax.rem(lax.div(s, 2), chips_z)
    x = lax.div(s, 2 * chips_z)
    nxt, prv = lax.rem(s + 1, scans), lax.rem(s + scans - 1, scans)
    m_up, m_dn = lax.rem(m + 1, MODES), lax.rem(m + MODES - 1, MODES)
    pair_a = jnp.where(lax.rem(m, 2) == 0, m + 1, m - 1)
    pair_b = MODES - 1 - m
    other_core = jnp.where(core == 0, s + 1, s - 1)
    wires = Wires(send_sem, recv_sem)

    def at_x(step):
        return (lax.rem(x + step, chips_x) * chips_z + z) * 2 + core

    def at_z(step):
        return (x * chips_z + lax.rem(z + step, chips_z)) * 2 + core

    partners = [(s, m_up), (s, m_dn), (nxt, m), (prv, m)]
    partners += [(at_x(step), m) for step in range(1, chips_x)]
    partners += [(at_z(step), m) for step in range(1, chips_z)]
    barrier = pltpu.get_barrier_semaphore()
    for partner in partners:
        pl.semaphore_signal(barrier, inc=1, device_id=partner, device_id_type=MESH)
    pl.semaphore_wait(barrier, len(partners))

    def cells_of(tile, part, t):
        return strip.at[tile, part, t * THIRD : (t + 1) * THIRD]

    def own_cells(part, t):
        return obj_ref.at[part, t * THIRD : (t + 1) * THIRD]

    up, dn, fwd_up, fwd_dn = {}, {}, {}, {}

    def send_own(t):
        up[0, t] = wires.put(own_cells(0, t), cells_of(m, 0, t), s, m_up)
        dn[1, t] = wires.put(own_cells(1, t), cells_of(m, 1, t), s, m_dn)
        up[1, t] = wires.put(own_cells(1, t), cells_of(m, 1, t), s, m_up)
        dn[0, t] = wires.put(own_cells(0, t), cells_of(m, 0, t), s, m_dn)

    def forward(t):
        up[0, t].wait_recv()
        fwd_up[t] = wires.put(cells_of(m_dn, 0, t), cells_of(m_dn, 0, t), s, m_up)
        dn[1, t].wait_recv()
        fwd_dn[t] = wires.put(cells_of(m_up, 1, t), cells_of(m_up, 1, t), s, m_dn)

    send_own(0)
    locals_ = [
        pltpu.make_async_copy(src, dst, local_sem.at[i])
        for i, (src, dst) in enumerate(
            [(obj_ref, strip.at[m]), (dft_hbm, dft_ref), (probe_hbm, probe_ref), (meas_hbm, meas_ref)]
        )
    ]
    for copy in locals_:
        copy.start()
    row_at = pos_ref[0, 0]
    col_at = pos_ref[0, 1]
    corners[1] = jnp.full((8, LANES), col_at, jnp.int32)
    pos_next = wires.put(corners.at[1], corners.at[0], nxt, m)
    pos_prev = wires.put(corners.at[1], corners.at[2], prv, m)
    send_own(1)
    send_own(2)
    for copy in locals_:
        copy.wait()

    def transforms():
        real, imag = dft_ref[0], dft_ref[1]
        for part, (re, im) in enumerate(zip(split(real), split(imag))):
            for which, sign in enumerate((im, -im)):
                row_ops[which, part, 0:PATCH, 0:PATCH] = re
                row_ops[which, part, 0:PATCH, PATCH:] = sign
                row_ops[which, part, PATCH:, 0:PATCH] = -sign
                row_ops[which, part, PATCH:, PATCH:] = re
                for i in range(CHUNKS):
                    rows = slice(i * CHUNK, (i + 1) * CHUNK)
                    at = (4 * i + 2 * part) * CHUNK
                    col_ops[which, at : at + CHUNK, 0:PATCH] = re[rows]
                    col_ops[which, at : at + CHUNK, PATCH:] = -sign[rows]
                    col_ops[which, at + CHUNK : at + 2 * CHUNK, 0:PATCH] = sign[rows]
                    col_ops[which, at + CHUNK : at + 2 * CHUNK, PATCH:] = re[rows]

    offset = row_at - ROWS * s + ROWS
    turn = jnp.bitwise_and(col_at, PATCH - 1)
    transforms()
    forward(0)
    for part in range(2):
        rolled = pltpu.roll(probe_ref[0, part], turn, 1)
        wave[part] = pltpu.roll(rolled, offset, 0)
    pos_next.wait_recv()
    pos_prev.wait_recv()

    def choose(t):
        corner = [corners[who] for who in range(3)]
        blocks = MODES * COLS // LANES
        for part in range(2):
            if part == 0:
                dn[0, t].wait_recv()
                fwd_up[t].wait_recv()
            else:
                up[1, t].wait_recv()
                fwd_dn[t].wait_recv()
            for row in range(t * THIRD, (t + 1) * THIRD, 8):
                rows = slice(row, row + 8)
                picked = [[jnp.zeros((8, LANES), F32)] * 2 for who in range(3)]
                for block in range(blocks):
                    tile, inner = divmod(block, COLS // LANES)
                    cells = strip[tile, part, rows, inner * LANES : (inner + 1) * LANES]
                    for who in range(3):
                        mask = column_mask(corner[who], block, (8, LANES))
                        picked[who][block % 2] = jnp.where(mask, cells, picked[who][block % 2])
                for half in range(2):
                    lanes = slice(half * LANES, (half + 1) * LANES)
                    pick_prev[part, rows, lanes] = picked[0][half]
                    patch[part, ROWS + row : ROWS + row + 8, lanes] = picked[1][half]
                    pick_next[part, rows, lanes] = picked[2][half]
        rows = slice(t * THIRD, (t + 1) * THIRD)
        return (
            wires.put(pick_next.at[:, rows], from_prev.at[:, rows], nxt, m),
            wires.put(pick_prev.at[:, rows], from_next.at[:, rows], prv, m),
        )

    def along_rows(value, which):
        high, low = split(value)
        count = value.shape[0]
        both = dot(jnp.concatenate([high, low], axis=0), row_ops[which, 0])
        return both[:count] + both[count:] + dot(high, row_ops[which, 1])

    def along_columns(i, which):
        at = 4 * CHUNK * i
        both = dot(col_ops[which, at : at + 4 * CHUNK], stack[0])
        result = both[: 2 * CHUNK] + both[2 * CHUNK :] + dot(col_ops[which, at : at + 2 * CHUNK], stack[1])
        return result[:CHUNK], result[CHUNK:]

    def keep(value, rows):
        high, low = split(value)
        for part in range(2):
            lanes = slice(part * PATCH, (part + 1) * PATCH)
            into = slice(part * PATCH + rows.start, part * PATCH + rows.stop)
            stack[0, into] = high[:, lanes]
            stack[1, into] = low[:, lanes]

    def first_stage(*pieces):
        waves = []
        for rows in pieces:
            p_re, p_im = wave[0, rows], wave[1, rows]
            o_re, o_im = patch[0, rows], patch[1, rows]
            waves.append(jnp.concatenate([p_re * o_re - p_im * o_im, p_re * o_im + p_im * o_re], axis=1))
        result = along_rows(jnp.concatenate(waves, axis=0), 0)
        at = 0
        for rows in pieces:
            count = rows.stop - rows.start
            keep(result[at : at + count], rows)
            at += count

    halos = [choose(0)]
    forward(1)
    halos.append(choose(1))
    forward(2)
    halos.append(choose(2))
    first_stage(slice(ROWS, 2 * ROWS))
    seam = lax.broadcasted_iota(jnp.int32, (32, PATCH), 0)
    for halo in halos[:2]:
        for copy in halo:
            copy.wait_recv()
    for part in range(2):
        patch[part, 192:256] = jnp.where(s < scans - 1, from_next[part, 0:64], 0.0)
        patch[part, 32:64] = jnp.where(s > 0, from_prev[part, 32:64], 0.0)
    first_stage(slice(192, 256), slice(32, 64))
    for copy in halos[2]:
        copy.wait_recv()
    for part in range(2):
        above = jnp.where(s > 0, from_prev[part, 0:32], 0.0)
        below = jnp.where(s < scans - 1, from_next[part, 64:96], 0.0)
        patch[part, 0:32] = jnp.where(seam >= offset, above, below)
        patch[part, 64:96] = jnp.where(s > 0, from_prev[part, 64:96], 0.0)
    first_stage(slice(0, 32), slice(64, 96))

    slices = [slice(i * CHUNK, (i + 1) * CHUNK) for i in range(CHUNKS)]

    def route(i):
        return (pair_a, pair_b) if i % 2 == 0 else (pair_b, pair_a)

    hops = []
    for i, rows in enumerate(slices):
        f_re, f_im = along_columns(i, 0)
        far[0, rows] = f_re
        far[1, rows] = f_im
        power[rows] = f_re * f_re + f_im * f_im
        hops.append(wires.put(power.at[rows], power_a.at[rows], s, route(i)[0]))
    more = []
    for i, rows in enumerate(slices):
        hops[i].wait_recv()
        power_sum[rows] = power[rows] + power_a[rows]
        more.append(wires.put(power_sum.at[rows], power_b.at[rows], s, route(i)[1]))
    for i, rows in enumerate(slices):
        more[i].wait_recv()
        intensity = power_sum[rows] + power_b[rows]
        factor = 1.0 - meas_ref[0, rows] / jnp.sqrt(jnp.maximum(intensity, 1.0))
        scaled = jnp.concatenate([far[0, rows] * factor, far[1, rows] * factor], axis=1)
        keep(along_rows(scaled, 1), rows)

    hops = []
    for i, rows in enumerate(slices):
        b_re, b_im = along_columns(i, 1)
        p_re, p_im = wave[0, rows], wave[1, rows]
        term[0, rows] = p_re * b_re + p_im * b_im
        term[1, rows] = p_re * b_im - p_im * b_re
        hops.append(wires.put(term.at[:, rows], term_a.at[:, rows], s, route(i)[0]))
        o_re, o_im = patch[0, rows], patch[1, rows]
        pgrad[0, rows] = o_re * b_re + o_im * b_im
        pgrad[1, rows] = o_re * b_im - o_im * b_re

    for part in range(2):
        turned = pltpu.roll(pgrad[part], PATCH - offset, 0)
        pgrad[part] = pltpu.roll(turned, PATCH - turn, 1)
    to_core = wires.put(pgrad.at[1 - core], pcore, other_core, m)

    more = []
    for i, rows in enumerate(slices[:2]):
        hops[i].wait_recv()
        term_sum[:, rows] = term[:, rows] + term_a[:, rows]
        more.append(wires.put(term_sum.at[:, rows], term_b.at[:, rows], s, route(i)[1]))

    def unit_slices(unit):
        return slice(unit // 2 * 8, unit // 2 * 8 + 8), slice(unit % 2 * LANES, (unit % 2 + 1) * LANES)

    to_core.wait_recv()
    own = pgrad.at[core]
    for unit in range(UNITS):
        rows, lanes = unit_slices(unit)
        units[unit] = own[rows, lanes] + pcore[rows, lanes]
    per_x = UNITS // chips_x
    per_z = per_x // chips_z
    to_x = []
    for step in range(1, chips_x):
        there = lax.rem(x + step, chips_x) * per_x
        to_x.append(wires.put(units.at[pl.ds(there, per_x)], units_x.at[step], at_x(step), m))

    for i, rows in list(enumerate(slices))[2:]:
        hops[i].wait_recv()
        term_sum[:, rows] = term[:, rows] + term_a[:, rows]
        more.append(wires.put(term_sum.at[:, rows], term_b.at[:, rows], s, route(i)[1]))

    total = units[pl.ds(x * per_x, per_x)]
    for step in range(1, chips_x):
        to_x[step - 1].wait_recv()
        total = total + units_x[step]
    shard[...] = total
    to_z = []
    for step in range(1, chips_z):
        there = lax.rem(z + step, chips_z) * per_z
        to_z.append(wires.put(shard.at[pl.ds(there, per_z)], units_z.at[step], at_z(step), m))
    total = shard[pl.ds(z * per_z, per_z)]
    for step in range(1, chips_z):
        to_z[step - 1].wait_recv()
        total = total + units_z[step]
    first = x * per_x + z * per_z
    scale = 1.0 / math.sqrt(scans)
    for i in range(per_z):
        unit = first + i
        rows = pl.ds(pl.multiple_of(lax.div(unit, 2) * 8, 8), 8)
        lanes = pl.ds(pl.multiple_of(lax.rem(unit, 2) * LANES, LANES), LANES)
        gathered[unit] = probe_ref[0, core, rows, lanes] - total[i] * scale
    mine = gathered.at[pl.ds(first, per_z)]
    back_z = [wires.put(mine, mine, at_z(step), m) for step in range(1, chips_z)]

    for i, rows in enumerate(slices):
        more[i].wait_recv()
        total_term[:, rows] = term_sum[:, rows] + term_b[:, rows]
    for part in range(2):
        edge = total_term[part, 0:32]
        rim_up[part, 0:32] = jnp.where(seam >= offset, edge, 0.0)
        rim_up[part, 32:96] = total_term[part, 32:96]
        rim_down[part, 0:64] = total_term[part, 192:256]
        rim_down[part, 64:96] = jnp.where(seam < offset, edge, 0.0)
    to_prev = wires.put(rim_up, grad_next, prv, m)
    to_next = wires.put(rim_down, grad_prev, nxt, m)

    for copy in back_z:
        copy.wait_recv()
    mine = gathered.at[pl.ds(x * per_x, per_x)]
    back_x = [wires.put(mine, mine, at_x(step), m) for step in range(1, chips_x)]

    to_prev.wait_recv()
    to_next.wait_recv()
    shape = (ROWS, LANES)
    for inner in range(COLS // LANES):
        block = m * (COLS // LANES) + inner
        lanes = pl.ds(pl.multiple_of(lax.rem(block, 2) * LANES, LANES), LANES)
        masks = [column_mask(jnp.broadcast_to(corners[who, 0:1, :], shape), block, shape) for who in range(3)]
        for part in range(2):
            above = jnp.where(s > 0, grad_prev[part, :, lanes], 0.0)
            below = jnp.where(s < scans - 1, grad_next[part, :, lanes], 0.0)
            total = jnp.where(masks[1], total_term[part, ROWS : 2 * ROWS, lanes], 0.0)
            total = total + jnp.where(masks[0], above, 0.0) + jnp.where(masks[2], below, 0.0)
            here = slice(inner * LANES, (inner + 1) * LANES)
            new_obj_ref[part, :, here] = strip[m, part, :, here] - object_rate * total

    for copy in back_x:
        copy.wait_recv()
    back_core = wires.put(gathered, gathered_other, other_core, m)
    for unit in range(UNITS):
        rows, lanes = unit_slices(unit)
        new_probe_ref[0, core, rows, lanes] = gathered[unit]
    back_core.wait_recv()
    for unit in range(UNITS):
        rows, lanes = unit_slices(unit)
        new_probe_ref[0, 1 - core, rows, lanes] = gathered_other[unit]
    for copy in wires.started:
        copy.wait_send()


def per_device(scans, chips_x, object_field, probe, measured, positions):
    chips_z = scans // (2 * chips_x)
    per_x = UNITS // chips_x
    per_z = per_x // chips_z
    wire_count = 28 + 6 * CHUNKS // 2 + 4 + 2 + 2 * (chips_x + chips_z) + CHUNKS
    field = pltpu.VMEM((2, PATCH, PATCH), F32)
    plane = pltpu.VMEM((PATCH, PATCH), F32)
    rim = pltpu.VMEM((2, ROWS, PATCH), F32)
    vmem = pl.BlockSpec(memory_space=pltpu.VMEM)
    hbm = pl.BlockSpec(memory_space=pltpu.HBM)
    return pl.pallas_call(
        functools.partial(kernel, scans, chips_x, chips_z),
        out_shape=(
            jax.ShapeDtypeStruct(object_field.shape, F32),
            jax.ShapeDtypeStruct(probe.shape, F32),
        ),
        in_specs=[pl.BlockSpec(memory_space=pltpu.SMEM)] + [hbm] * 4,
        out_specs=(vmem, vmem),
        scratch_shapes=[
            pltpu.VMEM(probe.shape, F32),
            pltpu.VMEM(measured.shape, F32),
            field,
            pltpu.VMEM((2, 2, 2 * PATCH, 2 * PATCH), BF16),
            pltpu.VMEM((2, 4 * PATCH, 2 * PATCH), BF16),
            pltpu.VMEM((MODES, 2, ROWS, COLS), F32),
            pltpu.VMEM((3, 8, LANES), jnp.int32),
            rim, rim, rim, rim,
            field, field,
            pltpu.VMEM((2, 2 * PATCH, PATCH), BF16),
            field,
            plane, plane, plane, plane,
            field, field, field, field, field,
            rim, rim, rim, rim,
            field, plane,
            pltpu.VMEM((UNITS, 8, LANES), F32),
            pltpu.VMEM((chips_x, per_x, 8, LANES), F32),
            pltpu.VMEM((per_x, 8, LANES), F32),
            pltpu.VMEM((chips_z, per_z, 8, LANES), F32),
            pltpu.VMEM((UNITS, 8, LANES), F32),
            pltpu.VMEM((UNITS, 8, LANES), F32),
            pltpu.SemaphoreType.DMA((wire_count,)),
            pltpu.SemaphoreType.DMA((wire_count,)),
            pltpu.SemaphoreType.DMA((4,)),
        ],
        compiler_params=pltpu.CompilerParams(
            collective_id=0, has_side_effects=True, vmem_limit_bytes=60 << 20
        ),
        cost_estimate=pl.CostEstimate(flops=1 << 31, bytes_accessed=4 << 20, transcendentals=0),
    )(positions, object_field, probe, measured, jnp.asarray(dft_parts()))


def solution(mesh):
    return jax.shard_map(
        functools.partial(per_device, mesh.shape["scan"], X_CHIPS),
        mesh=mesh,
        in_specs=(
            P(None, "scan", "mode"),
            P("mode", None, None, None),
            P("scan", None, None),
            P("scan", None),
        ),
        out_specs=(P(None, "scan", "mode"), P("mode", None, None, None)),
        check_vma=False,
    )
```

```python
import functools
import math

import jax
import jax.numpy as jnp
import ml_dtypes
import numpy as np
from jax import lax
from jax.experimental import pallas as pl
from jax.experimental.pallas import tpu as pltpu
from jax.sharding import PartitionSpec as P

MESH = pl.DeviceIdType.MESH
F32 = jnp.float32
BF16 = jnp.bfloat16
X_CHIPS = 4
MODES = 4
PATCH = 256
ROWS = 96
THIRD = 32
COLS = 384
LANES = 128
CHUNK = 64
SEAM = 32
CHUNKS = PATCH // CHUNK
object_rate = 0.25


def dft_parts():
    index = np.arange(PATCH)
    angle = 2.0 * math.pi / PATCH * (np.outer(index, index) % PATCH)
    scale = 1.0 / math.sqrt(PATCH)
    return np.stack([np.cos(angle) * scale, -np.sin(angle) * scale]).astype(np.float32)


def split(value):
    high = value.astype(BF16)
    return high, (value - high.astype(F32)).astype(BF16)


def dot(left, right):
    return jnp.dot(left, right, preferred_element_type=F32)


def column_mask(corner, block, shape):
    lane = lax.broadcasted_iota(jnp.int32, shape, 1) + block * LANES
    return (lane >= corner) & (lane < corner + PATCH)


def loop(count, body, start=0):
    def step(i, carry):
        body(i)
        return carry

    lax.fori_loop(start, count, step, 0)


def tiles(start, size, unit=8):
    return pl.ds(pl.multiple_of(start, unit), size)


class Wires:
    def __init__(self, send, recv):
        self.send, self.recv, self.used, self.open = send, recv, 0, []

    def take(self, count):
        first = self.used
        self.used += count
        return first

    def copy(self, src, dst, scan, mode, slot):
        return pltpu.make_async_remote_copy(
            src_ref=src,
            dst_ref=dst,
            send_sem=self.send.at[slot],
            recv_sem=self.recv.at[slot],
            device_id=(scan, mode),
            device_id_type=MESH,
        )

    def put(self, src, dst, scan, mode):
        copy = self.copy(src, dst, scan, mode, self.take(1))
        copy.start()
        self.open.append(copy)
        return copy

    def drain(self):
        for copy in self.open:
            copy.wait_send()
        self.open = []


def kernel(
    scans, chips_x, chips_z,
    pos_ref, obj_ref, probe_hbm, meas_hbm, dft_hbm,
    new_obj_ref, new_probe_ref,
    probe_ref, meas_ref, dft_ref, row_ops, col_ops,
    strip, corners, pick_next, pick_prev, from_prev, from_next,
    patch, wave, double, stack, far, power, power_a, power_sum, power_b,
    term, term_a, term_sum, term_b, total_term, rim_up, rim_down, grad_prev, grad_next,
    pgrad, pcore, halves, parts_x, shard, parts_z, gathered, gathered_other,
    send_sem, recv_sem, local_sem,
):
    s = lax.axis_index("scan")
    m = lax.axis_index("mode")
    core = lax.rem(s, 2)
    z = lax.rem(lax.div(s, 2), chips_z)
    x = lax.div(s, 2 * chips_z)
    nxt, prv = lax.rem(s + 1, scans), lax.rem(s + scans - 1, scans)
    m_up, m_dn = lax.rem(m + 1, MODES), lax.rem(m + MODES - 1, MODES)
    pair_a = jnp.where(lax.rem(m, 2) == 0, m + 1, m - 1)
    pair_b = MODES - 1 - m
    other_core = jnp.where(core == 0, s + 1, s - 1)
    wires = Wires(send_sem, recv_sem)
    per_z = 2 * CHUNK // chips_z

    def at_x(step):
        return (lax.rem(x + step, chips_x) * chips_z + z) * 2 + core

    def at_z(step):
        return (x * chips_z + lax.rem(z + step, chips_z)) * 2 + core

    barrier = pltpu.get_barrier_semaphore()

    def greet(scan, mode):
        pl.semaphore_signal(barrier, inc=1, device_id=(scan, mode), device_id_type=MESH)

    greet(s, m_up)
    greet(s, m_dn)
    greet(nxt, m)
    greet(prv, m)
    loop(chips_x, lambda step: greet(at_x(step), m), 1)
    loop(chips_z, lambda step: greet(at_z(step), m), 1)
    pl.semaphore_wait(barrier, 2 + chips_x + chips_z)

    def cells_of(tile, part, t):
        return strip.at[tile, part, t * THIRD : (t + 1) * THIRD]

    def own_cells(part, t):
        return obj_ref.at[part, t * THIRD : (t + 1) * THIRD]

    up, dn, fwd_up, fwd_dn = {}, {}, {}, {}

    def send_own(t):
        up[0, t] = wires.put(own_cells(0, t), cells_of(m, 0, t), s, m_up)
        dn[1, t] = wires.put(own_cells(1, t), cells_of(m, 1, t), s, m_dn)
        up[1, t] = wires.put(own_cells(1, t), cells_of(m, 1, t), s, m_up)
        dn[0, t] = wires.put(own_cells(0, t), cells_of(m, 0, t), s, m_dn)

    def forward(t):
        up[0, t].wait_recv()
        fwd_up[t] = wires.put(cells_of(m_dn, 0, t), cells_of(m_dn, 0, t), s, m_up)
        dn[1, t].wait_recv()
        fwd_dn[t] = wires.put(cells_of(m_up, 1, t), cells_of(m_up, 1, t), s, m_dn)

    send_own(0)
    moves = [(obj_ref, strip.at[m]), (dft_hbm, dft_ref), (probe_hbm, probe_ref), (meas_hbm, meas_ref)]
    local = [pltpu.make_async_copy(src, dst, local_sem.at[i]) for i, (src, dst) in enumerate(moves)]
    for copy in local:
        copy.start()
    row_at = pos_ref[0, 0]
    col_at = pos_ref[0, 1]
    corners[1] = jnp.full((8, LANES), col_at, jnp.int32)
    pos_next = wires.put(corners.at[1], corners.at[0], nxt, m)
    pos_prev = wires.put(corners.at[1], corners.at[2], prv, m)
    send_own(1)
    send_own(2)
    for copy in local:
        copy.wait()
    offset = row_at - ROWS * s + ROWS
    turn = jnp.bitwise_and(col_at, PATCH - 1)

    def transforms(i):
        rows = tiles(i * CHUNK, CHUNK, CHUNK)
        low_rows = tiles(PATCH + i * CHUNK, CHUNK, CHUNK)
        for part, (re, im) in enumerate(zip(split(dft_ref[0, rows]), split(dft_ref[1, rows]))):
            at = i * 4 * CHUNK + 2 * part * CHUNK
            for which, sign in enumerate((im, -im)):
                row_ops[which, part, rows, 0:PATCH] = re
                row_ops[which, part, rows, PATCH:] = sign
                row_ops[which, part, low_rows, 0:PATCH] = -sign
                row_ops[which, part, low_rows, PATCH:] = re
                col_ops[which, tiles(at, CHUNK, CHUNK), 0:PATCH] = re
                col_ops[which, tiles(at, CHUNK, CHUNK), PATCH:] = -sign
                col_ops[which, tiles(at + CHUNK, CHUNK, CHUNK), 0:PATCH] = sign
                col_ops[which, tiles(at + CHUNK, CHUNK, CHUNK), PATCH:] = re

    loop(CHUNKS, transforms)
    forward(0)

    def window(part, start, down):
        value = double[part, tiles(start, CHUNK + SEAM, SEAM)]
        return pltpu.roll(value, down, 0)[SEAM:]

    def turn_probe(i):
        rows = tiles(i * CHUNK, CHUNK, CHUNK)
        for part in range(2):
            rolled = pltpu.roll(probe_ref[0, part, rows], turn, 1)
            double[part, rows] = rolled
            double[part, tiles(PATCH + i * CHUNK, CHUNK, CHUNK)] = rolled

    def align_probe(i):
        for part in range(2):
            wave[part, tiles(i * CHUNK, CHUNK, CHUNK)] = window(part, i * CHUNK, offset)

    loop(CHUNKS, turn_probe)
    loop(CHUNKS, align_probe)
    pos_next.wait_recv()
    pos_prev.wait_recv()

    def choose(t):
        for copy in (dn[0, t], fwd_up[t], up[1, t], fwd_dn[t]):
            copy.wait_recv()

        def pick(j):
            part = lax.div(j, THIRD // 8)
            row = t * THIRD + lax.rem(j, THIRD // 8) * 8
            rows = tiles(row, 8)
            picked = [[jnp.zeros((8, LANES), F32)] * 2 for who in range(3)]
            corner = [corners[who] for who in range(3)]
            for block in range(MODES * COLS // LANES):
                tile, inner = divmod(block, COLS // LANES)
                cells = strip[tile, part, rows, inner * LANES : (inner + 1) * LANES]
                for who in range(3):
                    mask = column_mask(corner[who], block, (8, LANES))
                    picked[who][block % 2] = jnp.where(mask, cells, picked[who][block % 2])
            for half in range(2):
                lanes = slice(half * LANES, (half + 1) * LANES)
                pick_prev[part, rows, lanes] = picked[0][half]
                patch[part, tiles(CHUNK + row, 8), lanes] = picked[1][half]
                pick_next[part, rows, lanes] = picked[2][half]

        loop(2 * THIRD // 8, pick)
        rows = slice(t * THIRD, (t + 1) * THIRD)
        return (
            wires.put(pick_next.at[:, rows], from_prev.at[:, rows], nxt, m),
            wires.put(pick_prev.at[:, rows], from_next.at[:, rows], prv, m),
        )

    def along_rows(value, which):
        high, low = split(value)
        count = value.shape[0]
        both = dot(jnp.concatenate([high, low], axis=0), row_ops[which, 0])
        return both[:count] + both[count:] + dot(high, row_ops[which, 1])

    def along_columns(i, which):
        at = i * 4 * CHUNK
        both = dot(col_ops[which, tiles(at, 4 * CHUNK, CHUNK)], stack[0])
        result = both[: 2 * CHUNK] + both[2 * CHUNK :]
        result = result + dot(col_ops[which, tiles(at, 2 * CHUNK, CHUNK)], stack[1])
        return result[:CHUNK], result[CHUNK:]

    def keep(value, i):
        high, low = split(value)
        for part in range(2):
            lanes = slice(part * PATCH, (part + 1) * PATCH)
            into = tiles(part * PATCH + i * CHUNK, CHUNK, CHUNK)
            stack[0, into] = high[:, lanes]
            stack[1, into] = low[:, lanes]

    def first_stage(i):
        i = lax.rem(i, CHUNKS)
        rows = tiles(i * CHUNK, CHUNK, CHUNK)
        p_re, p_im = wave[0, rows], wave[1, rows]
        o_re, o_im = patch[0, rows], patch[1, rows]
        exit_wave = jnp.concatenate([p_re * o_re - p_im * o_im, p_re * o_im + p_im * o_re], axis=1)
        keep(along_rows(exit_wave, 0), i)

    halos = [choose(0)]
    forward(1)
    halos.append(choose(1))
    forward(2)
    halos.append(choose(2))
    for halo in halos[:2]:
        for copy in halo:
            copy.wait_recv()
    for part in range(2):
        patch[part, 160:224] = jnp.where(s < scans - 1, from_next[part, 0:64], 0.0)
    loop(3, first_stage, 1)
    seam = lax.broadcasted_iota(jnp.int32, (SEAM, PATCH), 0)
    for copy in halos[2]:
        copy.wait_recv()
    for part in range(2):
        above = jnp.where(s > 0, from_prev[part, 0:32], 0.0)
        below = jnp.where(s < scans - 1, from_next[part, 64:96], 0.0)
        patch[part, 224:256] = jnp.where(seam >= offset, above, below)
        patch[part, 0:64] = jnp.where(s > 0, from_prev[part, 32:96], 0.0)
    loop(5, first_stage, 3)

    def chunk_of(i):
        return tiles(i * CHUNK, CHUNK, CHUNK)

    def route(i):
        even = lax.rem(i, 2) == 0
        return jnp.where(even, pair_a, pair_b), jnp.where(even, pair_b, pair_a)

    power_slot = wires.take(2 * CHUNKS)

    def power_hop(i, second):
        rows = chunk_of(i)
        src, dst = (power_sum, power_b) if second else (power, power_a)
        slot = power_slot + second * CHUNKS + i
        return wires.copy(src.at[rows], dst.at[rows], s, route(i)[second], slot)

    def to_far(i):
        rows = chunk_of(i)
        f_re, f_im = along_columns(i, 0)
        far[0, rows] = f_re
        far[1, rows] = f_im
        power[rows] = f_re * f_re + f_im * f_im
        power_hop(i, 0).start()

    def add_power(i):
        rows = chunk_of(i)
        power_hop(i, 0).wait_recv()
        power_sum[rows] = power[rows] + power_a[rows]
        power_hop(i, 1).start()

    def rescale(i):
        rows = chunk_of(i)
        power_hop(i, 1).wait_recv()
        intensity = power_sum[rows] + power_b[rows]
        factor = 1.0 - meas_ref[0, rows] / jnp.sqrt(jnp.maximum(intensity, 1.0))
        scaled = jnp.concatenate([far[0, rows] * factor, far[1, rows] * factor], axis=1)
        keep(along_rows(scaled, 1), i)

    loop(CHUNKS, to_far)
    wires.drain()
    loop(CHUNKS, add_power)
    loop(CHUNKS, rescale)

    term_slot = wires.take(2 * CHUNKS)
    core_slot = wires.take(2 * CHUNKS)

    def nth(j):
        return lax.rem(x + j, CHUNKS)

    def term_hop(j, second):
        rows = chunk_of(nth(j))
        src, dst = (term_sum, term_b) if second else (term, term_a)
        slot = term_slot + second * CHUNKS + j
        return wires.copy(src.at[:, rows], dst.at[:, rows], s, route(j)[second], slot)

    def core_hop(j):
        n = nth(j)
        return wires.copy(pgrad.at[1 - core, n], pcore.at[n], other_core, m, core_slot + j - 1)

    def send_probe_terms(j):
        n = nth(j)
        for part in range(2):
            value = window(part, n * CHUNK + PATCH - SEAM, SEAM - offset)
            pgrad[part, n, 0:CHUNK] = value[:, :LANES]
            pgrad[part, n, CHUNK:] = value[:, LANES:]
        core_hop(j).start()

    def to_object(j):
        i = nth(j)
        rows = chunk_of(i)
        b_re, b_im = along_columns(i, 1)
        p_re, p_im = wave[0, rows], wave[1, rows]
        term[0, rows] = p_re * b_re + p_im * b_im
        term[1, rows] = p_re * b_im - p_im * b_re
        term_hop(j, 0).start()
        o_re, o_im = patch[0, rows], patch[1, rows]
        for part, value in enumerate((o_re * b_re + o_im * b_im, o_re * b_im - o_im * b_re)):
            value = pltpu.roll(value, PATCH - turn, 1)
            double[part, rows] = value
            double[part, tiles(PATCH + i * CHUNK, CHUNK, CHUNK)] = value

        @pl.when(j > 0)
        def _():
            send_probe_terms(j)

    loop(CHUNKS, to_object)
    send_probe_terms(CHUNKS)

    x_slot = wires.take(chips_x)
    back_x_slot = wires.take(chips_x)
    z_slot = wires.take(chips_z)
    back_z_slot = wires.take(chips_z)

    def x_hop(j):
        return wires.copy(halves.at[nth(j)], parts_x.at[j], at_x(j), m, x_slot + j)

    def add_core(j):
        n = nth(j)
        core_hop(j).wait_recv()
        halves[n] = pgrad[core, n] + pcore[n]

    def add_core_and_send(j):
        add_core(j)
        x_hop(j).start()

    loop(chips_x, add_core_and_send, 1)
    add_core(CHUNKS)

    def add_term(j):
        rows = chunk_of(nth(j))
        term_hop(j, 0).wait_recv()
        term_sum[:, rows] = term[:, rows] + term_a[:, rows]
        term_hop(j, 1).start()

    loop(CHUNKS, add_term)
    for j in range(1, chips_x):
        x_hop(j).wait_recv()
    total = halves[x]
    for j in range(1, chips_x):
        total = total + parts_x[j]
    shard[...] = total

    def z_rows(at):
        return tiles(at * per_z, per_z)

    def z_hop(j):
        there = z_rows(lax.rem(z + j, chips_z))
        return wires.copy(shard.at[there], parts_z.at[j], at_z(j), m, z_slot + j)

    loop(chips_z, lambda j: z_hop(j).start(), 1)
    loop(CHUNKS, lambda i: (power_hop(i, 0).wait_send(), power_hop(i, 1).wait_send()))

    def add_z(j, total):
        z_hop(j).wait_recv()
        return total + parts_z[j]

    total = lax.fori_loop(1, chips_z, add_z, shard[z_rows(z)])
    first = z * per_z
    half = lax.div(first, CHUNK) if per_z <= CHUNK else 0
    scale = 1.0 / math.sqrt(scans)
    old_rows = tiles(x * CHUNK + lax.rem(first, CHUNK), per_z)
    old = probe_ref[0, core, old_rows, tiles(half * LANES, LANES, LANES)]
    gathered[x, z_rows(z)] = old - total * scale

    def back_z_hop(j):
        mine = gathered.at[x, z_rows(z)]
        return wires.copy(mine, mine, at_z(j), m, back_z_slot + j)

    loop(chips_z, lambda j: back_z_hop(j).start(), 1)

    def total_terms(j):
        rows = chunk_of(nth(j))
        term_hop(j, 1).wait_recv()
        total_term[:, rows] = term_sum[:, rows] + term_b[:, rows]

    loop(CHUNKS, total_terms)
    for part in range(2):
        edge = total_term[part, 224:256]
        rim_up[part, 0:32] = jnp.where(seam >= offset, edge, 0.0)
        rim_up[part, 32:96] = total_term[part, 0:64]
        rim_down[part, 0:64] = total_term[part, 160:224]
        rim_down[part, 64:96] = jnp.where(seam < offset, edge, 0.0)
    to_prev = wires.put(rim_up, grad_next, prv, m)
    to_next = wires.put(rim_down, grad_prev, nxt, m)

    loop(chips_z, lambda j: back_z_hop(j).wait_recv(), 1)

    def back_x_hop(j):
        mine = gathered.at[x]
        return wires.copy(mine, mine, at_x(j), m, back_x_slot + j)

    def back_core_hop(j):
        mine = nth(CHUNKS - j)
        return wires.copy(gathered.at[mine], gathered_other.at[mine], other_core, m, core_slot + CHUNKS + j)

    loop(chips_x, lambda j: back_x_hop(j).start(), 1)
    back_core_hop(0).start()

    loop(CHUNKS, lambda j: (term_hop(j, 0).wait_send(), term_hop(j, 1).wait_send()))
    loop(CHUNKS + 1, lambda j: core_hop(j).wait_send(), 1)
    loop(chips_x, lambda j: x_hop(j).wait_send(), 1)
    loop(chips_z, lambda j: (z_hop(j).wait_send(), back_z_hop(j).wait_send()), 1)

    to_prev.wait_recv()
    to_next.wait_recv()
    shape = (ROWS, LANES)
    for inner in range(COLS // LANES):
        block = m * (COLS // LANES) + inner
        lanes = tiles(lax.rem(block, 2) * LANES, LANES, LANES)
        masks = [column_mask(jnp.broadcast_to(corners[who, 0:1, :], shape), block, shape) for who in range(3)]
        here = slice(inner * LANES, (inner + 1) * LANES)
        for part in range(2):
            above = jnp.where(s > 0, grad_prev[part, :, lanes], 0.0)
            below = jnp.where(s < scans - 1, grad_next[part, :, lanes], 0.0)
            total = jnp.where(masks[1], total_term[part, CHUNK : CHUNK + ROWS, lanes], 0.0)
            total = total + jnp.where(masks[0], above, 0.0) + jnp.where(masks[2], below, 0.0)
            new_obj_ref[part, :, here] = strip[m, part, :, here] - object_rate * total
    wires.drain()

    def pass_on(j):
        back_x_hop(j).wait_recv()
        back_core_hop(j).start()

    loop(chips_x, pass_on, 1)

    def put_probe(which, source, n):
        rows = chunk_of(n)
        new_probe_ref[0, which, rows, 0:LANES] = source[n, 0:CHUNK]
        new_probe_ref[0, which, rows, LANES:] = source[n, CHUNK:]

    loop(CHUNKS, lambda n: put_probe(core, gathered, n))

    def take_core(j):
        back_core_hop(j).wait_recv()
        put_probe(1 - core, gathered_other, nth(CHUNKS - j))

    loop(CHUNKS, take_core)
    loop(CHUNKS, lambda j: back_core_hop(j).wait_send())
    loop(chips_x, lambda j: back_x_hop(j).wait_send(), 1)


def per_device(scans, chips_x, object_field, probe, measured, positions):
    chips_z = scans // (2 * chips_x)
    per_z = 2 * CHUNK // chips_z
    wire_count = 28 + 6 * CHUNKS + 2 * (chips_x + chips_z)
    field = pltpu.VMEM((2, PATCH, PATCH), F32)
    plane = pltpu.VMEM((PATCH, PATCH), F32)
    rim = pltpu.VMEM((2, ROWS, PATCH), F32)
    share = pltpu.VMEM((CHUNKS, 2 * CHUNK, LANES), F32)
    vmem = pl.BlockSpec(memory_space=pltpu.VMEM)
    hbm = pl.BlockSpec(memory_space=pltpu.HBM)
    return pl.pallas_call(
        functools.partial(kernel, scans, chips_x, chips_z),
        out_shape=(
            jax.ShapeDtypeStruct(object_field.shape, F32),
            jax.ShapeDtypeStruct(probe.shape, F32),
        ),
        in_specs=[pl.BlockSpec(memory_space=pltpu.SMEM)] + [hbm] * 4,
        out_specs=(vmem, vmem),
        scratch_shapes=[
            pltpu.VMEM(probe.shape, F32),
            pltpu.VMEM(measured.shape, F32),
            field,
            pltpu.VMEM((2, 2, 2 * PATCH, 2 * PATCH), BF16),
            pltpu.VMEM((2, 4 * PATCH, 2 * PATCH), BF16),
            pltpu.VMEM((MODES, 2, ROWS, COLS), F32),
            pltpu.VMEM((3, 8, LANES), jnp.int32),
            rim, rim, rim, rim,
            field, field,
            pltpu.VMEM((2, 2 * PATCH, PATCH), F32),
            pltpu.VMEM((2, 2 * PATCH, PATCH), BF16),
            field,
            plane, plane, plane, plane,
            field, field, field, field, field,
            rim, rim, rim, rim,
            pltpu.VMEM((2, CHUNKS, 2 * CHUNK, LANES), F32),
            share, share, share,
            pltpu.VMEM((2 * CHUNK, LANES), F32),
            pltpu.VMEM((chips_z, per_z, LANES), F32),
            share, share,
            pltpu.SemaphoreType.DMA((wire_count,)),
            pltpu.SemaphoreType.DMA((wire_count,)),
            pltpu.SemaphoreType.DMA((4,)),
        ],
        compiler_params=pltpu.CompilerParams(
            collective_id=0, has_side_effects=True, vmem_limit_bytes=60 << 20
        ),
        cost_estimate=pl.CostEstimate(flops=1 << 31, bytes_accessed=4 << 20, transcendentals=0),
    )(positions, object_field, probe, measured, jnp.asarray(dft_parts()))


def solution(mesh):
    return jax.shard_map(
        functools.partial(per_device, mesh.shape["scan"], X_CHIPS),
        mesh=mesh,
        in_specs=(
            P(None, "scan", "mode"),
            P("mode", None, None, None),
            P("scan", None, None),
            P("scan", None),
        ),
        out_specs=(P(None, "scan", "mode"), P("mode", None, None, None)),
        check_vma=False,
    )
```

```python
import functools
import math

import jax
import jax.numpy as jnp
import ml_dtypes
import numpy as np
from jax import lax
from jax.experimental import pallas as pl
from jax.experimental.pallas import tpu as pltpu
from jax.sharding import PartitionSpec as P

MESH = pl.DeviceIdType.MESH
F32 = jnp.float32
BF16 = jnp.bfloat16
X_CHIPS = 4
MODES = 4
PATCH = 256
ROWS = 96
THIRD = 32
COLS = 384
LANES = 128
CHUNK = 64
SEAM = 32
CHUNKS = PATCH // CHUNK
object_rate = 0.25


def dft_parts():
    index = np.arange(PATCH)
    angle = 2.0 * math.pi / PATCH * (np.outer(index, index) % PATCH)
    scale = 1.0 / math.sqrt(PATCH)
    return np.stack([np.cos(angle) * scale, -np.sin(angle) * scale]).astype(np.float32)


def split(value):
    high = value.astype(BF16)
    return high, (value - high.astype(F32)).astype(BF16)


def dot(left, right):
    return jnp.dot(left, right, preferred_element_type=F32)


def column_mask(corner, block, shape):
    lane = lax.broadcasted_iota(jnp.int32, shape, 1) + block * LANES
    return (lane >= corner) & (lane < corner + PATCH)


def loop(count, body, start=0):
    def step(i, carry):
        body(i)
        return carry

    lax.fori_loop(start, count, step, 0)


def tiles(start, size, unit=8):
    return pl.ds(pl.multiple_of(start, unit), size)


class Wires:
    def __init__(self, send, recv):
        self.send, self.recv, self.used, self.open = send, recv, 0, []

    def take(self, count):
        first = self.used
        self.used += count
        return first

    def copy(self, src, dst, scan, mode, slot):
        return pltpu.make_async_remote_copy(
            src_ref=src,
            dst_ref=dst,
            send_sem=self.send.at[slot],
            recv_sem=self.recv.at[slot],
            device_id=(scan, mode),
            device_id_type=MESH,
        )

    def put(self, src, dst, scan, mode):
        copy = self.copy(src, dst, scan, mode, self.take(1))
        copy.start()
        self.open.append(copy)
        return copy

    def drain(self):
        for copy in self.open:
            copy.wait_send()
        self.open = []


def kernel(
    scans, chips_x, chips_z,
    pos_ref, obj_ref, probe_hbm, meas_hbm, dft_hbm,
    obj_out, probe_out,
    probe_ref, meas_ref, dft_ref, row_ops, col_ops,
    strip, corners, pick_next, pick_prev, from_prev, from_next,
    patch, wave, double, stack, far, power, power_a, power_sum, power_b,
    term, term_a, term_sum, term_b, total_term, rim_up, rim_down, grad_prev, grad_next,
    pgrad, pcore, halves, parts_x, shard, parts_z, gathered, gathered_other,
    new_obj, send_sem, recv_sem, local_sem, out_sem,
):
    s = lax.axis_index("scan")
    m = lax.axis_index("mode")
    core = lax.rem(s, 2)
    z = lax.rem(lax.div(s, 2), chips_z)
    x = lax.div(s, 2 * chips_z)
    nxt, prv = lax.rem(s + 1, scans), lax.rem(s + scans - 1, scans)
    m_up, m_dn = lax.rem(m + 1, MODES), lax.rem(m + MODES - 1, MODES)
    pair_a = jnp.where(lax.rem(m, 2) == 0, m + 1, m - 1)
    pair_b = MODES - 1 - m
    other_core = jnp.where(core == 0, s + 1, s - 1)
    wires = Wires(send_sem, recv_sem)
    per_z = 2 * CHUNK // chips_z

    def at_x(step):
        return (lax.rem(x + step, chips_x) * chips_z + z) * 2 + core

    def at_z(step):
        return (x * chips_z + lax.rem(z + step, chips_z)) * 2 + core

    barrier = pltpu.get_barrier_semaphore()

    def greet(scan, mode):
        pl.semaphore_signal(barrier, inc=1, device_id=(scan, mode), device_id_type=MESH)

    greet(s, m_up)
    greet(s, m_dn)
    greet(nxt, m)
    greet(prv, m)
    loop(chips_x, lambda step: greet(at_x(step), m), 1)
    loop(chips_z, lambda step: greet(at_z(step), m), 1)
    pl.semaphore_wait(barrier, 2 + chips_x + chips_z)

    def cells_of(tile, part, t):
        return strip.at[tile, part, t * THIRD : (t + 1) * THIRD]

    def own_cells(part, t):
        return obj_ref.at[part, t * THIRD : (t + 1) * THIRD]

    up, dn, fwd_up, fwd_dn = {}, {}, {}, {}

    def send_own(t):
        up[0, t] = wires.put(own_cells(0, t), cells_of(m, 0, t), s, m_up)
        dn[1, t] = wires.put(own_cells(1, t), cells_of(m, 1, t), s, m_dn)
        up[1, t] = wires.put(own_cells(1, t), cells_of(m, 1, t), s, m_up)
        dn[0, t] = wires.put(own_cells(0, t), cells_of(m, 0, t), s, m_dn)

    def forward(t):
        up[0, t].wait_recv()
        fwd_up[t] = wires.put(cells_of(m_dn, 0, t), cells_of(m_dn, 0, t), s, m_up)
        dn[1, t].wait_recv()
        fwd_dn[t] = wires.put(cells_of(m_up, 1, t), cells_of(m_up, 1, t), s, m_dn)

    send_own(0)
    moves = [(obj_ref, strip.at[m]), (dft_hbm, dft_ref), (probe_hbm, probe_ref), (meas_hbm, meas_ref)]
    local = [pltpu.make_async_copy(src, dst, local_sem.at[i]) for i, (src, dst) in enumerate(moves)]
    for copy in local:
        copy.start()
    row_at = pos_ref[0, 0]
    col_at = pos_ref[0, 1]
    corners[1] = jnp.full((8, LANES), col_at, jnp.int32)
    pos_next = wires.put(corners.at[1], corners.at[0], nxt, m)
    pos_prev = wires.put(corners.at[1], corners.at[2], prv, m)
    send_own(1)
    send_own(2)
    for copy in local:
        copy.wait()
    offset = row_at - ROWS * s + ROWS
    turn = jnp.bitwise_and(col_at, PATCH - 1)

    def transforms(i):
        rows = tiles(i * CHUNK, CHUNK, CHUNK)
        low_rows = tiles(PATCH + i * CHUNK, CHUNK, CHUNK)
        for part, (re, im) in enumerate(zip(split(dft_ref[0, rows]), split(dft_ref[1, rows]))):
            at = i * 4 * CHUNK + 2 * part * CHUNK
            for which, sign in enumerate((im, -im)):
                row_ops[which, part, rows, 0:PATCH] = re
                row_ops[which, part, rows, PATCH:] = sign
                row_ops[which, part, low_rows, 0:PATCH] = -sign
                row_ops[which, part, low_rows, PATCH:] = re
                col_ops[which, tiles(at, CHUNK, CHUNK), 0:PATCH] = re
                col_ops[which, tiles(at, CHUNK, CHUNK), PATCH:] = -sign
                col_ops[which, tiles(at + CHUNK, CHUNK, CHUNK), 0:PATCH] = sign
                col_ops[which, tiles(at + CHUNK, CHUNK, CHUNK), PATCH:] = re

    loop(CHUNKS, transforms)
    forward(0)

    def window(part, start, down):
        value = double[part, tiles(start, CHUNK + SEAM, SEAM)]
        return pltpu.roll(value, down, 0)[SEAM:]

    def turn_probe(i):
        rows = tiles(i * CHUNK, CHUNK, CHUNK)
        for part in range(2):
            rolled = pltpu.roll(probe_ref[0, part, rows], turn, 1)
            double[part, rows] = rolled
            double[part, tiles(PATCH + i * CHUNK, CHUNK, CHUNK)] = rolled

    def align_probe(i):
        for part in range(2):
            wave[part, tiles(i * CHUNK, CHUNK, CHUNK)] = window(part, i * CHUNK, offset)

    loop(CHUNKS, turn_probe)
    loop(CHUNKS, align_probe)
    pos_next.wait_recv()
    pos_prev.wait_recv()

    def choose(t):
        for copy in (dn[0, t], fwd_up[t], up[1, t], fwd_dn[t]):
            copy.wait_recv()

        def pick(j):
            part = lax.div(j, THIRD // 8)
            row = t * THIRD + lax.rem(j, THIRD // 8) * 8
            rows = tiles(row, 8)
            picked = [[jnp.zeros((8, LANES), F32)] * 2 for who in range(3)]
            corner = [corners[who] for who in range(3)]
            for block in range(MODES * COLS // LANES):
                tile, inner = divmod(block, COLS // LANES)
                cells = strip[tile, part, rows, inner * LANES : (inner + 1) * LANES]
                for who in range(3):
                    mask = column_mask(corner[who], block, (8, LANES))
                    picked[who][block % 2] = jnp.where(mask, cells, picked[who][block % 2])
            for half in range(2):
                lanes = slice(half * LANES, (half + 1) * LANES)
                pick_prev[part, rows, lanes] = picked[0][half]
                patch[part, tiles(CHUNK + row, 8), lanes] = picked[1][half]
                pick_next[part, rows, lanes] = picked[2][half]

        loop(2 * THIRD // 8, pick)
        rows = slice(t * THIRD, (t + 1) * THIRD)
        return (
            wires.put(pick_next.at[:, rows], from_prev.at[:, rows], nxt, m),
            wires.put(pick_prev.at[:, rows], from_next.at[:, rows], prv, m),
        )

    def along_rows(value, which):
        high, low = split(value)
        count = value.shape[0]
        both = dot(jnp.concatenate([high, low], axis=0), row_ops[which, 0])
        return both[:count] + both[count:] + dot(high, row_ops[which, 1])

    def along_columns(i, which):
        at = i * 4 * CHUNK
        both = dot(col_ops[which, tiles(at, 4 * CHUNK, CHUNK)], stack[0])
        result = both[: 2 * CHUNK] + both[2 * CHUNK :]
        result = result + dot(col_ops[which, tiles(at, 2 * CHUNK, CHUNK)], stack[1])
        return result[:CHUNK], result[CHUNK:]

    def keep(value, i):
        high, low = split(value)
        for part in range(2):
            lanes = slice(part * PATCH, (part + 1) * PATCH)
            into = tiles(part * PATCH + i * CHUNK, CHUNK, CHUNK)
            stack[0, into] = high[:, lanes]
            stack[1, into] = low[:, lanes]

    def first_stage(i):
        i = lax.rem(i, CHUNKS)
        rows = tiles(i * CHUNK, CHUNK, CHUNK)
        p_re, p_im = wave[0, rows], wave[1, rows]
        o_re, o_im = patch[0, rows], patch[1, rows]
        exit_wave = jnp.concatenate([p_re * o_re - p_im * o_im, p_re * o_im + p_im * o_re], axis=1)
        keep(along_rows(exit_wave, 0), i)

    halos = [choose(0)]
    forward(1)
    halos.append(choose(1))
    forward(2)
    halos.append(choose(2))
    for halo in halos[:2]:
        for copy in halo:
            copy.wait_recv()
    for part in range(2):
        patch[part, 160:224] = jnp.where(s < scans - 1, from_next[part, 0:64], 0.0)
    loop(3, first_stage, 1)
    seam = lax.broadcasted_iota(jnp.int32, (SEAM, PATCH), 0)
    for copy in halos[2]:
        copy.wait_recv()
    for part in range(2):
        above = jnp.where(s > 0, from_prev[part, 0:32], 0.0)
        below = jnp.where(s < scans - 1, from_next[part, 64:96], 0.0)
        patch[part, 224:256] = jnp.where(seam >= offset, above, below)
        patch[part, 0:64] = jnp.where(s > 0, from_prev[part, 32:96], 0.0)
    loop(5, first_stage, 3)

    def chunk_of(i):
        return tiles(i * CHUNK, CHUNK, CHUNK)

    def route(i):
        even = lax.rem(i, 2) == 0
        return jnp.where(even, pair_a, pair_b), jnp.where(even, pair_b, pair_a)

    power_slot = wires.take(2 * CHUNKS)

    def power_hop(i, second):
        rows = chunk_of(i)
        src, dst = (power_sum, power_b) if second else (power, power_a)
        slot = power_slot + second * CHUNKS + i
        return wires.copy(src.at[rows], dst.at[rows], s, route(i)[second], slot)

    def to_far(i):
        rows = chunk_of(i)
        f_re, f_im = along_columns(i, 0)
        far[0, rows] = f_re
        far[1, rows] = f_im
        power[rows] = f_re * f_re + f_im * f_im
        power_hop(i, 0).start()

    def add_power(i):
        rows = chunk_of(i)
        power_hop(i, 0).wait_recv()
        power_sum[rows] = power[rows] + power_a[rows]
        power_hop(i, 1).start()

    def rescale(i):
        rows = chunk_of(i)
        power_hop(i, 1).wait_recv()
        intensity = power_sum[rows] + power_b[rows]
        factor = 1.0 - meas_ref[0, rows] / jnp.sqrt(jnp.maximum(intensity, 1.0))
        scaled = jnp.concatenate([far[0, rows] * factor, far[1, rows] * factor], axis=1)
        keep(along_rows(scaled, 1), i)

    loop(CHUNKS, to_far)
    wires.drain()
    loop(CHUNKS, add_power)
    loop(CHUNKS, rescale)

    term_slot = wires.take(2 * CHUNKS)
    core_slot = wires.take(2 * CHUNKS)

    def nth(j):
        return lax.rem(x + j, CHUNKS)

    def term_hop(j, second):
        rows = chunk_of(nth(j))
        src, dst = (term_sum, term_b) if second else (term, term_a)
        slot = term_slot + second * CHUNKS + j
        return wires.copy(src.at[:, rows], dst.at[:, rows], s, route(j)[second], slot)

    def core_hop(j):
        n = nth(j)
        return wires.copy(pgrad.at[1 - core, n], pcore.at[n], other_core, m, core_slot + j - 1)

    def send_probe_terms(j):
        n = nth(j)
        for part in range(2):
            value = window(part, n * CHUNK + PATCH - SEAM, SEAM - offset)
            pgrad[part, n, 0:CHUNK] = value[:, :LANES]
            pgrad[part, n, CHUNK:] = value[:, LANES:]
        core_hop(j).start()

    def to_object(j):
        i = nth(j)
        rows = chunk_of(i)
        b_re, b_im = along_columns(i, 1)
        p_re, p_im = wave[0, rows], wave[1, rows]
        term[0, rows] = p_re * b_re + p_im * b_im
        term[1, rows] = p_re * b_im - p_im * b_re
        term_hop(j, 0).start()
        o_re, o_im = patch[0, rows], patch[1, rows]
        for part, value in enumerate((o_re * b_re + o_im * b_im, o_re * b_im - o_im * b_re)):
            value = pltpu.roll(value, PATCH - turn, 1)
            double[part, rows] = value
            double[part, tiles(PATCH + i * CHUNK, CHUNK, CHUNK)] = value

        @pl.when(j > 0)
        def _():
            send_probe_terms(j)

    loop(CHUNKS, to_object)
    send_probe_terms(CHUNKS)

    x_slot = wires.take(2 * chips_x)
    back_x_slot = wires.take(2 * chips_x)
    z_slot = wires.take(chips_z)
    back_z_slot = wires.take(chips_z)

    block_z = max(chips_z // 2, 1)
    blocks = chips_z // block_z

    def block_rows(b):
        return pl.ds(b * block_z * per_z, block_z * per_z)

    def x_hop(j, b):
        rows = block_rows(b)
        return wires.copy(halves.at[nth(j), rows], parts_x.at[j, rows], at_x(j), m, x_slot + 2 * j + b)

    def add_core(j):
        n = nth(j)
        core_hop(j).wait_recv()
        halves[n] = pgrad[core, n] + pcore[n]

    def add_core_and_send(j):
        add_core(j)
        x_hop(j, 0).start()

    loop(chips_x, add_core_and_send, 1)
    for b in range(1, blocks):
        loop(chips_x, lambda j: x_hop(j, b).start(), 1)
    add_core(CHUNKS)

    def add_term(j):
        rows = chunk_of(nth(j))
        term_hop(j, 0).wait_recv()
        term_sum[:, rows] = term[:, rows] + term_a[:, rows]
        term_hop(j, 1).start()

    loop(CHUNKS, add_term)
    def z_rows(at):
        return tiles(at * per_z, per_z)

    def z_hop(j):
        there = z_rows(lax.rem(z + j, chips_z))
        return wires.copy(shard.at[there], parts_z.at[j], at_z(j), m, z_slot + j)

    for b in range(blocks):
        rows = block_rows(b)
        total = halves[x, rows]
        for j in range(1, chips_x):
            x_hop(j, b).wait_recv()
            total = total + parts_x[j, rows]
        shard[rows] = total

        def send_z(i):
            j = lax.rem(b * block_z + lax.rem(z + i, block_z) - z + chips_z, chips_z)

            @pl.when(j > 0)
            def _():
                z_hop(j).start()

        loop(block_z, send_z)

    loop(CHUNKS, lambda i: (power_hop(i, 0).wait_send(), power_hop(i, 1).wait_send()))

    def add_z(j, total):
        z_hop(j).wait_recv()
        return total + parts_z[j]

    total = lax.fori_loop(1, chips_z, add_z, shard[z_rows(z)])
    first = z * per_z
    half = lax.div(first, CHUNK) if per_z <= CHUNK else 0
    scale = 1.0 / math.sqrt(scans)
    old_rows = tiles(x * CHUNK + lax.rem(first, CHUNK), per_z)
    old = probe_ref[0, core, old_rows, tiles(half * LANES, LANES, LANES)]
    gathered[x, z_rows(z)] = old - total * scale

    def back_z_hop(j):
        mine = gathered.at[x, z_rows(z)]
        return wires.copy(mine, mine, at_z(j), m, back_z_slot + j)

    loop(chips_z, lambda j: back_z_hop(j).start(), 1)

    def total_terms(j):
        rows = chunk_of(nth(j))
        term_hop(j, 1).wait_recv()
        total_term[:, rows] = term_sum[:, rows] + term_b[:, rows]

    loop(CHUNKS, total_terms)
    for part in range(2):
        edge = total_term[part, 224:256]
        rim_up[part, 0:32] = jnp.where(seam >= offset, edge, 0.0)
        rim_up[part, 32:96] = total_term[part, 0:64]
        rim_down[part, 0:64] = total_term[part, 160:224]
        rim_down[part, 64:96] = jnp.where(seam < offset, edge, 0.0)
    to_prev = wires.put(rim_up, grad_next, prv, m)
    to_next = wires.put(rim_down, grad_prev, nxt, m)

    def back_x_hop(j, b):
        mine = gathered.at[x, block_rows(b)]
        return wires.copy(mine, mine, at_x(j), m, back_x_slot + 2 * j + b)

    for b in range(blocks):

        def take_z(i):
            j = lax.rem(z - b * block_z - i + chips_z, chips_z)

            @pl.when(j > 0)
            def _():
                back_z_hop(j).wait_recv()

        loop(block_z, take_z)
        loop(chips_x, lambda j: back_x_hop(j, b).start(), 1)

    def back_core_hop(j):
        mine = nth(CHUNKS - j)
        return wires.copy(gathered.at[mine], gathered_other.at[mine], other_core, m, core_slot + CHUNKS + j)

    back_core_hop(0).start()

    loop(CHUNKS, lambda j: (term_hop(j, 0).wait_send(), term_hop(j, 1).wait_send()))
    loop(CHUNKS + 1, lambda j: core_hop(j).wait_send(), 1)
    for b in range(blocks):
        loop(chips_x, lambda j: x_hop(j, b).wait_send(), 1)
    loop(chips_z, lambda j: (z_hop(j).wait_send(), back_z_hop(j).wait_send()), 1)

    to_prev.wait_recv()
    to_next.wait_recv()
    shape = (ROWS, LANES)
    for inner in range(COLS // LANES):
        block = m * (COLS // LANES) + inner
        lanes = tiles(lax.rem(block, 2) * LANES, LANES, LANES)
        masks = [column_mask(jnp.broadcast_to(corners[who, 0:1, :], shape), block, shape) for who in range(3)]
        here = slice(inner * LANES, (inner + 1) * LANES)
        for part in range(2):
            above = jnp.where(s > 0, grad_prev[part, :, lanes], 0.0)
            below = jnp.where(s < scans - 1, grad_next[part, :, lanes], 0.0)
            total = jnp.where(masks[1], total_term[part, CHUNK : CHUNK + ROWS, lanes], 0.0)
            total = total + jnp.where(masks[0], above, 0.0) + jnp.where(masks[2], below, 0.0)
            new_obj[part, :, here] = strip[m, part, :, here] - object_rate * total
    obj_copy = pltpu.make_async_copy(new_obj, obj_out, out_sem.at[0])
    obj_copy.start()
    wires.drain()

    def probe_copy(which, source, n, half, slot):
        return pltpu.make_async_copy(
            source.at[n, half * CHUNK : (half + 1) * CHUNK],
            probe_out.at[0, which, chunk_of(n), half * LANES : (half + 1) * LANES],
            out_sem.at[slot],
        )

    def mine_copy(j, half):
        return probe_copy(core, gathered, nth(CHUNKS - j), half, 1 + 2 * j + half)

    def other_copy(j, half):
        return probe_copy(1 - core, gathered_other, nth(CHUNKS - j), half, 1 + 2 * (CHUNKS + j) + half)

    def put_both(copy, j):
        copy(j, 0).start()
        copy(j, 1).start()

    def wait_both(copy, j):
        copy(j, 0).wait()
        copy(j, 1).wait()

    put_both(mine_copy, 0)

    def pass_on(j):
        for b in range(blocks):
            back_x_hop(j, b).wait_recv()
        back_core_hop(j).start()
        put_both(mine_copy, j)

    loop(chips_x, pass_on, 1)

    def take_core(j):
        back_core_hop(j).wait_recv()
        put_both(other_copy, j)

    loop(CHUNKS, take_core)
    loop(CHUNKS, lambda j: back_core_hop(j).wait_send())
    for b in range(blocks):
        loop(chips_x, lambda j: back_x_hop(j, b).wait_send(), 1)
    obj_copy.wait()
    loop(CHUNKS, lambda j: (wait_both(mine_copy, j), wait_both(other_copy, j)))


PIECES = 4


def placing(obj_in, probe_in, obj_out, probe_out, sem):
    copies = []
    for src, dst, dim in ((obj_in, obj_out, 1), (probe_in, probe_out, 2)):
        size = src.shape[dim] // PIECES
        for i in range(PIECES):
            where = (slice(None),) * dim + (slice(i * size, (i + 1) * size),)
            copies.append(pltpu.make_async_copy(src.at[where], dst.at[where], sem.at[len(copies)]))
    for copy in copies:
        copy.start()
    for copy in copies:
        copy.wait()


def per_device(scans, chips_x, object_field, probe, measured, positions):
    chips_z = scans // (2 * chips_x)
    per_z = 2 * CHUNK // chips_z
    wire_count = 28 + 6 * CHUNKS + 4 * chips_x + 2 * chips_z
    field = pltpu.VMEM((2, PATCH, PATCH), F32)
    plane = pltpu.VMEM((PATCH, PATCH), F32)
    rim = pltpu.VMEM((2, ROWS, PATCH), F32)
    share = pltpu.VMEM((CHUNKS, 2 * CHUNK, LANES), F32)
    hbm = pl.BlockSpec(memory_space=pltpu.HBM)
    out_shape = (
        jax.ShapeDtypeStruct(object_field.shape, F32),
        jax.ShapeDtypeStruct(probe.shape, F32),
    )
    results = pl.pallas_call(
        functools.partial(kernel, scans, chips_x, chips_z),
        out_shape=out_shape,
        in_specs=[pl.BlockSpec(memory_space=pltpu.SMEM)] + [hbm] * 4,
        out_specs=(hbm, hbm),
        scratch_shapes=[
            pltpu.VMEM(probe.shape, F32),
            pltpu.VMEM(measured.shape, F32),
            field,
            pltpu.VMEM((2, 2, 2 * PATCH, 2 * PATCH), BF16),
            pltpu.VMEM((2, 4 * PATCH, 2 * PATCH), BF16),
            pltpu.VMEM((MODES, 2, ROWS, COLS), F32),
            pltpu.VMEM((3, 8, LANES), jnp.int32),
            rim, rim, rim, rim,
            field, field,
            pltpu.VMEM((2, 2 * PATCH, PATCH), F32),
            pltpu.VMEM((2, 2 * PATCH, PATCH), BF16),
            field,
            plane, plane, plane, plane,
            field, field, field, field, field,
            rim, rim, rim, rim,
            pltpu.VMEM((2, CHUNKS, 2 * CHUNK, LANES), F32),
            share, share, share,
            pltpu.VMEM((2 * CHUNK, LANES), F32),
            pltpu.VMEM((chips_z, per_z, LANES), F32),
            share, share,
            pltpu.VMEM(object_field.shape, F32),
            pltpu.SemaphoreType.DMA((wire_count,)),
            pltpu.SemaphoreType.DMA((wire_count,)),
            pltpu.SemaphoreType.DMA((4,)),
            pltpu.SemaphoreType.DMA((1 + 4 * CHUNKS,)),
        ],
        compiler_params=pltpu.CompilerParams(
            collective_id=0, has_side_effects=True, vmem_limit_bytes=60 << 20
        ),
        cost_estimate=pl.CostEstimate(flops=1 << 31, bytes_accessed=4 << 20, transcendentals=0),
    )(positions, object_field, probe, measured, jnp.asarray(dft_parts()))
    return pl.pallas_call(
        placing,
        out_shape=out_shape,
        in_specs=[hbm, hbm],
        out_specs=(hbm, hbm),
        scratch_shapes=[pltpu.SemaphoreType.DMA((2 * PIECES,))],
        compiler_params=pltpu.CompilerParams(vmem_limit_bytes=60 << 20),
    )(*results)


def solution(mesh):
    return jax.shard_map(
        functools.partial(per_device, mesh.shape["scan"], X_CHIPS),
        mesh=mesh,
        in_specs=(
            P(None, "scan", "mode"),
            P("mode", None, None, None),
            P("scan", None, None),
            P("scan", None),
        ),
        out_specs=(P(None, "scan", "mode"), P("mode", None, None, None)),
        check_vma=False,
    )
```

```python
import functools
import math

import jax
import jax.numpy as jnp
import ml_dtypes
import numpy as np
from jax import lax
from jax.experimental import pallas as pl
from jax.experimental.pallas import tpu as pltpu
from jax.sharding import PartitionSpec as P

MESH = pl.DeviceIdType.MESH
F32 = jnp.float32
BF16 = jnp.bfloat16
X_CHIPS = 4
MODES = 4
PATCH = 256
ROWS = 96
THIRD = 32
COLS = 384
LANES = 128
CHUNK = 64
SEAM = 32
CHUNKS = PATCH // CHUNK
object_rate = 0.25


def dft_parts():
    index = np.arange(PATCH)
    angle = 2.0 * math.pi / PATCH * (np.outer(index, index) % PATCH)
    scale = 1.0 / math.sqrt(PATCH)
    return np.stack([np.cos(angle) * scale, -np.sin(angle) * scale]).astype(np.float32)


def split(value):
    high = value.astype(BF16)
    return high, (value - high.astype(F32)).astype(BF16)


def dot(left, right):
    return jnp.dot(left, right, preferred_element_type=F32)


def column_mask(corner, block, shape):
    lane = lax.broadcasted_iota(jnp.int32, shape, 1) + block * LANES
    return (lane >= corner) & (lane < corner + PATCH)


def loop(count, body, start=0):
    def step(i, carry):
        body(i)
        return carry

    lax.fori_loop(start, count, step, 0)


def tiles(start, size, unit=8):
    return pl.ds(pl.multiple_of(start, unit), size)


class Wires:
    def __init__(self, send, recv):
        self.send, self.recv, self.used, self.open = send, recv, 0, []

    def take(self, count):
        first = self.used
        self.used += count
        return first

    def copy(self, src, dst, scan, mode, slot):
        return pltpu.make_async_remote_copy(
            src_ref=src,
            dst_ref=dst,
            send_sem=self.send.at[slot],
            recv_sem=self.recv.at[slot],
            device_id=(scan, mode),
            device_id_type=MESH,
        )

    def put(self, src, dst, scan, mode):
        copy = self.copy(src, dst, scan, mode, self.take(1))
        copy.start()
        self.open.append(copy)
        return copy

    def drain(self):
        for copy in self.open:
            copy.wait_send()
        self.open = []


def kernel(
    scans, chips_x, chips_z,
    pos_ref, obj_ref, probe_hbm, meas_hbm, dft_hbm,
    obj_out, probe_out,
    probe_ref, meas_ref, dft_ref, row_ops, col_ops,
    strip, corners, pick_next, pick_prev, from_prev, from_next,
    patch, wave, double, stack, far, power, power_a, power_sum, power_b,
    term, term_a, term_sum, term_b, total_term, rim_up, rim_down, grad_prev, grad_next,
    pgrad, pcore, halves, parts_x, shard, parts_z, gathered, gathered_other,
    new_obj, send_sem, recv_sem, local_sem, out_sem,
):
    s = lax.axis_index("scan")
    m = lax.axis_index("mode")
    core = lax.rem(s, 2)
    z = lax.rem(lax.div(s, 2), chips_z)
    x = lax.div(s, 2 * chips_z)
    nxt, prv = lax.rem(s + 1, scans), lax.rem(s + scans - 1, scans)
    m_up, m_dn = lax.rem(m + 1, MODES), lax.rem(m + MODES - 1, MODES)
    pair_a = jnp.where(lax.rem(m, 2) == 0, m + 1, m - 1)
    pair_b = MODES - 1 - m
    other_core = jnp.where(core == 0, s + 1, s - 1)
    wires = Wires(send_sem, recv_sem)
    per_z = 2 * CHUNK // chips_z

    def at_x(step):
        return (lax.rem(x + step, chips_x) * chips_z + z) * 2 + core

    def at_z(step):
        return (x * chips_z + lax.rem(z + step, chips_z)) * 2 + core

    moves = [(obj_ref, strip.at[m]), (dft_hbm, dft_ref), (probe_hbm, probe_ref), (meas_hbm, meas_ref)]
    local = [pltpu.make_async_copy(src, dst, local_sem.at[i]) for i, (src, dst) in enumerate(moves)]
    for copy in local:
        copy.start()
    barrier = pltpu.get_barrier_semaphore()

    def greet(scan, mode):
        pl.semaphore_signal(barrier, inc=1, device_id=(scan, mode), device_id_type=MESH)

    greet(s, m_up)
    greet(s, m_dn)
    greet(nxt, m)
    greet(prv, m)
    loop(chips_x, lambda step: greet(at_x(step), m), 1)
    loop(chips_z, lambda step: greet(at_z(step), m), 1)
    pl.semaphore_wait(barrier, 2 + chips_x + chips_z)

    def cells_of(tile, part, t):
        return strip.at[tile, part, t * THIRD : (t + 1) * THIRD]

    up, dn, fwd_up, fwd_dn = {}, {}, {}, {}

    def send_own(t):
        up[0, t] = wires.put(cells_of(m, 0, t), cells_of(m, 0, t), s, m_up)
        dn[1, t] = wires.put(cells_of(m, 1, t), cells_of(m, 1, t), s, m_dn)
        up[1, t] = wires.put(cells_of(m, 1, t), cells_of(m, 1, t), s, m_up)
        dn[0, t] = wires.put(cells_of(m, 0, t), cells_of(m, 0, t), s, m_dn)

    def forward(t):
        up[0, t].wait_recv()
        fwd_up[t] = wires.put(cells_of(m_dn, 0, t), cells_of(m_dn, 0, t), s, m_up)
        dn[1, t].wait_recv()
        fwd_dn[t] = wires.put(cells_of(m_up, 1, t), cells_of(m_up, 1, t), s, m_dn)

    local[0].wait()
    send_own(0)
    row_at = pos_ref[0, 0]
    col_at = pos_ref[0, 1]
    corners[1] = jnp.full((8, LANES), col_at, jnp.int32)
    pos_next = wires.put(corners.at[1], corners.at[0], nxt, m)
    pos_prev = wires.put(corners.at[1], corners.at[2], prv, m)
    send_own(1)
    send_own(2)
    for copy in local[1:]:
        copy.wait()
    offset = row_at - ROWS * s + ROWS
    turn = jnp.bitwise_and(col_at, PATCH - 1)

    def transforms(i):
        rows = tiles(i * CHUNK, CHUNK, CHUNK)
        low_rows = tiles(PATCH + i * CHUNK, CHUNK, CHUNK)
        for part, (re, im) in enumerate(zip(split(dft_ref[0, rows]), split(dft_ref[1, rows]))):
            at = i * 4 * CHUNK + 2 * part * CHUNK
            for which, sign in enumerate((im, -im)):
                row_ops[which, part, rows, 0:PATCH] = re
                row_ops[which, part, rows, PATCH:] = sign
                row_ops[which, part, low_rows, 0:PATCH] = -sign
                row_ops[which, part, low_rows, PATCH:] = re
                col_ops[which, tiles(at, CHUNK, CHUNK), 0:PATCH] = re
                col_ops[which, tiles(at, CHUNK, CHUNK), PATCH:] = -sign
                col_ops[which, tiles(at + CHUNK, CHUNK, CHUNK), 0:PATCH] = sign
                col_ops[which, tiles(at + CHUNK, CHUNK, CHUNK), PATCH:] = re

    loop(CHUNKS, transforms)
    forward(0)

    def window(part, start, down):
        value = double[part, tiles(start, CHUNK + SEAM, SEAM)]
        return pltpu.roll(value, down, 0)[SEAM:]

    def turn_probe(i):
        rows = tiles(i * CHUNK, CHUNK, CHUNK)
        for part in range(2):
            rolled = pltpu.roll(probe_ref[0, part, rows], turn, 1)
            double[part, rows] = rolled
            double[part, tiles(PATCH + i * CHUNK, CHUNK, CHUNK)] = rolled

    def align_probe(i):
        for part in range(2):
            wave[part, tiles(i * CHUNK, CHUNK, CHUNK)] = window(part, i * CHUNK, offset)

    loop(CHUNKS, turn_probe)
    loop(CHUNKS, align_probe)
    pos_next.wait_recv()
    pos_prev.wait_recv()

    def choose(t):
        for copy in (dn[0, t], fwd_up[t], up[1, t], fwd_dn[t]):
            copy.wait_recv()

        def pick(j):
            part = lax.div(j, THIRD // 8)
            row = t * THIRD + lax.rem(j, THIRD // 8) * 8
            rows = tiles(row, 8)
            picked = [[jnp.zeros((8, LANES), F32)] * 2 for who in range(3)]
            corner = [corners[who] for who in range(3)]
            for block in range(MODES * COLS // LANES):
                tile, inner = divmod(block, COLS // LANES)
                cells = strip[tile, part, rows, inner * LANES : (inner + 1) * LANES]
                for who in range(3):
                    mask = column_mask(corner[who], block, (8, LANES))
                    picked[who][block % 2] = jnp.where(mask, cells, picked[who][block % 2])
            for half in range(2):
                lanes = slice(half * LANES, (half + 1) * LANES)
                pick_prev[part, rows, lanes] = picked[0][half]
                patch[part, tiles(CHUNK + row, 8), lanes] = picked[1][half]
                pick_next[part, rows, lanes] = picked[2][half]

        loop(2 * THIRD // 8, pick)
        rows = slice(t * THIRD, (t + 1) * THIRD)
        return (
            wires.put(pick_next.at[:, rows], from_prev.at[:, rows], nxt, m),
            wires.put(pick_prev.at[:, rows], from_next.at[:, rows], prv, m),
        )

    def along_rows(value, which):
        high, low = split(value)
        count = value.shape[0]
        both = dot(jnp.concatenate([high, low], axis=0), row_ops[which, 0])
        return both[:count] + both[count:] + dot(high, row_ops[which, 1])

    def along_columns(i, which):
        at = i * 4 * CHUNK
        both = dot(col_ops[which, tiles(at, 4 * CHUNK, CHUNK)], stack[0])
        result = both[: 2 * CHUNK] + both[2 * CHUNK :]
        result = result + dot(col_ops[which, tiles(at, 2 * CHUNK, CHUNK)], stack[1])
        return result[:CHUNK], result[CHUNK:]

    def keep(value, i):
        high, low = split(value)
        for part in range(2):
            lanes = slice(part * PATCH, (part + 1) * PATCH)
            into = tiles(part * PATCH + i * CHUNK, CHUNK, CHUNK)
            stack[0, into] = high[:, lanes]
            stack[1, into] = low[:, lanes]

    def first_stage(i):
        i = lax.rem(i, CHUNKS)
        rows = tiles(i * CHUNK, CHUNK, CHUNK)
        p_re, p_im = wave[0, rows], wave[1, rows]
        o_re, o_im = patch[0, rows], patch[1, rows]
        exit_wave = jnp.concatenate([p_re * o_re - p_im * o_im, p_re * o_im + p_im * o_re], axis=1)
        keep(along_rows(exit_wave, 0), i)

    halos = [choose(0)]
    forward(1)
    halos.append(choose(1))
    forward(2)
    halos.append(choose(2))
    for halo in halos[:2]:
        for copy in halo:
            copy.wait_recv()
    for part in range(2):
        patch[part, 160:224] = jnp.where(s < scans - 1, from_next[part, 0:64], 0.0)
    loop(3, first_stage, 1)
    seam = lax.broadcasted_iota(jnp.int32, (SEAM, PATCH), 0)
    for copy in halos[2]:
        copy.wait_recv()
    for part in range(2):
        above = jnp.where(s > 0, from_prev[part, 0:32], 0.0)
        below = jnp.where(s < scans - 1, from_next[part, 64:96], 0.0)
        patch[part, 224:256] = jnp.where(seam >= offset, above, below)
        patch[part, 0:64] = jnp.where(s > 0, from_prev[part, 32:96], 0.0)
    loop(5, first_stage, 3)

    def chunk_of(i):
        return tiles(i * CHUNK, CHUNK, CHUNK)

    def route(i):
        even = lax.rem(i, 2) == 0
        return jnp.where(even, pair_a, pair_b), jnp.where(even, pair_b, pair_a)

    power_slot = wires.take(2 * CHUNKS)

    def power_hop(i, second):
        rows = chunk_of(i)
        src, dst = (power_sum, power_b) if second else (power, power_a)
        slot = power_slot + second * CHUNKS + i
        return wires.copy(src.at[rows], dst.at[rows], s, route(i)[second], slot)

    def to_far(i):
        rows = chunk_of(i)
        f_re, f_im = along_columns(i, 0)
        far[0, rows] = f_re
        far[1, rows] = f_im
        power[rows] = f_re * f_re + f_im * f_im
        power_hop(i, 0).start()

    def add_power(i):
        rows = chunk_of(i)
        power_hop(i, 0).wait_recv()
        power_sum[rows] = power[rows] + power_a[rows]
        power_hop(i, 1).start()

    def rescale(i):
        rows = chunk_of(i)
        power_hop(i, 1).wait_recv()
        intensity = power_sum[rows] + power_b[rows]
        factor = 1.0 - meas_ref[0, rows] / jnp.sqrt(jnp.maximum(intensity, 1.0))
        scaled = jnp.concatenate([far[0, rows] * factor, far[1, rows] * factor], axis=1)
        keep(along_rows(scaled, 1), i)

    loop(CHUNKS, to_far)
    wires.drain()
    loop(CHUNKS, add_power)
    loop(CHUNKS, rescale)

    term_slot = wires.take(2 * CHUNKS)
    core_slot = wires.take(2 * CHUNKS)

    def nth(j):
        return lax.rem(x + j, CHUNKS)

    def term_hop(j, second):
        rows = chunk_of(nth(j))
        src, dst = (term_sum, term_b) if second else (term, term_a)
        slot = term_slot + second * CHUNKS + j
        return wires.copy(src.at[:, rows], dst.at[:, rows], s, route(j)[second], slot)

    def core_hop(j):
        n = nth(j)
        return wires.copy(pgrad.at[1 - core, n], pcore.at[n], other_core, m, core_slot + j - 1)

    def send_probe_terms(j):
        n = nth(j)
        for part in range(2):
            value = window(part, n * CHUNK + PATCH - SEAM, SEAM - offset)
            pgrad[part, n, 0:CHUNK] = value[:, :LANES]
            pgrad[part, n, CHUNK:] = value[:, LANES:]
        core_hop(j).start()

    def to_object(j):
        i = nth(j)
        rows = chunk_of(i)
        b_re, b_im = along_columns(i, 1)
        p_re, p_im = wave[0, rows], wave[1, rows]
        term[0, rows] = p_re * b_re + p_im * b_im
        term[1, rows] = p_re * b_im - p_im * b_re
        term_hop(j, 0).start()
        o_re, o_im = patch[0, rows], patch[1, rows]
        for part, value in enumerate((o_re * b_re + o_im * b_im, o_re * b_im - o_im * b_re)):
            value = pltpu.roll(value, PATCH - turn, 1)
            double[part, rows] = value
            double[part, tiles(PATCH + i * CHUNK, CHUNK, CHUNK)] = value

        @pl.when(j > 0)
        def _():
            send_probe_terms(j)

    loop(CHUNKS, to_object)
    send_probe_terms(CHUNKS)

    x_slot = wires.take(2 * chips_x)
    back_x_slot = wires.take(2 * chips_x)
    z_slot = wires.take(chips_z)
    back_z_slot = wires.take(chips_z)

    block_z = max(chips_z // 2, 1)
    blocks = chips_z // block_z

    def block_rows(b):
        return pl.ds(b * block_z * per_z, block_z * per_z)

    def x_hop(j, b):
        rows = block_rows(b)
        return wires.copy(halves.at[nth(j), rows], parts_x.at[j, rows], at_x(j), m, x_slot + 2 * j + b)

    def add_core(j):
        n = nth(j)
        core_hop(j).wait_recv()
        halves[n] = pgrad[core, n] + pcore[n]

    def add_core_and_send(j):
        add_core(j)
        x_hop(j, 0).start()

    loop(chips_x, add_core_and_send, 1)
    for b in range(1, blocks):
        loop(chips_x, lambda j: x_hop(j, b).start(), 1)
    add_core(CHUNKS)

    def add_term(j):
        rows = chunk_of(nth(j))
        term_hop(j, 0).wait_recv()
        term_sum[:, rows] = term[:, rows] + term_a[:, rows]
        term_hop(j, 1).start()

    def z_rows(at):
        return tiles(at * per_z, per_z)

    def z_hop(j):
        there = z_rows(lax.rem(z + j, chips_z))
        return wires.copy(shard.at[there], parts_z.at[j], at_z(j), m, z_slot + j)

    per_block = CHUNKS // blocks
    for b in range(blocks):
        loop((b + 1) * per_block, add_term, b * per_block)
        rows = block_rows(b)
        total = halves[x, rows]
        for j in range(1, chips_x):
            x_hop(j, b).wait_recv()
            total = total + parts_x[j, rows]
        shard[rows] = total

        def send_z(i):
            j = lax.rem(b * block_z + lax.rem(z + i, block_z) - z + chips_z, chips_z)

            @pl.when(j > 0)
            def _():
                z_hop(j).start()

        loop(block_z, send_z)

    loop(CHUNKS, lambda i: (power_hop(i, 0).wait_send(), power_hop(i, 1).wait_send()))

    def add_z(j, total):
        z_hop(j).wait_recv()
        return total + parts_z[j]

    total = lax.fori_loop(1, chips_z, add_z, shard[z_rows(z)])
    first = z * per_z
    half = lax.div(first, CHUNK) if per_z <= CHUNK else 0
    scale = 1.0 / math.sqrt(scans)
    old_rows = tiles(x * CHUNK + lax.rem(first, CHUNK), per_z)
    old = probe_ref[0, core, old_rows, tiles(half * LANES, LANES, LANES)]
    gathered[x, z_rows(z)] = old - total * scale

    def back_z_hop(j):
        mine = gathered.at[x, z_rows(z)]
        return wires.copy(mine, mine, at_z(j), m, back_z_slot + j)

    loop(chips_z, lambda j: back_z_hop(j).start(), 1)

    def back_x_hop(j, b):
        mine = gathered.at[x, block_rows(b)]
        return wires.copy(mine, mine, at_x(j), m, back_x_slot + 2 * j + b)

    for b in range(blocks):

        def take_z(i):
            j = lax.rem(z - b * block_z - i + chips_z, chips_z)

            @pl.when(j > 0)
            def _():
                back_z_hop(j).wait_recv()

        loop(block_z, take_z)
        loop(chips_x, lambda j: back_x_hop(j, b).start(), 1)

    def back_core_hop(j):
        mine = nth(CHUNKS - j)
        return wires.copy(gathered.at[mine], gathered_other.at[mine], other_core, m, core_slot + CHUNKS + j)

    back_core_hop(0).start()

    def total_terms(j):
        rows = chunk_of(nth(j))
        term_hop(j, 1).wait_recv()
        total_term[:, rows] = term_sum[:, rows] + term_b[:, rows]

    loop(CHUNKS, total_terms)
    for part in range(2):
        edge = total_term[part, 224:256]
        rim_up[part, 0:32] = jnp.where(seam >= offset, edge, 0.0)
        rim_up[part, 32:96] = total_term[part, 0:64]
        rim_down[part, 0:64] = total_term[part, 160:224]
        rim_down[part, 64:96] = jnp.where(seam < offset, edge, 0.0)
    to_prev = wires.put(rim_up, grad_next, prv, m)
    to_next = wires.put(rim_down, grad_prev, nxt, m)

    loop(CHUNKS, lambda j: (term_hop(j, 0).wait_send(), term_hop(j, 1).wait_send()))
    loop(CHUNKS + 1, lambda j: core_hop(j).wait_send(), 1)
    for b in range(blocks):
        loop(chips_x, lambda j: x_hop(j, b).wait_send(), 1)
    loop(chips_z, lambda j: (z_hop(j).wait_send(), back_z_hop(j).wait_send()), 1)

    def probe_copy(which, source, n, half, slot):
        return pltpu.make_async_copy(
            source.at[n, half * CHUNK : (half + 1) * CHUNK],
            probe_out.at[0, which, chunk_of(n), half * LANES : (half + 1) * LANES],
            out_sem.at[slot],
        )

    def mine_copy(j, half):
        return probe_copy(core, gathered, nth(CHUNKS - j), half, 1 + 2 * j + half)

    def other_copy(j, half):
        return probe_copy(1 - core, gathered_other, nth(CHUNKS - j), half, 1 + 2 * (CHUNKS + j) + half)

    def put_both(copy, j):
        copy(j, 0).start()
        copy(j, 1).start()

    def wait_both(copy, j):
        copy(j, 0).wait()
        copy(j, 1).wait()

    put_both(mine_copy, 0)

    def pass_on(j):
        for b in range(blocks):
            back_x_hop(j, b).wait_recv()
        back_core_hop(j).start()
        put_both(mine_copy, j)

    loop(chips_x, pass_on, 1)

    to_prev.wait_recv()
    to_next.wait_recv()
    shape = (ROWS, LANES)
    for inner in range(COLS // LANES):
        block = m * (COLS // LANES) + inner
        lanes = tiles(lax.rem(block, 2) * LANES, LANES, LANES)
        masks = [column_mask(jnp.broadcast_to(corners[who, 0:1, :], shape), block, shape) for who in range(3)]
        here = slice(inner * LANES, (inner + 1) * LANES)
        for part in range(2):
            above = jnp.where(s > 0, grad_prev[part, :, lanes], 0.0)
            below = jnp.where(s < scans - 1, grad_next[part, :, lanes], 0.0)
            total = jnp.where(masks[1], total_term[part, CHUNK : CHUNK + ROWS, lanes], 0.0)
            total = total + jnp.where(masks[0], above, 0.0) + jnp.where(masks[2], below, 0.0)
            new_obj[part, :, here] = strip[m, part, :, here] - object_rate * total
    obj_copy = pltpu.make_async_copy(new_obj, obj_out, out_sem.at[0])
    obj_copy.start()
    wires.drain()

    def take_core(j):
        back_core_hop(j).wait_recv()
        put_both(other_copy, j)

    loop(CHUNKS, take_core)
    loop(CHUNKS, lambda j: back_core_hop(j).wait_send())
    for b in range(blocks):
        loop(chips_x, lambda j: back_x_hop(j, b).wait_send(), 1)
    obj_copy.wait()
    loop(CHUNKS, lambda j: (wait_both(mine_copy, j), wait_both(other_copy, j)))


PIECES = 4


def placing(obj_in, probe_in, obj_out, probe_out, obj_held, probe_held, into, out):
    pieces = []
    for src, held, dst, dim in ((obj_in, obj_held, obj_out, 1), (probe_in, probe_held, probe_out, 2)):
        size = src.shape[dim] // PIECES
        for i in range(PIECES):
            at = (slice(None),) * dim + (slice(i * size, (i + 1) * size),)
            slot = len(pieces)
            first = pltpu.make_async_copy(src.at[at], held.at[at], into.at[slot])
            pieces.append((first, pltpu.make_async_copy(held.at[at], dst.at[at], out.at[slot])))
    for first, second in pieces:
        first.start()
    for first, second in pieces:
        first.wait()
        second.start()
    for first, second in pieces:
        second.wait()


def per_device(scans, chips_x, object_field, probe, measured, positions):
    chips_z = scans // (2 * chips_x)
    per_z = 2 * CHUNK // chips_z
    wire_count = 28 + 6 * CHUNKS + 4 * chips_x + 2 * chips_z
    field = pltpu.VMEM((2, PATCH, PATCH), F32)
    plane = pltpu.VMEM((PATCH, PATCH), F32)
    rim = pltpu.VMEM((2, ROWS, PATCH), F32)
    share = pltpu.VMEM((CHUNKS, 2 * CHUNK, LANES), F32)
    hbm = pl.BlockSpec(memory_space=pltpu.HBM)
    out_shape = (
        jax.ShapeDtypeStruct(object_field.shape, F32),
        jax.ShapeDtypeStruct(probe.shape, F32),
    )
    results = pl.pallas_call(
        functools.partial(kernel, scans, chips_x, chips_z),
        out_shape=out_shape,
        in_specs=[pl.BlockSpec(memory_space=pltpu.SMEM)] + [hbm] * 4,
        out_specs=(hbm, hbm),
        scratch_shapes=[
            pltpu.VMEM(probe.shape, F32),
            pltpu.VMEM(measured.shape, F32),
            field,
            pltpu.VMEM((2, 2, 2 * PATCH, 2 * PATCH), BF16),
            pltpu.VMEM((2, 4 * PATCH, 2 * PATCH), BF16),
            pltpu.VMEM((MODES, 2, ROWS, COLS), F32),
            pltpu.VMEM((3, 8, LANES), jnp.int32),
            rim, rim, rim, rim,
            field, field,
            pltpu.VMEM((2, 2 * PATCH, PATCH), F32),
            pltpu.VMEM((2, 2 * PATCH, PATCH), BF16),
            field,
            plane, plane, plane, plane,
            field, field, field, field, field,
            rim, rim, rim, rim,
            pltpu.VMEM((2, CHUNKS, 2 * CHUNK, LANES), F32),
            share, share, share,
            pltpu.VMEM((2 * CHUNK, LANES), F32),
            pltpu.VMEM((chips_z, per_z, LANES), F32),
            share, share,
            pltpu.VMEM(object_field.shape, F32),
            pltpu.SemaphoreType.DMA((wire_count,)),
            pltpu.SemaphoreType.DMA((wire_count,)),
            pltpu.SemaphoreType.DMA((4,)),
            pltpu.SemaphoreType.DMA((1 + 4 * CHUNKS,)),
        ],
        compiler_params=pltpu.CompilerParams(
            collective_id=0, has_side_effects=True, vmem_limit_bytes=60 << 20
        ),
        cost_estimate=pl.CostEstimate(flops=1 << 31, bytes_accessed=4 << 20, transcendentals=0),
    )(positions, object_field, probe, measured, jnp.asarray(dft_parts()))
    return pl.pallas_call(
        placing,
        out_shape=out_shape,
        in_specs=[hbm, hbm],
        out_specs=(hbm, hbm),
        scratch_shapes=[
            pltpu.VMEM(object_field.shape, F32),
            pltpu.VMEM(probe.shape, F32),
            pltpu.SemaphoreType.DMA((2 * PIECES,)),
            pltpu.SemaphoreType.DMA((2 * PIECES,)),
        ],
        compiler_params=pltpu.CompilerParams(vmem_limit_bytes=60 << 20),
    )(*results)


def solution(mesh):
    return jax.shard_map(
        functools.partial(per_device, mesh.shape["scan"], X_CHIPS),
        mesh=mesh,
        in_specs=(
            P(None, "scan", "mode"),
            P("mode", None, None, None),
            P("scan", None, None),
            P("scan", None),
        ),
        out_specs=(P(None, "scan", "mode"), P("mode", None, None, None)),
        check_vma=False,
    )
```

```python
import functools
import math

import jax
import jax.numpy as jnp
import ml_dtypes
import numpy as np
from jax import lax
from jax.experimental import pallas as pl
from jax.experimental.pallas import tpu as pltpu
from jax.sharding import PartitionSpec as P

MESH = pl.DeviceIdType.MESH
F32 = jnp.float32
BF16 = jnp.bfloat16
X_CHIPS = 4
MODES = 4
PATCH = 256
ROWS = 96
THIRD = 32
COLS = 384
LANES = 128
CHUNK = 64
SEAM = 32
CHUNKS = PATCH // CHUNK
object_rate = 0.25


def dft_parts():
    index = np.arange(PATCH)
    angle = 2.0 * math.pi / PATCH * (np.outer(index, index) % PATCH)
    scale = 1.0 / math.sqrt(PATCH)
    return np.stack([np.cos(angle) * scale, -np.sin(angle) * scale]).astype(np.float32)


def split(value):
    high = value.astype(BF16)
    return high, (value - high.astype(F32)).astype(BF16)


def dot(left, right):
    return jnp.dot(left, right, preferred_element_type=F32)


def column_mask(corner, block, shape):
    lane = lax.broadcasted_iota(jnp.int32, shape, 1) + block * LANES
    return (lane >= corner) & (lane < corner + PATCH)


def loop(count, body, start=0):
    def step(i, carry):
        body(i)
        return carry

    lax.fori_loop(start, count, step, 0)


def tiles(start, size, unit=8):
    return pl.ds(pl.multiple_of(start, unit), size)


class Wires:
    def __init__(self, send, recv):
        self.send, self.recv, self.used, self.open = send, recv, 0, []

    def take(self, count):
        first = self.used
        self.used += count
        return first

    def copy(self, src, dst, scan, mode, slot):
        return pltpu.make_async_remote_copy(
            src_ref=src,
            dst_ref=dst,
            send_sem=self.send.at[slot],
            recv_sem=self.recv.at[slot],
            device_id=(scan, mode),
            device_id_type=MESH,
        )

    def put(self, src, dst, scan, mode):
        copy = self.copy(src, dst, scan, mode, self.take(1))
        copy.start()
        self.open.append(copy)
        return copy

    def drain(self):
        for copy in self.open:
            copy.wait_send()
        self.open = []


def kernel(
    scans, chips_x, chips_z,
    pos_ref, obj_ref, probe_hbm, meas_hbm, dft_hbm,
    obj_out, probe_out,
    probe_ref, meas_ref, dft_ref, row_ops, col_ops,
    strip, corners, pick_next, pick_prev, from_prev, from_next,
    patch, wave, double, stack, far, power, power_a, power_sum, power_b,
    term, term_a, term_sum, term_b, total_term, rim_up, rim_down, grad_prev, grad_next,
    pgrad, pcore, halves, parts_x, shard, parts_z, gathered, gathered_other,
    new_obj, send_sem, recv_sem, local_sem, out_sem, token_sem_x, token_sem_z,
):
    s = lax.axis_index("scan")
    m = lax.axis_index("mode")
    core = lax.rem(s, 2)
    z = lax.rem(lax.div(s, 2), chips_z)
    x = lax.div(s, 2 * chips_z)
    nxt, prv = lax.rem(s + 1, scans), lax.rem(s + scans - 1, scans)
    m_up, m_dn = lax.rem(m + 1, MODES), lax.rem(m + MODES - 1, MODES)
    pair_a = jnp.where(lax.rem(m, 2) == 0, m + 1, m - 1)
    pair_b = MODES - 1 - m
    other_core = jnp.where(core == 0, s + 1, s - 1)
    wires = Wires(send_sem, recv_sem)
    per_z = 2 * CHUNK // chips_z

    def at_x(step):
        return (lax.rem(x + step, chips_x) * chips_z + z) * 2 + core

    def at_z(step):
        return (x * chips_z + lax.rem(z + step, chips_z)) * 2 + core

    moves = [(obj_ref, strip.at[m]), (dft_hbm, dft_ref), (probe_hbm, probe_ref), (meas_hbm, meas_ref)]
    local = [pltpu.make_async_copy(src, dst, local_sem.at[i]) for i, (src, dst) in enumerate(moves)]
    for copy in local:
        copy.start()
    barrier = pltpu.get_barrier_semaphore()

    def greet(scan, mode):
        pl.semaphore_signal(barrier, inc=1, device_id=(scan, mode), device_id_type=MESH)

    greet(s, m_up)
    greet(s, m_dn)
    greet(nxt, m)
    greet(prv, m)
    near_x = sorted({1, chips_x - 1})
    near_z = sorted({1, chips_z - 1})
    for step in near_x:
        greet(at_x(step), m)
    for step in near_z:
        greet(at_z(step), m)
    pl.semaphore_wait(barrier, 4 + len(near_x) + len(near_z))

    rounds_x = chips_x // 2 - 1
    rounds_z = chips_z // 2 - 1

    def send_token(sem, at, near, turn):
        for way, step in enumerate(near):
            pl.semaphore_signal(sem.at[turn, way], inc=1, device_id=(at(step), m), device_id_type=MESH)

    def take_token(sem, near, turn):
        for way in range(len(near)):
            pl.semaphore_wait(sem.at[turn, way], 1)

    def token_z(turn):
        if 0 < turn <= rounds_z:
            take_token(token_sem_z, near_z, turn - 1)
        if turn < rounds_z:
            send_token(token_sem_z, at_z, near_z, turn)

    def token_x(turn):
        if 0 < turn <= rounds_x:
            take_token(token_sem_x, near_x, turn - 1)
        if turn < rounds_x:
            send_token(token_sem_x, at_x, near_x, turn)

    def cells_of(tile, part, t):
        return strip.at[tile, part, t * THIRD : (t + 1) * THIRD]

    up, dn, fwd_up, fwd_dn = {}, {}, {}, {}

    def send_own(t):
        up[0, t] = wires.put(cells_of(m, 0, t), cells_of(m, 0, t), s, m_up)
        dn[1, t] = wires.put(cells_of(m, 1, t), cells_of(m, 1, t), s, m_dn)
        up[1, t] = wires.put(cells_of(m, 1, t), cells_of(m, 1, t), s, m_up)
        dn[0, t] = wires.put(cells_of(m, 0, t), cells_of(m, 0, t), s, m_dn)

    def forward(t):
        up[0, t].wait_recv()
        fwd_up[t] = wires.put(cells_of(m_dn, 0, t), cells_of(m_dn, 0, t), s, m_up)
        dn[1, t].wait_recv()
        fwd_dn[t] = wires.put(cells_of(m_up, 1, t), cells_of(m_up, 1, t), s, m_dn)

    local[0].wait()
    send_own(0)
    row_at = pos_ref[0, 0]
    col_at = pos_ref[0, 1]
    corners[1] = jnp.full((8, LANES), col_at, jnp.int32)
    pos_next = wires.put(corners.at[1], corners.at[0], nxt, m)
    pos_prev = wires.put(corners.at[1], corners.at[2], prv, m)
    send_own(1)
    send_own(2)
    token_x(0)
    token_z(0)
    for copy in local[1:]:
        copy.wait()
    offset = row_at - ROWS * s + ROWS
    turn = jnp.bitwise_and(col_at, PATCH - 1)

    def transforms(i):
        rows = tiles(i * CHUNK, CHUNK, CHUNK)
        low_rows = tiles(PATCH + i * CHUNK, CHUNK, CHUNK)
        for part, (re, im) in enumerate(zip(split(dft_ref[0, rows]), split(dft_ref[1, rows]))):
            at = i * 4 * CHUNK + 2 * part * CHUNK
            for which, sign in enumerate((im, -im)):
                row_ops[which, part, rows, 0:PATCH] = re
                row_ops[which, part, rows, PATCH:] = sign
                row_ops[which, part, low_rows, 0:PATCH] = -sign
                row_ops[which, part, low_rows, PATCH:] = re
                col_ops[which, tiles(at, CHUNK, CHUNK), 0:PATCH] = re
                col_ops[which, tiles(at, CHUNK, CHUNK), PATCH:] = -sign
                col_ops[which, tiles(at + CHUNK, CHUNK, CHUNK), 0:PATCH] = sign
                col_ops[which, tiles(at + CHUNK, CHUNK, CHUNK), PATCH:] = re

    loop(CHUNKS, transforms)
    token_z(1)
    forward(0)

    def window(part, start, down):
        value = double[part, tiles(start, CHUNK + SEAM, SEAM)]
        return pltpu.roll(value, down, 0)[SEAM:]

    def turn_probe(i):
        rows = tiles(i * CHUNK, CHUNK, CHUNK)
        for part in range(2):
            rolled = pltpu.roll(probe_ref[0, part, rows], turn, 1)
            double[part, rows] = rolled
            double[part, tiles(PATCH + i * CHUNK, CHUNK, CHUNK)] = rolled

    def align_probe(i):
        for part in range(2):
            wave[part, tiles(i * CHUNK, CHUNK, CHUNK)] = window(part, i * CHUNK, offset)

    loop(CHUNKS, turn_probe)
    loop(CHUNKS, align_probe)
    token_z(2)
    forward(1)
    pos_next.wait_recv()
    pos_prev.wait_recv()
    token_z(3)
    forward(2)
    token_z(4)

    def choose(t):
        for copy in (dn[0, t], fwd_up[t], up[1, t], fwd_dn[t]):
            copy.wait_recv()

        def pick(j):
            part = lax.div(j, THIRD // 8)
            row = t * THIRD + lax.rem(j, THIRD // 8) * 8
            rows = tiles(row, 8)
            picked = [[jnp.zeros((8, LANES), F32)] * 2 for who in range(3)]
            corner = [corners[who] for who in range(3)]
            for block in range(MODES * COLS // LANES):
                tile, inner = divmod(block, COLS // LANES)
                cells = strip[tile, part, rows, inner * LANES : (inner + 1) * LANES]
                for who in range(3):
                    mask = column_mask(corner[who], block, (8, LANES))
                    picked[who][block % 2] = jnp.where(mask, cells, picked[who][block % 2])
            for half in range(2):
                lanes = slice(half * LANES, (half + 1) * LANES)
                pick_prev[part, rows, lanes] = picked[0][half]
                patch[part, tiles(CHUNK + row, 8), lanes] = picked[1][half]
                pick_next[part, rows, lanes] = picked[2][half]

        loop(2 * THIRD // 8, pick)
        rows = slice(t * THIRD, (t + 1) * THIRD)
        return (
            wires.put(pick_next.at[:, rows], from_prev.at[:, rows], nxt, m),
            wires.put(pick_prev.at[:, rows], from_next.at[:, rows], prv, m),
        )

    def along_rows(value, which):
        high, low = split(value)
        count = value.shape[0]
        both = dot(jnp.concatenate([high, low], axis=0), row_ops[which, 0])
        return both[:count] + both[count:] + dot(high, row_ops[which, 1])

    def along_columns(i, which):
        at = i * 4 * CHUNK
        both = dot(col_ops[which, tiles(at, 4 * CHUNK, CHUNK)], stack[0])
        result = both[: 2 * CHUNK] + both[2 * CHUNK :]
        result = result + dot(col_ops[which, tiles(at, 2 * CHUNK, CHUNK)], stack[1])
        return result[:CHUNK], result[CHUNK:]

    def keep(value, i):
        high, low = split(value)
        for part in range(2):
            lanes = slice(part * PATCH, (part + 1) * PATCH)
            into = tiles(part * PATCH + i * CHUNK, CHUNK, CHUNK)
            stack[0, into] = high[:, lanes]
            stack[1, into] = low[:, lanes]

    def first_stage(i):
        i = lax.rem(i, CHUNKS)
        rows = tiles(i * CHUNK, CHUNK, CHUNK)
        p_re, p_im = wave[0, rows], wave[1, rows]
        o_re, o_im = patch[0, rows], patch[1, rows]
        exit_wave = jnp.concatenate([p_re * o_re - p_im * o_im, p_re * o_im + p_im * o_re], axis=1)
        keep(along_rows(exit_wave, 0), i)

    halos = [choose(0), choose(1), choose(2)]
    token_z(5)
    for halo in halos[:2]:
        for copy in halo:
            copy.wait_recv()
    for part in range(2):
        patch[part, 160:224] = jnp.where(s < scans - 1, from_next[part, 0:64], 0.0)
    loop(3, first_stage, 1)
    seam = lax.broadcasted_iota(jnp.int32, (SEAM, PATCH), 0)
    for copy in halos[2]:
        copy.wait_recv()
    for part in range(2):
        above = jnp.where(s > 0, from_prev[part, 0:32], 0.0)
        below = jnp.where(s < scans - 1, from_next[part, 64:96], 0.0)
        patch[part, 224:256] = jnp.where(seam >= offset, above, below)
        patch[part, 0:64] = jnp.where(s > 0, from_prev[part, 32:96], 0.0)
    loop(5, first_stage, 3)

    def chunk_of(i):
        return tiles(i * CHUNK, CHUNK, CHUNK)

    def route(i):
        even = lax.rem(i, 2) == 0
        return jnp.where(even, pair_a, pair_b), jnp.where(even, pair_b, pair_a)

    power_slot = wires.take(2 * CHUNKS)

    def power_hop(i, second):
        rows = chunk_of(i)
        src, dst = (power_sum, power_b) if second else (power, power_a)
        slot = power_slot + second * CHUNKS + i
        return wires.copy(src.at[rows], dst.at[rows], s, route(i)[second], slot)

    def to_far(i):
        rows = chunk_of(i)
        f_re, f_im = along_columns(i, 0)
        far[0, rows] = f_re
        far[1, rows] = f_im
        power[rows] = f_re * f_re + f_im * f_im
        power_hop(i, 0).start()

    def add_power(i):
        rows = chunk_of(i)
        power_hop(i, 0).wait_recv()
        power_sum[rows] = power[rows] + power_a[rows]
        power_hop(i, 1).start()

    def rescale(i):
        rows = chunk_of(i)
        power_hop(i, 1).wait_recv()
        intensity = power_sum[rows] + power_b[rows]
        factor = 1.0 - meas_ref[0, rows] / jnp.sqrt(jnp.maximum(intensity, 1.0))
        scaled = jnp.concatenate([far[0, rows] * factor, far[1, rows] * factor], axis=1)
        keep(along_rows(scaled, 1), i)

    loop(CHUNKS, to_far)
    token_z(6)
    wires.drain()
    loop(CHUNKS, add_power)
    token_z(7)
    token_x(1)
    loop(CHUNKS, rescale)

    term_slot = wires.take(2 * CHUNKS)
    core_slot = wires.take(2 * CHUNKS)

    def nth(j):
        return lax.rem(x + j, CHUNKS)

    def term_hop(j, second):
        rows = chunk_of(nth(j))
        src, dst = (term_sum, term_b) if second else (term, term_a)
        slot = term_slot + second * CHUNKS + j
        return wires.copy(src.at[:, rows], dst.at[:, rows], s, route(j)[second], slot)

    def core_hop(j):
        n = nth(j)
        return wires.copy(pgrad.at[1 - core, n], pcore.at[n], other_core, m, core_slot + j - 1)

    def send_probe_terms(j):
        n = nth(j)
        for part in range(2):
            value = window(part, n * CHUNK + PATCH - SEAM, SEAM - offset)
            pgrad[part, n, 0:CHUNK] = value[:, :LANES]
            pgrad[part, n, CHUNK:] = value[:, LANES:]
        core_hop(j).start()

    def to_object(j):
        i = nth(j)
        rows = chunk_of(i)
        b_re, b_im = along_columns(i, 1)
        p_re, p_im = wave[0, rows], wave[1, rows]
        term[0, rows] = p_re * b_re + p_im * b_im
        term[1, rows] = p_re * b_im - p_im * b_re
        term_hop(j, 0).start()
        o_re, o_im = patch[0, rows], patch[1, rows]
        for part, value in enumerate((o_re * b_re + o_im * b_im, o_re * b_im - o_im * b_re)):
            value = pltpu.roll(value, PATCH - turn, 1)
            double[part, rows] = value
            double[part, tiles(PATCH + i * CHUNK, CHUNK, CHUNK)] = value

        @pl.when(j > 0)
        def _():
            send_probe_terms(j)

    loop(CHUNKS, to_object)
    send_probe_terms(CHUNKS)

    assert rounds_x <= 1 and rounds_z <= 7

    x_slot = wires.take(2 * chips_x)
    back_x_slot = wires.take(2 * chips_x)
    z_slot = wires.take(chips_z)
    back_z_slot = wires.take(chips_z)

    block_z = max(chips_z // 2, 1)
    blocks = chips_z // block_z

    def block_rows(b):
        return pl.ds(b * block_z * per_z, block_z * per_z)

    def x_hop(j, b):
        rows = block_rows(b)
        return wires.copy(halves.at[nth(j), rows], parts_x.at[j, rows], at_x(j), m, x_slot + 2 * j + b)

    def add_core(j):
        n = nth(j)
        core_hop(j).wait_recv()
        halves[n] = pgrad[core, n] + pcore[n]

    def add_core_and_send(j):
        add_core(j)
        x_hop(j, 0).start()

    loop(chips_x, add_core_and_send, 1)
    for b in range(1, blocks):
        loop(chips_x, lambda j: x_hop(j, b).start(), 1)
    add_core(CHUNKS)

    def add_term(j):
        rows = chunk_of(nth(j))
        term_hop(j, 0).wait_recv()
        term_sum[:, rows] = term[:, rows] + term_a[:, rows]
        term_hop(j, 1).start()

    def z_rows(at):
        return tiles(at * per_z, per_z)

    def z_hop(j):
        there = z_rows(lax.rem(z + j, chips_z))
        return wires.copy(shard.at[there], parts_z.at[j], at_z(j), m, z_slot + j)

    per_block = CHUNKS // blocks
    for b in range(blocks):
        loop((b + 1) * per_block, add_term, b * per_block)
        rows = block_rows(b)
        total = halves[x, rows]
        for j in range(1, chips_x):
            x_hop(j, b).wait_recv()
            total = total + parts_x[j, rows]
        shard[rows] = total

        def send_z(i):
            j = lax.rem(b * block_z + lax.rem(z + i, block_z) - z + chips_z, chips_z)

            @pl.when(j > 0)
            def _():
                z_hop(j).start()

        loop(block_z, send_z)

    loop(CHUNKS, lambda i: (power_hop(i, 0).wait_send(), power_hop(i, 1).wait_send()))

    def add_z(j, total):
        z_hop(j).wait_recv()
        return total + parts_z[j]

    total = lax.fori_loop(1, chips_z, add_z, shard[z_rows(z)])
    first = z * per_z
    half = lax.div(first, CHUNK) if per_z <= CHUNK else 0
    scale = 1.0 / math.sqrt(scans)
    old_rows = tiles(x * CHUNK + lax.rem(first, CHUNK), per_z)
    old = probe_ref[0, core, old_rows, tiles(half * LANES, LANES, LANES)]
    gathered[x, z_rows(z)] = old - total * scale

    def back_z_hop(j):
        mine = gathered.at[x, z_rows(z)]
        return wires.copy(mine, mine, at_z(j), m, back_z_slot + j)

    loop(chips_z, lambda j: back_z_hop(j).start(), 1)

    def back_x_hop(j, b):
        mine = gathered.at[x, block_rows(b)]
        return wires.copy(mine, mine, at_x(j), m, back_x_slot + 2 * j + b)

    for b in range(blocks):

        def take_z(i):
            j = lax.rem(z - b * block_z - i + chips_z, chips_z)

            @pl.when(j > 0)
            def _():
                back_z_hop(j).wait_recv()

        loop(block_z, take_z)
        loop(chips_x, lambda j: back_x_hop(j, b).start(), 1)

    def back_core_hop(j):
        mine = nth(CHUNKS - j)
        return wires.copy(gathered.at[mine], gathered_other.at[mine], other_core, m, core_slot + CHUNKS + j)

    back_core_hop(0).start()

    def total_terms(j):
        rows = chunk_of(nth(j))
        term_hop(j, 1).wait_recv()
        total_term[:, rows] = term_sum[:, rows] + term_b[:, rows]

    loop(CHUNKS, total_terms)
    for part in range(2):
        edge = total_term[part, 224:256]
        rim_up[part, 0:32] = jnp.where(seam >= offset, edge, 0.0)
        rim_up[part, 32:96] = total_term[part, 0:64]
        rim_down[part, 0:64] = total_term[part, 160:224]
        rim_down[part, 64:96] = jnp.where(seam < offset, edge, 0.0)
    to_prev = wires.put(rim_up, grad_next, prv, m)
    to_next = wires.put(rim_down, grad_prev, nxt, m)

    loop(CHUNKS, lambda j: (term_hop(j, 0).wait_send(), term_hop(j, 1).wait_send()))
    loop(CHUNKS + 1, lambda j: core_hop(j).wait_send(), 1)
    for b in range(blocks):
        loop(chips_x, lambda j: x_hop(j, b).wait_send(), 1)
    loop(chips_z, lambda j: (z_hop(j).wait_send(), back_z_hop(j).wait_send()), 1)

    def probe_copy(which, source, n, half, slot):
        return pltpu.make_async_copy(
            source.at[n, half * CHUNK : (half + 1) * CHUNK],
            probe_out.at[0, which, chunk_of(n), half * LANES : (half + 1) * LANES],
            out_sem.at[slot],
        )

    def mine_copy(j, half):
        return probe_copy(core, gathered, nth(CHUNKS - j), half, 1 + 2 * j + half)

    def other_copy(j, half):
        return probe_copy(1 - core, gathered_other, nth(CHUNKS - j), half, 1 + 2 * (CHUNKS + j) + half)

    def put_both(copy, j):
        copy(j, 0).start()
        copy(j, 1).start()

    def wait_both(copy, j):
        copy(j, 0).wait()
        copy(j, 1).wait()

    put_both(mine_copy, 0)

    def pass_on(j):
        for b in range(blocks):
            back_x_hop(j, b).wait_recv()
        back_core_hop(j).start()
        put_both(mine_copy, j)

    loop(chips_x, pass_on, 1)

    to_prev.wait_recv()
    to_next.wait_recv()
    shape = (ROWS, LANES)
    for inner in range(COLS // LANES):
        block = m * (COLS // LANES) + inner
        lanes = tiles(lax.rem(block, 2) * LANES, LANES, LANES)
        masks = [column_mask(jnp.broadcast_to(corners[who, 0:1, :], shape), block, shape) for who in range(3)]
        here = slice(inner * LANES, (inner + 1) * LANES)
        for part in range(2):
            above = jnp.where(s > 0, grad_prev[part, :, lanes], 0.0)
            below = jnp.where(s < scans - 1, grad_next[part, :, lanes], 0.0)
            total = jnp.where(masks[1], total_term[part, CHUNK : CHUNK + ROWS, lanes], 0.0)
            total = total + jnp.where(masks[0], above, 0.0) + jnp.where(masks[2], below, 0.0)
            new_obj[part, :, here] = strip[m, part, :, here] - object_rate * total
    obj_copy = pltpu.make_async_copy(new_obj, obj_out, out_sem.at[0])
    obj_copy.start()
    wires.drain()

    def take_core(j):
        back_core_hop(j).wait_recv()
        put_both(other_copy, j)

    loop(CHUNKS, take_core)
    loop(CHUNKS, lambda j: back_core_hop(j).wait_send())
    for b in range(blocks):
        loop(chips_x, lambda j: back_x_hop(j, b).wait_send(), 1)
    obj_copy.wait()
    loop(CHUNKS, lambda j: (wait_both(mine_copy, j), wait_both(other_copy, j)))


PIECES = 4


def placing(obj_in, probe_in, obj_out, probe_out, obj_held, probe_held, into, out):
    pieces = []
    for src, held, dst, dim in ((obj_in, obj_held, obj_out, 1), (probe_in, probe_held, probe_out, 2)):
        size = src.shape[dim] // PIECES
        for i in range(PIECES):
            at = (slice(None),) * dim + (slice(i * size, (i + 1) * size),)
            slot = len(pieces)
            first = pltpu.make_async_copy(src.at[at], held.at[at], into.at[slot])
            pieces.append((first, pltpu.make_async_copy(held.at[at], dst.at[at], out.at[slot])))
    for first, second in pieces:
        first.start()
    for first, second in pieces:
        first.wait()
        second.start()
    for first, second in pieces:
        second.wait()


def per_device(scans, chips_x, object_field, probe, measured, positions):
    chips_z = scans // (2 * chips_x)
    per_z = 2 * CHUNK // chips_z
    wire_count = 28 + 6 * CHUNKS + 4 * chips_x + 2 * chips_z
    field = pltpu.VMEM((2, PATCH, PATCH), F32)
    plane = pltpu.VMEM((PATCH, PATCH), F32)
    rim = pltpu.VMEM((2, ROWS, PATCH), F32)
    share = pltpu.VMEM((CHUNKS, 2 * CHUNK, LANES), F32)
    hbm = pl.BlockSpec(memory_space=pltpu.HBM)
    out_shape = (
        jax.ShapeDtypeStruct(object_field.shape, F32),
        jax.ShapeDtypeStruct(probe.shape, F32),
    )
    results = pl.pallas_call(
        functools.partial(kernel, scans, chips_x, chips_z),
        out_shape=out_shape,
        in_specs=[pl.BlockSpec(memory_space=pltpu.SMEM)] + [hbm] * 4,
        out_specs=(hbm, hbm),
        scratch_shapes=[
            pltpu.VMEM(probe.shape, F32),
            pltpu.VMEM(measured.shape, F32),
            field,
            pltpu.VMEM((2, 2, 2 * PATCH, 2 * PATCH), BF16),
            pltpu.VMEM((2, 4 * PATCH, 2 * PATCH), BF16),
            pltpu.VMEM((MODES, 2, ROWS, COLS), F32),
            pltpu.VMEM((3, 8, LANES), jnp.int32),
            rim, rim, rim, rim,
            field, field,
            pltpu.VMEM((2, 2 * PATCH, PATCH), F32),
            pltpu.VMEM((2, 2 * PATCH, PATCH), BF16),
            field,
            plane, plane, plane, plane,
            field, field, field, field, field,
            rim, rim, rim, rim,
            pltpu.VMEM((2, CHUNKS, 2 * CHUNK, LANES), F32),
            share, share, share,
            pltpu.VMEM((2 * CHUNK, LANES), F32),
            pltpu.VMEM((chips_z, per_z, LANES), F32),
            share, share,
            pltpu.VMEM(object_field.shape, F32),
            pltpu.SemaphoreType.DMA((wire_count,)),
            pltpu.SemaphoreType.DMA((wire_count,)),
            pltpu.SemaphoreType.DMA((4,)),
            pltpu.SemaphoreType.DMA((1 + 4 * CHUNKS,)),
            pltpu.SemaphoreType.REGULAR((max(chips_x // 2 - 1, 1), 2)),
            pltpu.SemaphoreType.REGULAR((max(chips_z // 2 - 1, 1), 2)),
        ],
        compiler_params=pltpu.CompilerParams(
            collective_id=0, has_side_effects=True, vmem_limit_bytes=60 << 20
        ),
        cost_estimate=pl.CostEstimate(flops=1 << 31, bytes_accessed=4 << 20, transcendentals=0),
    )(positions, object_field, probe, measured, jnp.asarray(dft_parts()))
    return pl.pallas_call(
        placing,
        out_shape=out_shape,
        in_specs=[hbm, hbm],
        out_specs=(hbm, hbm),
        scratch_shapes=[
            pltpu.VMEM(object_field.shape, F32),
            pltpu.VMEM(probe.shape, F32),
            pltpu.SemaphoreType.DMA((2 * PIECES,)),
            pltpu.SemaphoreType.DMA((2 * PIECES,)),
        ],
        compiler_params=pltpu.CompilerParams(vmem_limit_bytes=60 << 20),
    )(*results)


def solution(mesh):
    return jax.shard_map(
        functools.partial(per_device, mesh.shape["scan"], X_CHIPS),
        mesh=mesh,
        in_specs=(
            P(None, "scan", "mode"),
            P("mode", None, None, None),
            P("scan", None, None),
            P("scan", None),
        ),
        out_specs=(P(None, "scan", "mode"), P("mode", None, None, None)),
        check_vma=False,
    )
```

```python
import functools
import math

import jax
import jax.numpy as jnp
import ml_dtypes
import numpy as np
from jax import lax
from jax.experimental import pallas as pl
from jax.experimental.pallas import tpu as pltpu
from jax.sharding import PartitionSpec as P

MESH = pl.DeviceIdType.MESH
F32 = jnp.float32
BF16 = jnp.bfloat16
X_CHIPS = 4
MODES = 4
PATCH = 256
ROWS = 96
BANDS = ((0, 40), (40, 80), (80, 96))
COLS = 384
LANES = 128
CHUNK = 64
SEAM = 32
CHUNKS = PATCH // CHUNK
object_rate = 0.25


def dft_parts():
    index = np.arange(PATCH)
    angle = 2.0 * math.pi / PATCH * (np.outer(index, index) % PATCH)
    scale = 1.0 / math.sqrt(PATCH)
    return np.stack([np.cos(angle) * scale, -np.sin(angle) * scale]).astype(np.float32)


def split(value):
    high = value.astype(BF16)
    return high, (value - high.astype(F32)).astype(BF16)


def dot(left, right):
    return jnp.dot(left, right, preferred_element_type=F32)


def column_mask(corner, block, shape):
    lane = lax.broadcasted_iota(jnp.int32, shape, 1) + block * LANES
    return (lane >= corner) & (lane < corner + PATCH)


def loop(count, body, start=0):
    def step(i, carry):
        body(i)
        return carry

    lax.fori_loop(start, count, step, 0)


def tiles(start, size, unit=8):
    return pl.ds(pl.multiple_of(start, unit), size)


class Wires:
    def __init__(self, send, recv):
        self.send, self.recv, self.used, self.open = send, recv, 0, []

    def take(self, count):
        first = self.used
        self.used += count
        return first

    def copy(self, src, dst, scan, mode, slot):
        return pltpu.make_async_remote_copy(
            src_ref=src,
            dst_ref=dst,
            send_sem=self.send.at[slot],
            recv_sem=self.recv.at[slot],
            device_id=(scan, mode),
            device_id_type=MESH,
        )

    def put(self, src, dst, scan, mode):
        copy = self.copy(src, dst, scan, mode, self.take(1))
        copy.start()
        self.open.append(copy)
        return copy

    def drain(self):
        for copy in self.open:
            copy.wait_send()
        self.open = []


def kernel(
    scans, chips_x, chips_z,
    pos_ref, obj_ref, probe_hbm, meas_hbm, dft_hbm,
    obj_out, probe_out,
    probe_ref, meas_ref, dft_ref, row_ops, col_ops,
    strip, corners, pick_next, pick_prev, from_prev, from_next,
    patch, wave, double, stack, far, power, power_a, power_sum, power_b,
    term, term_a, term_sum, term_b, total_term, rim_up, rim_down, grad_prev, grad_next,
    pgrad, pcore, halves, parts_x, shard, parts_z, gathered, gathered_other,
    ordered, new_obj, send_sem, recv_sem, local_sem, out_sem, token_sem_x, token_sem_z,
):
    s = lax.axis_index("scan")
    m = lax.axis_index("mode")
    core = lax.rem(s, 2)
    z = lax.rem(lax.div(s, 2), chips_z)
    x = lax.div(s, 2 * chips_z)
    nxt, prv = lax.rem(s + 1, scans), lax.rem(s + scans - 1, scans)
    m_up, m_dn = lax.rem(m + 1, MODES), lax.rem(m + MODES - 1, MODES)
    pair_a = jnp.where(lax.rem(m, 2) == 0, m + 1, m - 1)
    pair_b = MODES - 1 - m
    other_core = jnp.where(core == 0, s + 1, s - 1)
    wires = Wires(send_sem, recv_sem)
    per_z = 2 * CHUNK // chips_z

    def at_x(step):
        return (lax.rem(x + step, chips_x) * chips_z + z) * 2 + core

    def at_z(step):
        return (x * chips_z + lax.rem(z + step, chips_z)) * 2 + core

    moves = [(obj_ref, strip.at[m]), (dft_hbm, dft_ref), (probe_hbm, probe_ref), (meas_hbm, meas_ref)]
    local = [pltpu.make_async_copy(src, dst, local_sem.at[i]) for i, (src, dst) in enumerate(moves)]
    for copy in local:
        copy.start()
    barrier = pltpu.get_barrier_semaphore()

    def greet(scan, mode):
        pl.semaphore_signal(barrier, inc=1, device_id=(scan, mode), device_id_type=MESH)

    greet(s, m_up)
    greet(s, m_dn)
    greet(nxt, m)
    greet(prv, m)
    near_x = sorted({1, chips_x - 1})
    near_z = sorted({1, chips_z - 1})
    for step in near_x:
        greet(at_x(step), m)
    for step in near_z:
        greet(at_z(step), m)
    pl.semaphore_wait(barrier, 4 + len(near_x) + len(near_z))

    rounds_x = chips_x // 2 - 1
    rounds_z = chips_z // 2 - 1

    def send_token(sem, at, near, turn):
        for way, step in enumerate(near):
            pl.semaphore_signal(sem.at[turn, way], inc=1, device_id=(at(step), m), device_id_type=MESH)

    def take_token(sem, near, turn):
        for way in range(len(near)):
            pl.semaphore_wait(sem.at[turn, way], 1)

    def token_z(turn):
        if 0 < turn <= rounds_z:
            take_token(token_sem_z, near_z, turn - 1)
        if turn < rounds_z:
            send_token(token_sem_z, at_z, near_z, turn)

    def token_x(turn):
        if 0 < turn <= rounds_x:
            take_token(token_sem_x, near_x, turn - 1)
        if turn < rounds_x:
            send_token(token_sem_x, at_x, near_x, turn)

    def cells_of(tile, part, t):
        return strip.at[tile, part, slice(*BANDS[t])]

    up, dn, fwd_up, fwd_dn = {}, {}, {}, {}

    def send_own(t):
        up[0, t] = wires.put(cells_of(m, 0, t), cells_of(m, 0, t), s, m_up)
        dn[1, t] = wires.put(cells_of(m, 1, t), cells_of(m, 1, t), s, m_dn)
        up[1, t] = wires.put(cells_of(m, 1, t), cells_of(m, 1, t), s, m_up)
        dn[0, t] = wires.put(cells_of(m, 0, t), cells_of(m, 0, t), s, m_dn)

    def forward(t):
        up[0, t].wait_recv()
        fwd_up[t] = wires.put(cells_of(m_dn, 0, t), cells_of(m_dn, 0, t), s, m_up)
        dn[1, t].wait_recv()
        fwd_dn[t] = wires.put(cells_of(m_up, 1, t), cells_of(m_up, 1, t), s, m_dn)

    local[0].wait()
    send_own(0)
    row_at = pos_ref[0, 0]
    col_at = pos_ref[0, 1]
    corners[1] = jnp.full((8, LANES), col_at, jnp.int32)
    pos_next = wires.put(corners.at[1], corners.at[0], nxt, m)
    pos_prev = wires.put(corners.at[1], corners.at[2], prv, m)
    send_own(1)
    send_own(2)
    token_x(0)
    token_z(0)
    for copy in local[1:]:
        copy.wait()
    offset = row_at - ROWS * s + ROWS
    turn = jnp.bitwise_and(col_at, PATCH - 1)

    def transforms(i):
        rows = tiles(i * CHUNK, CHUNK, CHUNK)
        low_rows = tiles(PATCH + i * CHUNK, CHUNK, CHUNK)
        for part, (re, im) in enumerate(zip(split(dft_ref[0, rows]), split(dft_ref[1, rows]))):
            at = i * 4 * CHUNK + 2 * part * CHUNK
            for which, sign in enumerate((im, -im)):
                row_ops[which, part, rows, 0:PATCH] = re
                row_ops[which, part, rows, PATCH:] = sign
                row_ops[which, part, low_rows, 0:PATCH] = -sign
                row_ops[which, part, low_rows, PATCH:] = re
                col_ops[which, tiles(at, CHUNK, CHUNK), 0:PATCH] = re
                col_ops[which, tiles(at, CHUNK, CHUNK), PATCH:] = -sign
                col_ops[which, tiles(at + CHUNK, CHUNK, CHUNK), 0:PATCH] = sign
                col_ops[which, tiles(at + CHUNK, CHUNK, CHUNK), PATCH:] = re

    loop(CHUNKS, transforms)
    forward(0)

    def window(part, start, down):
        value = double[part, tiles(start, CHUNK + SEAM, SEAM)]
        return pltpu.roll(value, down, 0)[SEAM:]

    def turn_probe(i):
        rows = tiles(i * CHUNK, CHUNK, CHUNK)
        for part in range(2):
            rolled = pltpu.roll(probe_ref[0, part, rows], turn, 1)
            double[part, rows] = rolled
            double[part, tiles(PATCH + i * CHUNK, CHUNK, CHUNK)] = rolled

    def align_probe(i):
        for part in range(2):
            wave[part, tiles(i * CHUNK, CHUNK, CHUNK)] = window(part, i * CHUNK, offset)

    loop(CHUNKS, turn_probe)
    loop(CHUNKS, align_probe)
    forward(1)
    token_z(1)
    pos_next.wait_recv()
    pos_prev.wait_recv()
    forward(2)
    token_z(2)

    def choose(t):
        for copy in (dn[0, t], fwd_up[t], up[1, t], fwd_dn[t]):
            copy.wait_recv()

        count = (BANDS[t][1] - BANDS[t][0]) // 8

        def pick(j):
            part = lax.div(j, count)
            row = BANDS[t][0] + lax.rem(j, count) * 8
            rows = tiles(row, 8)
            picked = [[jnp.zeros((8, LANES), F32)] * 2 for who in range(3)]
            corner = [corners[who] for who in range(3)]
            for block in range(MODES * COLS // LANES):
                tile, inner = divmod(block, COLS // LANES)
                cells = strip[tile, part, rows, inner * LANES : (inner + 1) * LANES]
                for who in range(3):
                    mask = column_mask(corner[who], block, (8, LANES))
                    picked[who][block % 2] = jnp.where(mask, cells, picked[who][block % 2])
            for half in range(2):
                lanes = slice(half * LANES, (half + 1) * LANES)
                pick_prev[part, rows, lanes] = picked[0][half]
                patch[part, tiles(CHUNK + row, 8), lanes] = picked[1][half]
                pick_next[part, rows, lanes] = picked[2][half]

        loop(2 * count, pick)
        rows = slice(*BANDS[t])
        return (
            wires.put(pick_next.at[:, rows], from_prev.at[:, rows], nxt, m),
            wires.put(pick_prev.at[:, rows], from_next.at[:, rows], prv, m),
        )

    def along_rows(value, which):
        high, low = split(value)
        count = value.shape[0]
        both = dot(jnp.concatenate([high, low], axis=0), row_ops[which, 0])
        return both[:count] + both[count:] + dot(high, row_ops[which, 1])

    def along_columns(i, which):
        at = i * 4 * CHUNK
        both = dot(col_ops[which, tiles(at, 4 * CHUNK, CHUNK)], stack[0])
        result = both[: 2 * CHUNK] + both[2 * CHUNK :]
        result = result + dot(col_ops[which, tiles(at, 2 * CHUNK, CHUNK)], stack[1])
        return result[:CHUNK], result[CHUNK:]

    def keep(value, i):
        high, low = split(value)
        for part in range(2):
            lanes = slice(part * PATCH, (part + 1) * PATCH)
            into = tiles(part * PATCH + i * CHUNK, CHUNK, CHUNK)
            stack[0, into] = high[:, lanes]
            stack[1, into] = low[:, lanes]

    def first_stage(i):
        i = lax.rem(i, CHUNKS)
        rows = tiles(i * CHUNK, CHUNK, CHUNK)
        p_re, p_im = wave[0, rows], wave[1, rows]
        o_re, o_im = patch[0, rows], patch[1, rows]
        exit_wave = jnp.concatenate([p_re * o_re - p_im * o_im, p_re * o_im + p_im * o_re], axis=1)
        keep(along_rows(exit_wave, 0), i)

    halos = []
    for t in range(3):
        halos.append(choose(t))
        token_z(3 + t)
    for halo in halos[:2]:
        for copy in halo:
            copy.wait_recv()
    for part in range(2):
        patch[part, 160:224] = jnp.where(s < scans - 1, from_next[part, 0:64], 0.0)
    loop(3, first_stage, 1)
    seam = lax.broadcasted_iota(jnp.int32, (SEAM, PATCH), 0)
    for copy in halos[2]:
        copy.wait_recv()
    for part in range(2):
        above = jnp.where(s > 0, from_prev[part, 0:32], 0.0)
        below = jnp.where(s < scans - 1, from_next[part, 64:96], 0.0)
        patch[part, 224:256] = jnp.where(seam >= offset, above, below)
        patch[part, 0:64] = jnp.where(s > 0, from_prev[part, 32:96], 0.0)
    loop(5, first_stage, 3)

    def chunk_of(i):
        return tiles(i * CHUNK, CHUNK, CHUNK)

    def route(i):
        even = lax.rem(i, 2) == 0
        return jnp.where(even, pair_a, pair_b), jnp.where(even, pair_b, pair_a)

    power_slot = wires.take(2 * CHUNKS)

    def power_hop(i, second):
        rows = chunk_of(i)
        src, dst = (power_sum, power_b) if second else (power, power_a)
        slot = power_slot + second * CHUNKS + i
        return wires.copy(src.at[rows], dst.at[rows], s, route(i)[second], slot)

    def to_far(i):
        rows = chunk_of(i)
        f_re, f_im = along_columns(i, 0)
        far[0, rows] = f_re
        far[1, rows] = f_im
        power[rows] = f_re * f_re + f_im * f_im
        power_hop(i, 0).start()

    def add_power(i):
        rows = chunk_of(i)
        power_hop(i, 0).wait_recv()
        power_sum[rows] = power[rows] + power_a[rows]
        power_hop(i, 1).start()

    def rescale(i):
        rows = chunk_of(i)
        power_hop(i, 1).wait_recv()
        intensity = power_sum[rows] + power_b[rows]
        factor = 1.0 - meas_ref[0, rows] / jnp.sqrt(jnp.maximum(intensity, 1.0))
        scaled = jnp.concatenate([far[0, rows] * factor, far[1, rows] * factor], axis=1)
        keep(along_rows(scaled, 1), i)

    loop(CHUNKS, to_far)
    token_z(6)
    wires.drain()
    loop(CHUNKS, add_power)
    token_z(7)
    token_x(1)
    loop(CHUNKS, rescale)

    term_slot = wires.take(2 * CHUNKS)
    core_slot = wires.take(2 * CHUNKS)

    def nth(j):
        return lax.rem(x + j, CHUNKS)

    def term_hop(j, second):
        rows = chunk_of(nth(j))
        src, dst = (term_sum, term_b) if second else (term, term_a)
        slot = term_slot + second * CHUNKS + j
        return wires.copy(src.at[:, rows], dst.at[:, rows], s, route(j)[second], slot)

    def core_hop(j):
        n = nth(j)
        return wires.copy(pgrad.at[1 - core, n], pcore.at[n], other_core, m, core_slot + j - 1)

    def send_probe_terms(j):
        n = nth(j)
        for part in range(2):
            value = window(part, n * CHUNK + PATCH - SEAM, SEAM - offset)
            pgrad[part, n, 0:CHUNK] = value[:, :LANES]
            pgrad[part, n, CHUNK:] = value[:, LANES:]
        core_hop(j).start()

    def to_object(j):
        i = nth(j)
        rows = chunk_of(i)
        b_re, b_im = along_columns(i, 1)
        p_re, p_im = wave[0, rows], wave[1, rows]
        term[0, rows] = p_re * b_re + p_im * b_im
        term[1, rows] = p_re * b_im - p_im * b_re
        o_re, o_im = patch[0, rows], patch[1, rows]
        for part, value in enumerate((o_re * b_re + o_im * b_im, o_re * b_im - o_im * b_re)):
            value = pltpu.roll(value, PATCH - turn, 1)
            double[part, rows] = value
            double[part, tiles(PATCH + i * CHUNK, CHUNK, CHUNK)] = value

        @pl.when(j > 0)
        def _():
            send_probe_terms(j)

    loop(CHUNKS, to_object)
    send_probe_terms(CHUNKS)
    loop(CHUNKS // 2, lambda j: term_hop(j, 0).start())

    assert rounds_x <= 1 and rounds_z <= 7


    block_z = max(chips_z // 4, 1)
    blocks = chips_z // block_z
    order = sorted(range(chips_z), key=lambda step: -min(step, chips_z - step))

    def piece(i):
        return slice(i * per_z, (i + 1) * per_z)

    def piece_z(i):
        return lax.rem(z + order[i], chips_z)

    def distance(i):
        return order[i]

    def opposite(i):
        return order.index((chips_z - order[i]) % chips_z)

    mine_at = order.index(0)
    x_slot = wires.take(blocks * chips_x)
    back_x_slot = wires.take(blocks * chips_x)
    z_slot = wires.take(chips_z)
    back_z_slot = wires.take(chips_z)

    def block_rows(b):
        return pl.ds(b * block_z * per_z, block_z * per_z)

    def x_hop(j, b):
        rows = block_rows(b)
        return wires.copy(halves.at[nth(j), rows], parts_x.at[j, rows], at_x(j), m, x_slot + blocks * j + b)

    def z_rows(at):
        return tiles(at * per_z, per_z)

    def add_core(j):
        n = nth(j)
        core_hop(j).wait_recv()
        for i in range(chips_z):
            rows = z_rows(piece_z(i))
            halves[n, piece(i)] = pgrad[core, n, rows] + pcore[n, rows]

    def add_core_and_send(j):
        add_core(j)
        x_hop(j, 0).start()

    loop(chips_x, add_core_and_send, 1)
    for b in range(1, blocks):
        loop(chips_x, lambda j: x_hop(j, b).start(), 1)
    loop(CHUNKS, lambda j: term_hop(j, 0).start(), CHUNKS // 2)
    add_core(CHUNKS)

    def add_term(j):
        rows = chunk_of(nth(j))
        term_hop(j, 0).wait_recv()
        term_sum[:, rows] = term[:, rows] + term_a[:, rows]
        term_hop(j, 1).start()

    def z_hop(i):
        j = distance(i)
        return wires.copy(shard.at[piece(i)], parts_z.at[j], at_z(j), m, z_slot + j)

    others = [i for i in range(chips_z) if i != mine_at]

    loop(CHUNKS // 2, add_term)
    for b in range(blocks):
        rows = block_rows(b)
        total = halves[x, rows]
        for j in range(1, chips_x):
            x_hop(j, b).wait_recv()
            total = total + parts_x[j, rows]
        shard[rows] = total

        for i in (i for i in others if i // block_z == b):
            z_hop(i).start()

    loop(CHUNKS, add_term, CHUNKS // 2)
    loop(CHUNKS, lambda i: (power_hop(i, 0).wait_send(), power_hop(i, 1).wait_send()))

    total = shard[piece(mine_at)]
    for i in reversed(others):
        z_hop(i).wait_recv()
        total = total + parts_z[distance(i)]
    first = z * per_z
    half = lax.div(first, CHUNK) if per_z <= CHUNK else 0
    scale = 1.0 / math.sqrt(scans)
    old_rows = tiles(x * CHUNK + lax.rem(first, CHUNK), per_z)
    old = probe_ref[0, core, old_rows, tiles(half * LANES, LANES, LANES)]
    gathered[x, piece(mine_at)] = old - total * scale

    def back_z_hop(i):
        j = distance(i)
        there = piece(opposite(i))
        src = gathered.at[x, piece(mine_at)]
        return wires.copy(src, gathered.at[x, there], at_z(j), m, back_z_slot + j)

    for i in others:
        back_z_hop(i).start()

    def back_x_hop(j, b):
        mine = gathered.at[x, block_rows(b)]
        return wires.copy(mine, mine, at_x(j), m, back_x_slot + blocks * j + b)

    def total_terms(j):
        rows = chunk_of(nth(j))
        term_hop(j, 1).wait_recv()
        total_term[:, rows] = term_sum[:, rows] + term_b[:, rows]

    def make_rims():
        loop(CHUNKS, total_terms)
        for part in range(2):
            edge = total_term[part, 224:256]
            rim_up[part, 0:32] = jnp.where(seam >= offset, edge, 0.0)
            rim_up[part, 32:96] = total_term[part, 0:64]
            rim_down[part, 0:64] = total_term[part, 160:224]
            rim_down[part, 64:96] = jnp.where(seam < offset, edge, 0.0)

    for b in reversed(range(blocks)):
        for i in others:
            if opposite(i) // block_z == b:
                back_z_hop(i).wait_recv()
        loop(chips_x, lambda j: back_x_hop(j, b).start(), 1)
        if b == max(blocks - 2, 0):
            make_rims()

    def back_core_hop(j):
        mine = nth(CHUNKS - j)
        return wires.copy(gathered.at[mine], gathered_other.at[mine], other_core, m, core_slot + CHUNKS + j)

    back_core_hop(0).start()

    to_prev = wires.put(rim_up, grad_next, prv, m)
    to_next = wires.put(rim_down, grad_prev, nxt, m)

    loop(CHUNKS, lambda j: (term_hop(j, 0).wait_send(), term_hop(j, 1).wait_send()))
    loop(CHUNKS + 1, lambda j: core_hop(j).wait_send(), 1)
    for b in range(blocks):
        loop(chips_x, lambda j: x_hop(j, b).wait_send(), 1)
    for i in others:
        z_hop(i).wait_send()
        back_z_hop(i).wait_send()

    def probe_copy(which, source, n, half, slot):
        return pltpu.make_async_copy(
            source.at[n, half * CHUNK : (half + 1) * CHUNK],
            probe_out.at[0, which, chunk_of(n), half * LANES : (half + 1) * LANES],
            out_sem.at[slot],
        )

    def mine_copy(j, half):
        return probe_copy(core, ordered.at[0], nth(CHUNKS - j), half, 1 + 2 * j + half)

    def other_copy(j, half):
        return probe_copy(1 - core, ordered.at[1], nth(CHUNKS - j), half, 1 + 2 * (CHUNKS + j) + half)

    def put_both(copy, source, j):
        n = nth(CHUNKS - j)
        for i in range(chips_z):
            ordered_rows = z_rows(piece_z(i))
            ordered[source, n, ordered_rows] = (gathered, gathered_other)[source][n, piece(i)]
        copy(j, 0).start()
        copy(j, 1).start()

    def wait_both(copy, j):
        copy(j, 0).wait()
        copy(j, 1).wait()

    put_both(mine_copy, 0, 0)

    def tile_part(inner):
        shape = (ROWS, LANES)
        block = m * (COLS // LANES) + inner
        lanes = tiles(lax.rem(block, 2) * LANES, LANES, LANES)

        def mask(who):
            return column_mask(jnp.broadcast_to(corners[who, 0:1, :], shape), block, shape)

        return slice(inner * LANES, (inner + 1) * LANES), lanes, mask

    for inner in range(COLS // LANES):
        here, lanes, mask = tile_part(inner)
        for part in range(2):
            own = jnp.where(mask(1), total_term[part, CHUNK : CHUNK + ROWS, lanes], 0.0)
            new_obj[part, :, here] = strip[m, part, :, here] - object_rate * own

    def pass_on(j):
        for b in range(blocks):
            back_x_hop(j, b).wait_recv()
        back_core_hop(j).start()
        put_both(mine_copy, 0, j)

    loop(chips_x, pass_on, 1)

    to_prev.wait_recv()
    to_next.wait_recv()
    for inner in range(COLS // LANES):
        here, lanes, mask = tile_part(inner)
        for part in range(2):
            above = jnp.where(mask(0) & (s > 0), grad_prev[part, :, lanes], 0.0)
            below = jnp.where(mask(2) & (s < scans - 1), grad_next[part, :, lanes], 0.0)
            new_obj[part, :, here] = new_obj[part, :, here] - object_rate * (above + below)
    obj_copy = pltpu.make_async_copy(new_obj, obj_out, out_sem.at[0])
    obj_copy.start()
    wires.drain()

    def take_core(j):
        back_core_hop(j).wait_recv()
        put_both(other_copy, 1, j)

    loop(CHUNKS, take_core)
    loop(CHUNKS, lambda j: back_core_hop(j).wait_send())
    for b in range(blocks):
        loop(chips_x, lambda j: back_x_hop(j, b).wait_send(), 1)
    obj_copy.wait()
    loop(CHUNKS, lambda j: (wait_both(mine_copy, j), wait_both(other_copy, j)))


PIECES = 4


def placing(obj_in, probe_in, obj_out, probe_out, sem):
    copies = []
    for src, dst, dim in ((obj_in, obj_out, 1), (probe_in, probe_out, 2)):
        size = src.shape[dim] // PIECES
        for i in range(PIECES):
            at = (slice(None),) * dim + (slice(i * size, (i + 1) * size),)
            copies.append(pltpu.make_async_copy(src.at[at], dst.at[at], sem.at[len(copies)]))
    for copy in copies:
        copy.start()
    for copy in copies:
        copy.wait()


def per_device(scans, chips_x, object_field, probe, measured, positions):
    chips_z = scans // (2 * chips_x)
    per_z = 2 * CHUNK // chips_z
    wire_count = 28 + 6 * CHUNKS + 8 * chips_x + 2 * chips_z
    field = pltpu.VMEM((2, PATCH, PATCH), F32)
    plane = pltpu.VMEM((PATCH, PATCH), F32)
    rim = pltpu.VMEM((2, ROWS, PATCH), F32)
    share = pltpu.VMEM((CHUNKS, 2 * CHUNK, LANES), F32)
    hbm = pl.BlockSpec(memory_space=pltpu.HBM)
    anywhere = pl.BlockSpec(memory_space=pl.ANY)
    out_shape = (
        jax.ShapeDtypeStruct(object_field.shape, F32),
        jax.ShapeDtypeStruct(probe.shape, F32),
    )
    results = pl.pallas_call(
        functools.partial(kernel, scans, chips_x, chips_z),
        out_shape=out_shape,
        in_specs=[pl.BlockSpec(memory_space=pltpu.SMEM)] + [hbm] * 4,
        out_specs=(anywhere, anywhere),
        scratch_shapes=[
            pltpu.VMEM(probe.shape, F32),
            pltpu.VMEM(measured.shape, F32),
            field,
            pltpu.VMEM((2, 2, 2 * PATCH, 2 * PATCH), BF16),
            pltpu.VMEM((2, 4 * PATCH, 2 * PATCH), BF16),
            pltpu.VMEM((MODES, 2, ROWS, COLS), F32),
            pltpu.VMEM((3, 8, LANES), jnp.int32),
            rim, rim, rim, rim,
            field, field,
            pltpu.VMEM((2, 2 * PATCH, PATCH), F32),
            pltpu.VMEM((2, 2 * PATCH, PATCH), BF16),
            field,
            plane, plane, plane, plane,
            field, field, field, field, field,
            rim, rim, rim, rim,
            pltpu.VMEM((2, CHUNKS, 2 * CHUNK, LANES), F32),
            share, share, share,
            pltpu.VMEM((2 * CHUNK, LANES), F32),
            pltpu.VMEM((chips_z, per_z, LANES), F32),
            share, share,
            pltpu.VMEM((2, CHUNKS, 2 * CHUNK, LANES), F32),
            pltpu.VMEM(object_field.shape, F32),
            pltpu.SemaphoreType.DMA((wire_count,)),
            pltpu.SemaphoreType.DMA((wire_count,)),
            pltpu.SemaphoreType.DMA((4,)),
            pltpu.SemaphoreType.DMA((1 + 4 * CHUNKS,)),
            pltpu.SemaphoreType.REGULAR((max(chips_x // 2 - 1, 1), 2)),
            pltpu.SemaphoreType.REGULAR((max(chips_z // 2 - 1, 1), 2)),
        ],
        compiler_params=pltpu.CompilerParams(
            collective_id=0, has_side_effects=True, vmem_limit_bytes=32 << 20
        ),
        cost_estimate=pl.CostEstimate(flops=1 << 31, bytes_accessed=4 << 20, transcendentals=0),
    )(*[
        pltpu.with_memory_space_constraint(value, pltpu.HBM)
        for value in (positions, object_field, probe, measured, jnp.asarray(dft_parts()))
    ])
    return pl.pallas_call(
        placing,
        out_shape=out_shape,
        in_specs=[anywhere, anywhere],
        out_specs=(hbm, hbm),
        scratch_shapes=[pltpu.SemaphoreType.DMA((2 * PIECES,))],
    )(*[pltpu.with_memory_space_constraint(value, pltpu.VMEM) for value in results])


def solution(mesh):
    return jax.shard_map(
        functools.partial(per_device, mesh.shape["scan"], X_CHIPS),
        mesh=mesh,
        in_specs=(
            P(None, "scan", "mode"),
            P("mode", None, None, None),
            P("scan", None, None),
            P("scan", None),
        ),
        out_specs=(P(None, "scan", "mode"), P("mode", None, None, None)),
        check_vma=False,
    )
```

```python
import functools
import math

import jax
import jax.numpy as jnp
import ml_dtypes
import numpy as np
from jax import lax
from jax.experimental import pallas as pl
from jax.experimental.pallas import tpu as pltpu
from jax.sharding import PartitionSpec as P

MESH = pl.DeviceIdType.MESH
F32 = jnp.float32
BF16 = jnp.bfloat16
X_CHIPS = 4
MODES = 4
PATCH = 256
ROWS = 96
BANDS = ((0, 40), (40, 80), (80, 96))
COLS = 384
LANES = 128
CHUNK = 64
SEAM = 32
CHUNKS = PATCH // CHUNK
object_rate = 0.25


def dft_parts():
    index = np.arange(PATCH)
    angle = 2.0 * math.pi / PATCH * (np.outer(index, index) % PATCH)
    scale = 1.0 / math.sqrt(PATCH)
    return np.stack([np.cos(angle) * scale, -np.sin(angle) * scale]).astype(np.float32)


def split(value):
    high = value.astype(BF16)
    return high, (value - high.astype(F32)).astype(BF16)


def dot(left, right):
    return jnp.dot(left, right, preferred_element_type=F32)


def column_mask(corner, block, shape):
    lane = lax.broadcasted_iota(jnp.int32, shape, 1) + block * LANES
    return (lane >= corner) & (lane < corner + PATCH)


def loop(count, body, start=0):
    def step(i, carry):
        body(i)
        return carry

    lax.fori_loop(start, count, step, 0)


def tiles(start, size, unit=8):
    return pl.ds(pl.multiple_of(start, unit), size)


class Wires:
    def __init__(self, send, recv):
        self.send, self.recv, self.used, self.open = send, recv, 0, []

    def take(self, count):
        first = self.used
        self.used += count
        return first

    def copy(self, src, dst, scan, mode, slot):
        return pltpu.make_async_remote_copy(
            src_ref=src,
            dst_ref=dst,
            send_sem=self.send.at[slot],
            recv_sem=self.recv.at[slot],
            device_id=(scan, mode),
            device_id_type=MESH,
        )

    def put(self, src, dst, scan, mode):
        copy = self.copy(src, dst, scan, mode, self.take(1))
        copy.start()
        self.open.append(copy)
        return copy

    def drain(self):
        for copy in self.open:
            copy.wait_send()
        self.open = []


def kernel(
    scans, chips_x, chips_z,
    pos_ref, obj_ref, probe_hbm, meas_hbm, dft_hbm,
    obj_out, probe_out,
    probe_ref, meas_ref, dft_ref, row_ops, col_ops,
    strip, corners, pick_next, pick_prev, from_prev, from_next,
    patch, wave, double, stack, far, power, power_a, power_sum, power_b,
    term, term_a, term_sum, term_b, total_term, rim_up, rim_down, grad_prev, grad_next,
    pgrad, pcore, halves, parts_x, shard, parts_z, gathered, gathered_other,
    ordered, new_obj, send_sem, recv_sem, local_sem, out_sem, token_sem_x, token_sem_z,
):
    s = lax.axis_index("scan")
    m = lax.axis_index("mode")
    core = lax.rem(s, 2)
    z = lax.rem(lax.div(s, 2), chips_z)
    x = lax.div(s, 2 * chips_z)
    nxt, prv = lax.rem(s + 1, scans), lax.rem(s + scans - 1, scans)
    m_up, m_dn = lax.rem(m + 1, MODES), lax.rem(m + MODES - 1, MODES)
    pair_a = jnp.where(lax.rem(m, 2) == 0, m + 1, m - 1)
    pair_b = MODES - 1 - m
    other_core = jnp.where(core == 0, s + 1, s - 1)
    wires = Wires(send_sem, recv_sem)
    per_z = 2 * CHUNK // chips_z

    def at_x(step):
        return (lax.rem(x + step, chips_x) * chips_z + z) * 2 + core

    def at_z(step):
        return (x * chips_z + lax.rem(z + step, chips_z)) * 2 + core

    moves = [(obj_ref, strip.at[m]), (dft_hbm, dft_ref), (probe_hbm, probe_ref), (meas_hbm, meas_ref)]
    local = [pltpu.make_async_copy(src, dst, local_sem.at[i]) for i, (src, dst) in enumerate(moves)]
    for copy in local:
        copy.start()
    barrier = pltpu.get_barrier_semaphore()

    def greet(scan, mode):
        pl.semaphore_signal(barrier, inc=1, device_id=(scan, mode), device_id_type=MESH)

    greet(s, m_up)
    greet(s, m_dn)
    greet(nxt, m)
    greet(prv, m)
    near_x = sorted({1, chips_x - 1})
    near_z = sorted({1, chips_z - 1})
    for step in near_x:
        greet(at_x(step), m)
    for step in near_z:
        greet(at_z(step), m)
    pl.semaphore_wait(barrier, 4 + len(near_x) + len(near_z))

    rounds_x = chips_x // 2 - 1
    rounds_z = chips_z // 2 - 1

    def send_token(sem, at, near, turn):
        for way, step in enumerate(near):
            pl.semaphore_signal(sem.at[turn, way], inc=1, device_id=(at(step), m), device_id_type=MESH)

    def take_token(sem, near, turn):
        for way in range(len(near)):
            pl.semaphore_wait(sem.at[turn, way], 1)

    def token_z(turn):
        if 0 < turn <= rounds_z:
            take_token(token_sem_z, near_z, turn - 1)
        if turn < rounds_z:
            send_token(token_sem_z, at_z, near_z, turn)

    def token_x(turn):
        if 0 < turn <= rounds_x:
            take_token(token_sem_x, near_x, turn - 1)
        if turn < rounds_x:
            send_token(token_sem_x, at_x, near_x, turn)

    def cells_of(tile, part, t):
        return strip.at[tile, part, slice(*BANDS[t])]

    up, dn, fwd_up, fwd_dn = {}, {}, {}, {}

    def send_own(t):
        up[0, t] = wires.put(cells_of(m, 0, t), cells_of(m, 0, t), s, m_up)
        dn[1, t] = wires.put(cells_of(m, 1, t), cells_of(m, 1, t), s, m_dn)
        up[1, t] = wires.put(cells_of(m, 1, t), cells_of(m, 1, t), s, m_up)
        dn[0, t] = wires.put(cells_of(m, 0, t), cells_of(m, 0, t), s, m_dn)

    def forward(t):
        up[0, t].wait_recv()
        fwd_up[t] = wires.put(cells_of(m_dn, 0, t), cells_of(m_dn, 0, t), s, m_up)
        dn[1, t].wait_recv()
        fwd_dn[t] = wires.put(cells_of(m_up, 1, t), cells_of(m_up, 1, t), s, m_dn)

    local[0].wait()
    send_own(0)
    row_at = pos_ref[0, 0]
    col_at = pos_ref[0, 1]
    corners[1] = jnp.full((8, LANES), col_at, jnp.int32)
    pos_next = wires.put(corners.at[1], corners.at[0], nxt, m)
    pos_prev = wires.put(corners.at[1], corners.at[2], prv, m)
    send_own(1)
    send_own(2)
    token_x(0)
    token_z(0)
    for copy in local[1:]:
        copy.wait()
    offset = row_at - ROWS * s + ROWS
    turn = jnp.bitwise_and(col_at, PATCH - 1)

    def transforms(i):
        rows = tiles(i * CHUNK, CHUNK, CHUNK)
        low_rows = tiles(PATCH + i * CHUNK, CHUNK, CHUNK)
        for part, (re, im) in enumerate(zip(split(dft_ref[0, rows]), split(dft_ref[1, rows]))):
            at = i * 4 * CHUNK + 2 * part * CHUNK
            for which, sign in enumerate((im, -im)):
                row_ops[which, part, rows, 0:PATCH] = re
                row_ops[which, part, rows, PATCH:] = sign
                row_ops[which, part, low_rows, 0:PATCH] = -sign
                row_ops[which, part, low_rows, PATCH:] = re
                col_ops[which, tiles(at, CHUNK, CHUNK), 0:PATCH] = re
                col_ops[which, tiles(at, CHUNK, CHUNK), PATCH:] = -sign
                col_ops[which, tiles(at + CHUNK, CHUNK, CHUNK), 0:PATCH] = sign
                col_ops[which, tiles(at + CHUNK, CHUNK, CHUNK), PATCH:] = re

    loop(CHUNKS, transforms)
    forward(0)

    def window(part, start, down):
        value = double[part, tiles(start, CHUNK + SEAM, SEAM)]
        return pltpu.roll(value, down, 0)[SEAM:]

    def turn_probe(i):
        rows = tiles(i * CHUNK, CHUNK, CHUNK)
        for part in range(2):
            rolled = pltpu.roll(probe_ref[0, part, rows], turn, 1)
            double[part, rows] = rolled
            double[part, tiles(PATCH + i * CHUNK, CHUNK, CHUNK)] = rolled

    def align_probe(i):
        for part in range(2):
            wave[part, tiles(i * CHUNK, CHUNK, CHUNK)] = window(part, i * CHUNK, offset)

    loop(CHUNKS, turn_probe)
    loop(CHUNKS, align_probe)
    forward(1)
    token_z(1)
    pos_next.wait_recv()
    pos_prev.wait_recv()
    forward(2)
    token_z(2)

    def choose(t):
        for copy in (dn[0, t], fwd_up[t], up[1, t], fwd_dn[t]):
            copy.wait_recv()

        count = (BANDS[t][1] - BANDS[t][0]) // 8

        def pick(j):
            part = lax.div(j, count)
            row = BANDS[t][0] + lax.rem(j, count) * 8
            rows = tiles(row, 8)
            picked = [[jnp.zeros((8, LANES), F32)] * 2 for who in range(3)]
            corner = [corners[who] for who in range(3)]
            for block in range(MODES * COLS // LANES):
                tile, inner = divmod(block, COLS // LANES)
                cells = strip[tile, part, rows, inner * LANES : (inner + 1) * LANES]
                for who in range(3):
                    mask = column_mask(corner[who], block, (8, LANES))
                    picked[who][block % 2] = jnp.where(mask, cells, picked[who][block % 2])
            for half in range(2):
                lanes = slice(half * LANES, (half + 1) * LANES)
                pick_prev[part, rows, lanes] = picked[0][half]
                patch[part, tiles(CHUNK + row, 8), lanes] = picked[1][half]
                pick_next[part, rows, lanes] = picked[2][half]

        loop(2 * count, pick)
        rows = slice(*BANDS[t])
        return (
            wires.put(pick_next.at[:, rows], from_prev.at[:, rows], nxt, m),
            wires.put(pick_prev.at[:, rows], from_next.at[:, rows], prv, m),
        )

    def along_rows(value, which):
        high, low = split(value)
        count = value.shape[0]
        both = dot(jnp.concatenate([high, low], axis=0), row_ops[which, 0])
        return both[:count] + both[count:] + dot(high, row_ops[which, 1])

    def along_columns(i, which):
        at = i * 4 * CHUNK
        both = dot(col_ops[which, tiles(at, 4 * CHUNK, CHUNK)], stack[0])
        result = both[: 2 * CHUNK] + both[2 * CHUNK :]
        result = result + dot(col_ops[which, tiles(at, 2 * CHUNK, CHUNK)], stack[1])
        return result[:CHUNK], result[CHUNK:]

    def keep(value, i):
        high, low = split(value)
        for part in range(2):
            lanes = slice(part * PATCH, (part + 1) * PATCH)
            into = tiles(part * PATCH + i * CHUNK, CHUNK, CHUNK)
            stack[0, into] = high[:, lanes]
            stack[1, into] = low[:, lanes]

    def first_stage(i):
        i = lax.rem(i, CHUNKS)
        rows = tiles(i * CHUNK, CHUNK, CHUNK)
        p_re, p_im = wave[0, rows], wave[1, rows]
        o_re, o_im = patch[0, rows], patch[1, rows]
        exit_wave = jnp.concatenate([p_re * o_re - p_im * o_im, p_re * o_im + p_im * o_re], axis=1)
        keep(along_rows(exit_wave, 0), i)

    halos = []
    for t in range(3):
        halos.append(choose(t))
        token_z(3 + t)
    for halo in halos[:2]:
        for copy in halo:
            copy.wait_recv()
    for part in range(2):
        patch[part, 160:224] = jnp.where(s < scans - 1, from_next[part, 0:64], 0.0)
    loop(3, first_stage, 1)
    seam = lax.broadcasted_iota(jnp.int32, (SEAM, PATCH), 0)
    for copy in halos[2]:
        copy.wait_recv()
    for part in range(2):
        above = jnp.where(s > 0, from_prev[part, 0:32], 0.0)
        below = jnp.where(s < scans - 1, from_next[part, 64:96], 0.0)
        patch[part, 224:256] = jnp.where(seam >= offset, above, below)
        patch[part, 0:64] = jnp.where(s > 0, from_prev[part, 32:96], 0.0)
    loop(5, first_stage, 3)

    def chunk_of(i):
        return tiles(i * CHUNK, CHUNK, CHUNK)

    def route(i):
        even = lax.rem(i, 2) == 0
        return jnp.where(even, pair_a, pair_b), jnp.where(even, pair_b, pair_a)

    power_slot = wires.take(2 * CHUNKS)

    def power_hop(i, second):
        rows = chunk_of(i)
        src, dst = (power_sum, power_b) if second else (power, power_a)
        slot = power_slot + second * CHUNKS + i
        return wires.copy(src.at[rows], dst.at[rows], s, route(i)[second], slot)

    def to_far(i):
        rows = chunk_of(i)
        f_re, f_im = along_columns(i, 0)
        far[0, rows] = f_re
        far[1, rows] = f_im
        power[rows] = f_re * f_re + f_im * f_im
        power_hop(i, 0).start()

    def add_power(i):
        rows = chunk_of(i)
        power_hop(i, 0).wait_recv()
        power_sum[rows] = power[rows] + power_a[rows]
        power_hop(i, 1).start()

    def rescale(i):
        rows = chunk_of(i)
        power_hop(i, 1).wait_recv()
        intensity = power_sum[rows] + power_b[rows]
        factor = 1.0 - meas_ref[0, rows] / jnp.sqrt(jnp.maximum(intensity, 1.0))
        scaled = jnp.concatenate([far[0, rows] * factor, far[1, rows] * factor], axis=1)
        keep(along_rows(scaled, 1), i)

    loop(CHUNKS, to_far)
    token_z(6)
    wires.drain()
    loop(CHUNKS, add_power)
    token_z(7)
    token_x(1)
    loop(CHUNKS, rescale)

    term_slot = wires.take(2 * CHUNKS)
    core_slot = wires.take(2 * CHUNKS)

    def nth(j):
        return lax.rem(x + j, CHUNKS)

    def term_hop(j, second):
        rows = chunk_of(nth(j))
        src, dst = (term_sum, term_b) if second else (term, term_a)
        slot = term_slot + second * CHUNKS + j
        return wires.copy(src.at[:, rows], dst.at[:, rows], s, route(j)[second], slot)

    def core_hop(j):
        n = nth(j)
        return wires.copy(pgrad.at[1 - core, n], pcore.at[n], other_core, m, core_slot + j - 1)

    def send_probe_terms(j):
        n = nth(j)
        for part in range(2):
            value = window(part, n * CHUNK + PATCH - SEAM, SEAM - offset)
            pgrad[part, n, 0:CHUNK] = value[:, :LANES]
            pgrad[part, n, CHUNK:] = value[:, LANES:]
        core_hop(j).start()

    def to_object(j):
        i = nth(j)
        rows = chunk_of(i)
        b_re, b_im = along_columns(i, 1)
        p_re, p_im = wave[0, rows], wave[1, rows]
        term[0, rows] = p_re * b_re + p_im * b_im
        term[1, rows] = p_re * b_im - p_im * b_re
        o_re, o_im = patch[0, rows], patch[1, rows]
        for part, value in enumerate((o_re * b_re + o_im * b_im, o_re * b_im - o_im * b_re)):
            value = pltpu.roll(value, PATCH - turn, 1)
            double[part, rows] = value
            double[part, tiles(PATCH + i * CHUNK, CHUNK, CHUNK)] = value

        @pl.when(j > 0)
        def _():
            send_probe_terms(j)

    loop(CHUNKS, to_object)
    send_probe_terms(CHUNKS)
    loop(CHUNKS // 2, lambda j: term_hop(j, 0).start())

    assert rounds_x <= 1 and rounds_z <= 7

    x_slot = wires.take(2 * chips_x)
    back_x_slot = wires.take(2 * chips_x)
    z_slot = wires.take(chips_z)
    back_z_slot = wires.take(chips_z)

    block_z = max(chips_z // 2, 1)
    blocks = chips_z // block_z
    quarter = chips_z // 4

    def piece(i):
        return slice(i * per_z, (i + 1) * per_z)

    def piece_z(i):
        return lax.rem(z + quarter + i, chips_z)

    def distance(i):
        return (quarter + i) % chips_z

    mine_at = (chips_z - quarter) % chips_z

    def far_first(places):
        return sorted(places, key=lambda i: -min(distance(i), chips_z - distance(i)))

    def block_rows(b):
        return pl.ds(b * block_z * per_z, block_z * per_z)

    def x_hop(j, b):
        rows = block_rows(b)
        return wires.copy(halves.at[nth(j), rows], parts_x.at[j, rows], at_x(j), m, x_slot + 2 * j + b)

    def z_rows(at):
        return tiles(at * per_z, per_z)

    def add_core(j):
        n = nth(j)
        core_hop(j).wait_recv()
        for i in range(chips_z):
            rows = z_rows(piece_z(i))
            halves[n, piece(i)] = pgrad[core, n, rows] + pcore[n, rows]

    def add_core_and_send(j):
        add_core(j)
        x_hop(j, 0).start()

    loop(chips_x, add_core_and_send, 1)
    for b in range(1, blocks):
        loop(chips_x, lambda j: x_hop(j, b).start(), 1)
    loop(CHUNKS, lambda j: term_hop(j, 0).start(), CHUNKS // 2)
    add_core(CHUNKS)

    def add_term(j):
        rows = chunk_of(nth(j))
        term_hop(j, 0).wait_recv()
        term_sum[:, rows] = term[:, rows] + term_a[:, rows]
        term_hop(j, 1).start()

    def z_hop(i):
        j = distance(i)
        return wires.copy(shard.at[piece(i)], parts_z.at[j], at_z(j), m, z_slot + j)

    others = [i for i in range(chips_z) if i != mine_at]

    loop(CHUNKS // 2, add_term)
    for b in range(blocks):
        rows = block_rows(b)
        total = halves[x, rows]
        for j in range(1, chips_x):
            x_hop(j, b).wait_recv()
            total = total + parts_x[j, rows]
        shard[rows] = total

        for i in far_first(i for i in others if i // block_z == b):
            z_hop(i).start()

    loop(CHUNKS, add_term, CHUNKS // 2)
    loop(CHUNKS, lambda i: (power_hop(i, 0).wait_send(), power_hop(i, 1).wait_send()))

    total = shard[piece(mine_at)]
    for i in reversed(far_first(others)):
        z_hop(i).wait_recv()
        total = total + parts_z[distance(i)]
    first = z * per_z
    half = lax.div(first, CHUNK) if per_z <= CHUNK else 0
    scale = 1.0 / math.sqrt(scans)
    old_rows = tiles(x * CHUNK + lax.rem(first, CHUNK), per_z)
    old = probe_ref[0, core, old_rows, tiles(half * LANES, LANES, LANES)]
    gathered[x, piece(mine_at)] = old - total * scale

    def back_z_hop(i):
        j = distance(i)
        there = piece((mine_at - j) % chips_z)
        src = gathered.at[x, piece(mine_at)]
        return wires.copy(src, gathered.at[x, there], at_z(j), m, back_z_slot + j)

    for i in far_first(others):
        back_z_hop(i).start()

    def back_x_hop(j, b):
        mine = gathered.at[x, block_rows(b)]
        return wires.copy(mine, mine, at_x(j), m, back_x_slot + 2 * j + b)

    def total_terms(j):
        rows = chunk_of(nth(j))
        term_hop(j, 1).wait_recv()
        total_term[:, rows] = term_sum[:, rows] + term_b[:, rows]

    def make_rims():
        loop(CHUNKS, total_terms)
        for part in range(2):
            edge = total_term[part, 224:256]
            rim_up[part, 0:32] = jnp.where(seam >= offset, edge, 0.0)
            rim_up[part, 32:96] = total_term[part, 0:64]
            rim_down[part, 0:64] = total_term[part, 160:224]
            rim_down[part, 64:96] = jnp.where(seam < offset, edge, 0.0)

    for b in reversed(range(blocks)):
        for i in range(chips_z):
            if i != mine_at and (mine_at - distance(i)) % chips_z // block_z == b:
                back_z_hop(i).wait_recv()
        loop(chips_x, lambda j: back_x_hop(j, b).start(), 1)
        if b == blocks - 1:
            make_rims()

    def back_core_hop(j):
        mine = nth(CHUNKS - j)
        return wires.copy(gathered.at[mine], gathered_other.at[mine], other_core, m, core_slot + CHUNKS + j)

    back_core_hop(0).start()

    to_prev = wires.put(rim_up, grad_next, prv, m)
    to_next = wires.put(rim_down, grad_prev, nxt, m)

    loop(CHUNKS, lambda j: (term_hop(j, 0).wait_send(), term_hop(j, 1).wait_send()))
    loop(CHUNKS + 1, lambda j: core_hop(j).wait_send(), 1)
    for b in range(blocks):
        loop(chips_x, lambda j: x_hop(j, b).wait_send(), 1)
    for i in others:
        z_hop(i).wait_send()
        back_z_hop(i).wait_send()

    def probe_copy(which, source, n, half, slot):
        return pltpu.make_async_copy(
            source.at[n, half * CHUNK : (half + 1) * CHUNK],
            probe_out.at[0, which, chunk_of(n), half * LANES : (half + 1) * LANES],
            out_sem.at[slot],
        )

    def mine_copy(j, half):
        return probe_copy(core, ordered.at[0], nth(CHUNKS - j), half, 1 + 2 * j + half)

    def other_copy(j, half):
        return probe_copy(1 - core, ordered.at[1], nth(CHUNKS - j), half, 1 + 2 * (CHUNKS + j) + half)

    def put_both(copy, source, j):
        n = nth(CHUNKS - j)
        for i in range(chips_z):
            ordered_rows = z_rows(piece_z(i))
            ordered[source, n, ordered_rows] = (gathered, gathered_other)[source][n, piece(i)]
        copy(j, 0).start()
        copy(j, 1).start()

    def wait_both(copy, j):
        copy(j, 0).wait()
        copy(j, 1).wait()

    put_both(mine_copy, 0, 0)

    def tile_part(inner):
        shape = (ROWS, LANES)
        block = m * (COLS // LANES) + inner
        lanes = tiles(lax.rem(block, 2) * LANES, LANES, LANES)

        def mask(who):
            return column_mask(jnp.broadcast_to(corners[who, 0:1, :], shape), block, shape)

        return slice(inner * LANES, (inner + 1) * LANES), lanes, mask

    for inner in range(COLS // LANES):
        here, lanes, mask = tile_part(inner)
        for part in range(2):
            own = jnp.where(mask(1), total_term[part, CHUNK : CHUNK + ROWS, lanes], 0.0)
            new_obj[part, :, here] = strip[m, part, :, here] - object_rate * own

    def pass_on(j):
        for b in range(blocks):
            back_x_hop(j, b).wait_recv()
        back_core_hop(j).start()
        put_both(mine_copy, 0, j)

    loop(chips_x, pass_on, 1)

    to_prev.wait_recv()
    to_next.wait_recv()
    for inner in range(COLS // LANES):
        here, lanes, mask = tile_part(inner)
        for part in range(2):
            above = jnp.where(mask(0) & (s > 0), grad_prev[part, :, lanes], 0.0)
            below = jnp.where(mask(2) & (s < scans - 1), grad_next[part, :, lanes], 0.0)
            new_obj[part, :, here] = new_obj[part, :, here] - object_rate * (above + below)
    obj_copy = pltpu.make_async_copy(new_obj, obj_out, out_sem.at[0])
    obj_copy.start()
    wires.drain()

    def take_core(j):
        back_core_hop(j).wait_recv()
        put_both(other_copy, 1, j)

    loop(CHUNKS, take_core)
    loop(CHUNKS, lambda j: back_core_hop(j).wait_send())
    for b in range(blocks):
        loop(chips_x, lambda j: back_x_hop(j, b).wait_send(), 1)
    obj_copy.wait()
    loop(CHUNKS, lambda j: (wait_both(mine_copy, j), wait_both(other_copy, j)))


PIECES = 4


def placing(obj_in, probe_in, obj_out, probe_out, sem):
    copies = []
    for src, dst, dim in ((obj_in, obj_out, 1), (probe_in, probe_out, 2)):
        size = src.shape[dim] // PIECES
        for i in range(PIECES):
            at = (slice(None),) * dim + (slice(i * size, (i + 1) * size),)
            copies.append(pltpu.make_async_copy(src.at[at], dst.at[at], sem.at[len(copies)]))
    for copy in copies:
        copy.start()
    for copy in copies:
        copy.wait()


def per_device(scans, chips_x, object_field, probe, measured, positions):
    chips_z = scans // (2 * chips_x)
    per_z = 2 * CHUNK // chips_z
    wire_count = 28 + 6 * CHUNKS + 4 * chips_x + 2 * chips_z
    field = pltpu.VMEM((2, PATCH, PATCH), F32)
    plane = pltpu.VMEM((PATCH, PATCH), F32)
    rim = pltpu.VMEM((2, ROWS, PATCH), F32)
    share = pltpu.VMEM((CHUNKS, 2 * CHUNK, LANES), F32)
    hbm = pl.BlockSpec(memory_space=pltpu.HBM)
    anywhere = pl.BlockSpec(memory_space=pl.ANY)
    out_shape = (
        jax.ShapeDtypeStruct(object_field.shape, F32),
        jax.ShapeDtypeStruct(probe.shape, F32),
    )
    results = pl.pallas_call(
        functools.partial(kernel, scans, chips_x, chips_z),
        out_shape=out_shape,
        in_specs=[pl.BlockSpec(memory_space=pltpu.SMEM)] + [hbm] * 4,
        out_specs=(anywhere, anywhere),
        scratch_shapes=[
            pltpu.VMEM(probe.shape, F32),
            pltpu.VMEM(measured.shape, F32),
            field,
            pltpu.VMEM((2, 2, 2 * PATCH, 2 * PATCH), BF16),
            pltpu.VMEM((2, 4 * PATCH, 2 * PATCH), BF16),
            pltpu.VMEM((MODES, 2, ROWS, COLS), F32),
            pltpu.VMEM((3, 8, LANES), jnp.int32),
            rim, rim, rim, rim,
            field, field,
            pltpu.VMEM((2, 2 * PATCH, PATCH), F32),
            pltpu.VMEM((2, 2 * PATCH, PATCH), BF16),
            field,
            plane, plane, plane, plane,
            field, field, field, field, field,
            rim, rim, rim, rim,
            pltpu.VMEM((2, CHUNKS, 2 * CHUNK, LANES), F32),
            share, share, share,
            pltpu.VMEM((2 * CHUNK, LANES), F32),
            pltpu.VMEM((chips_z, per_z, LANES), F32),
            share, share,
            pltpu.VMEM((2, CHUNKS, 2 * CHUNK, LANES), F32),
            pltpu.VMEM(object_field.shape, F32),
            pltpu.SemaphoreType.DMA((wire_count,)),
            pltpu.SemaphoreType.DMA((wire_count,)),
            pltpu.SemaphoreType.DMA((4,)),
            pltpu.SemaphoreType.DMA((1 + 4 * CHUNKS,)),
            pltpu.SemaphoreType.REGULAR((max(chips_x // 2 - 1, 1), 2)),
            pltpu.SemaphoreType.REGULAR((max(chips_z // 2 - 1, 1), 2)),
        ],
        compiler_params=pltpu.CompilerParams(
            collective_id=0, has_side_effects=True, vmem_limit_bytes=32 << 20
        ),
        cost_estimate=pl.CostEstimate(flops=1 << 31, bytes_accessed=4 << 20, transcendentals=0),
    )(*[
        pltpu.with_memory_space_constraint(value, pltpu.HBM)
        for value in (positions, object_field, probe, measured, jnp.asarray(dft_parts()))
    ])
    return pl.pallas_call(
        placing,
        out_shape=out_shape,
        in_specs=[anywhere, anywhere],
        out_specs=(hbm, hbm),
        scratch_shapes=[pltpu.SemaphoreType.DMA((2 * PIECES,))],
    )(*[pltpu.with_memory_space_constraint(value, pltpu.VMEM) for value in results])


def solution(mesh):
    return jax.shard_map(
        functools.partial(per_device, mesh.shape["scan"], X_CHIPS),
        mesh=mesh,
        in_specs=(
            P(None, "scan", "mode"),
            P("mode", None, None, None),
            P("scan", None, None),
            P("scan", None),
        ),
        out_specs=(P(None, "scan", "mode"), P("mode", None, None, None)),
        check_vma=False,
    )
```
